256 devices in a mesh: gx: 32 (over y, z_hi, core), gy: 8 (over z_lo, x).
Axes of the slice: x: 4, y: 4, z: 8 (z_hi: 4, z_lo: 2; z = z_hi * 2 + z_lo), core: 2. Of those that a mesh axis runs over, the one named last changes fastest.
Arguments:
- positions: float32 [3, 32768], P(None, ('gx', 'gy')), as said below
- species: int32 [32768], P(('gx', 'gy')), may hold values from 0 to 5
- neighbours: int32 [64, 32768], P(None, ('gx', 'gy')), may hold values from 0 to 512, as said below
- face_sends: int32 [4, 16384], P(None, ('gx', 'gy')), may hold values from 0 to 127, as said below
- corner_sends: int32 [4, 8192], P(None, ('gx', 'gy')), may hold values from 0 to 127, as said below
- embed: float32 [6, 128], replicated, may hold values from -6 to 6
- radial: float32 [2, 8, 128], replicated, may hold values from -6 to 6
- w_up: float32 [128, 128], replicated, may hold values from -0.5 to 0.5
- w_charge: float32 [128, 128], replicated, may hold values from -0.5 to 0.5
- kvec: float32 [3, 2048], replicated, may hold values from -4 to 4
- kfilter: float32 [2048, 128], replicated, may hold values from -6 to 6
- read: float32 [128], replicated, may hold values from -0.5 to 0.5
Outputs:
- atom_energy: float32 [32768], P(('gx', 'gy'))
- forces: float32 [3, 32768], P(None, ('gx', 'gy'))
- grad_embed: float32 [6, 128], replicated
- grad_radial: float32 [2, 8, 128], replicated
- grad_up: float32 [128, 128], replicated
- grad_charge: float32 [128, 128], replicated
- grad_filter: float32 [2048, 128], replicated
- grad_read: float32 [128], replicated
The draws below stay inside these ranges and needn't reach their ends.
Inputs may be any that keep to these rules, and one draw needn't show every extreme that they name: `positions`: each domain is 8.8 wide along the first two dimensions; coordinates are relative to its corner. `neighbours`: entry [s, i] names a slot of atom i's device's extended list: 0 to 127 are its own atoms in order, then 64 atoms for each face direction and 32 for each corner direction, in the order of the steps; the value 128 + 6 * 64 marks an empty slot. An atom never names itself. `face_sends`: row f of a device lists 64 of its own atoms for face direction f; every own atom appears in some row. `corner_sends`: row f of a device lists 64 / 2 of its own atoms for corner direction f; every own atom appears in some row.
All inputs are finite; a program needn't handle non-finite values.
Results may differ from the reference program's by a relative error of at most 0.0003.
Values sent between devices are 32-bit elements; how exact they have to be, the bound alone decides.
No kernel may reach another device: no remote copies, remote signals or barrier semaphores. Data moves between devices by JAX's collectives and lax.ppermute only.
A program may use at most 64 MiB of HBM per device.

```python
import math
import jax
import jax.numpy as jnp
import numpy as np
from jax import lax

C = 128
RADIAL = 8
SPECIES = 6
KVEC = 2048
NBR = 64
ATOM_DEV = 128
HALO = 64
ATOMS = 32768
N_GX = 32
N_GY = 8


def offset_table():
    found = []
    for step_x in range(-2, 3):
        for step_y in range(-2, 3):
            for step_z in range(-2, 3):
                norm_sq = step_x * step_x + step_y * step_y + step_z * step_z
                if 0 < norm_sq <= 5:
                    found.append((step_x, step_y, step_z))
    return np.array(found, dtype=np.int32)


def lattice_layout(key):
    devices = N_GX * N_GY
    keys = jax.random.split(key, devices)
    site_of = jax.vmap(lambda sub: jax.random.permutation(sub, ATOM_DEV))(keys).astype(jnp.int32)
    slot_of = jnp.argsort(site_of, axis=1).astype(jnp.int32)
    return (site_of, slot_of)


def draw_positions(key, part):
    site_of, slot_of = lattice_layout(key)
    key = jax.random.fold_in(key, 7)
    depth = ATOM_DEV // 16
    site_x = site_of // (4 * depth)
    site_y = site_of // depth % 4
    site_z = site_of % depth
    lattice = jnp.stack([site_x, site_y, site_z]).astype(jnp.float32) * 2.2 + 1.1
    jitter = jax.random.uniform(key, lattice.shape, jnp.float32, -0.3, 0.3)
    return (lattice + jitter).reshape(3, -1)


def draw_neighbours(key, part):
    site_of, slot_of = lattice_layout(key)
    key = jax.random.fold_in(key, 8)
    devices = N_GX * N_GY
    depth = ATOM_DEV // 16
    half = ATOM_DEV // 2
    quarter = ATOM_DEV // 4
    empty = ATOM_DEV + 6 * half
    offsets = jnp.asarray(offset_table())
    site_x = (site_of // (4 * depth))[..., None]
    site_y = (site_of // depth % 4)[..., None]
    site_z = (site_of % depth)[..., None]
    target_x = site_x + offsets[:, 0]
    target_y = site_y + offsets[:, 1]
    target_z = site_z + offsets[:, 2]
    move_x = (target_x >= 4).astype(jnp.int32) - (target_x < 0).astype(jnp.int32)
    move_y = (target_y >= 4).astype(jnp.int32) - (target_y < 0).astype(jnp.int32)
    wrap_x = target_x - 4 * move_x
    wrap_y = target_y - 4 * move_y
    inside = (target_z >= 0) & (target_z < depth)
    clip_z = jnp.clip(target_z, 0, depth - 1)
    near_x = jnp.where(move_x == 1, wrap_x, wrap_x - 2)
    near_y = jnp.where(move_y == 1, wrap_y, wrap_y - 2)
    own_site = (wrap_x * 4 + wrap_y) * depth + clip_z
    own_slot = jnp.take_along_axis(slot_of, own_site.reshape(devices, -1), axis=1).reshape(own_site.shape)
    face_x = ATOM_DEV + jnp.where(move_x == 1, 0, 1) * half + (near_x * 4 + wrap_y) * depth + clip_z
    face_y = ATOM_DEV + jnp.where(move_y == 1, 2, 3) * half + (wrap_x * 2 + near_y) * depth + clip_z
    corner_num = 2 * (move_x == -1).astype(jnp.int32) + (move_y == -1).astype(jnp.int32)
    corner = ATOM_DEV + 4 * half + corner_num * quarter + (near_x * 2 + near_y) * depth + clip_z
    entry = jnp.where((move_x == 0) & (move_y == 0), own_slot, jnp.where(move_y == 0, face_x, jnp.where(move_x == 0, face_y, corner)))
    entry = jnp.where(inside, entry, empty)
    padding = jnp.full(entry.shape[:2] + (NBR - offsets.shape[0],), empty, jnp.int32)
    entry = jnp.concatenate([entry.astype(jnp.int32), padding], axis=2)
    rolls = jax.random.randint(key, entry.shape[:2] + (1,), 0, NBR)
    columns = (jnp.arange(NBR, dtype=jnp.int32)[None, None, :] + rolls) % NBR
    entry = jnp.take_along_axis(entry, columns, axis=2)
    return entry.transpose(2, 0, 1).reshape(NBR, -1)


def draw_face_sends(key, part):
    site_of, slot_of = lattice_layout(key)
    depth = ATOM_DEV // 16
    half = ATOM_DEV // 2
    place = jnp.arange(half, dtype=jnp.int32)
    layer_z = place % depth
    deep_x = place // (4 * depth)
    across_y = place // depth % 4
    across_x = place // (2 * depth)
    deep_y = place // depth % 2
    rows = jnp.stack([(deep_x * 4 + across_y) * depth + layer_z, ((deep_x + 2) * 4 + across_y) * depth + layer_z, (across_x * 4 + deep_y) * depth + layer_z, (across_x * 4 + deep_y + 2) * depth + layer_z])
    slots = slot_of[:, rows]
    return slots.transpose(1, 0, 2).reshape(4, -1)


def draw_corner_sends(key, part):
    site_of, slot_of = lattice_layout(key)
    depth = ATOM_DEV // 16
    quarter = ATOM_DEV // 4
    place = jnp.arange(quarter, dtype=jnp.int32)
    layer_z = place % depth
    deep_x = place // (2 * depth)
    deep_y = place // depth % 2
    rows = jnp.stack([(deep_x * 4 + deep_y) * depth + layer_z, (deep_x * 4 + deep_y + 2) * depth + layer_z, ((deep_x + 2) * 4 + deep_y) * depth + layer_z, ((deep_x + 2) * 4 + deep_y + 2) * depth + layer_z])
    slots = slot_of[:, rows]
    return slots.transpose(1, 0, 2).reshape(4, -1)


def place_ends(entries, stream_key, least, largest):
    index_at = [jax.random.randint(jax.random.fold_in(stream_key, axis), (), 0, length) for axis, length in enumerate(entries.shape)]
    widest = entries.shape.index(max(entries.shape))
    neighbour = index_at[:widest] + [(index_at[widest] + 1) % entries.shape[widest]] + index_at[widest + 1:]
    return entries.at[tuple(index_at)].set(least).at[tuple(neighbour)].set(largest)


def noise(stream_key, dims, spread, most, held_as=jnp.bfloat16):
    return jnp.clip(spread * jax.random.normal(stream_key, dims, jnp.float32), -most, most).astype(held_as)


def setup_inputs(seed: int = 0) -> dict:
    streams_of = jax.random.split(jax.random.key(seed), 13)
    positions = draw_positions(jax.random.fold_in(streams_of[12], 71), 0)
    species = place_ends(jax.random.randint(streams_of[1], (ATOMS,), 0, SPECIES), jax.random.fold_in(streams_of[1], 1), 0, SPECIES - 1).astype(jnp.int32)
    neighbours = draw_neighbours(jax.random.fold_in(streams_of[12], 71), 0)
    face_sends = draw_face_sends(jax.random.fold_in(streams_of[12], 71), 0)
    corner_sends = draw_corner_sends(jax.random.fold_in(streams_of[12], 71), 0)
    embed = noise(streams_of[5], (SPECIES, C), 1.0, 6.0, jnp.float32)
    radial = noise(streams_of[6], (2, RADIAL, C), 1.0, 6.0, jnp.float32)
    w_up = noise(streams_of[7], (C, C), C ** -0.5, 0.5, jnp.float32)
    w_charge = noise(streams_of[8], (C, C), C ** -0.5, 0.5, jnp.float32)
    kvec = noise(streams_of[9], (3, KVEC), 0.5, 4.0, jnp.float32)
    kfilter = noise(streams_of[10], (KVEC, C), 1.0, 6.0, jnp.float32)
    read = noise(streams_of[11], (C,), C ** -0.5, 0.5, jnp.float32)
    return dict(positions=positions, species=species, neighbours=neighbours, face_sends=face_sends, corner_sends=corner_sends, embed=embed, radial=radial, w_up=w_up, w_charge=w_charge, kvec=kvec, kfilter=kfilter, read=read)


CUTOFF = 5.0
SOFTEN = 0.01
WIDTH_GAUSS = 2.0
NORMALIZE = 4.0
DOMAIN = 8.8
slot_group = 16
HIGHEST = lax.Precision.HIGHEST
FACE_DIRS = ((1, 0), (-1, 0), (0, 1), (0, -1))
CORNER_DIRS = ((1, 1), (1, -1), (-1, 1), (-1, -1))

def product(left, right):
    return jnp.dot(left, right, precision=HIGHEST, preferred_element_type=jnp.float32)

def edge_block(coords, ext_pos, ext_feat, weights, centers, slots):
    limit = ext_pos.shape[1]
    valid = (slots < limit).astype(jnp.float32)
    index = jnp.minimum(slots, limit - 1)
    offset_vec = ext_pos[:, index] - coords[:, None, :]
    dist_sq = lax.optimization_barrier(jnp.sum(offset_vec * offset_vec, axis=0))
    radius = jnp.sqrt(dist_sq + SOFTEN)
    envelope = jnp.square(jnp.maximum(1.0 - dist_sq / (CUTOFF * CUTOFF), 0.0)) * valid
    basis = jnp.exp(-WIDTH_GAUSS * jnp.square(radius[None] - centers[:, None, None])) * envelope[None]
    radial_zero = jnp.einsum('bc,bsa->csa', weights[0], basis, precision=HIGHEST)
    radial_one = jnp.einsum('bc,bsa->csa', weights[1], basis, precision=HIGHEST)
    gathered = ext_feat[:, index]
    scalar_part = lax.optimization_barrier(jnp.sum(radial_zero * gathered, axis=1))
    vector_part = jnp.einsum('csa,dsa->dca', radial_one * gathered, offset_vec, precision=HIGHEST)
    return (scalar_part, vector_part)

def edge_features(coords, halo_pos, features, halo_feat, weights, neighbours):
    ext_pos = jnp.concatenate([coords, halo_pos], axis=1)
    ext_feat = jnp.concatenate([features, halo_feat], axis=1)
    basis_count = weights.shape[1]
    centers = jnp.arange(basis_count, dtype=jnp.float32) * (CUTOFF / (basis_count - 1))
    channels = features.shape[0]
    atoms = coords.shape[1]
    groups = neighbours.reshape(-1, slot_group, atoms)
    blocked = jax.checkpoint(edge_block)

    def step(carry, slots):
        first, second = blocked(coords, ext_pos, ext_feat, weights, centers, slots)
        return ((carry[0] + first, carry[1] + second), None)
    start = (jnp.zeros((channels, atoms), jnp.float32), jnp.zeros((3, channels, atoms), jnp.float32))
    (scalar_msg, vector_msg), _ = lax.scan(step, start, groups)
    scalar_msg = scalar_msg / NORMALIZE
    vector_msg = vector_msg / (NORMALIZE * CUTOFF)
    return scalar_msg + lax.optimization_barrier(jnp.sum(jnp.square(vector_msg), axis=0))

def phase_block(global_pos, k_block):
    phase_angle = k_block[0][:, None] * global_pos[0][None, :] + k_block[1][:, None] * global_pos[1][None, :] + k_block[2][:, None] * global_pos[2][None, :]
    return (jnp.cos(phase_angle), jnp.sin(phase_angle))

def reference(positions, species, neighbours, face_sends, corner_sends, embed, radial, w_up, w_charge, kvec, kfilter, read):
    devices = N_GX * N_GY
    pos_dev = positions.reshape(3, devices, ATOM_DEV).transpose(1, 0, 2)
    nbr_dev = neighbours.reshape(NBR, devices, ATOM_DEV).transpose(1, 0, 2)
    face_dev = face_sends.reshape(4, devices, HALO).transpose(1, 0, 2)
    corner_dev = corner_sends.reshape(4, devices, HALO // 2).transpose(1, 0, 2)
    spec_dev = species.reshape(devices, ATOM_DEV)
    dev_ids = jnp.arange(devices, dtype=jnp.int32)
    scale = 1.0 / math.sqrt(ATOMS * KVEC)

    def global_pos(device, coords):
        row_index = (device // N_GY).astype(jnp.float32)
        col_index = (device % N_GY).astype(jnp.float32)
        anchor = jnp.stack([row_index * DOMAIN, col_index * DOMAIN, jnp.zeros((), jnp.float32)])
        return coords + anchor[:, None]

    def energies(pos_dev, embed, radial, w_up, w_charge, kfilter, read):
        onehot = (spec_dev[:, None, :] == jnp.arange(SPECIES, dtype=jnp.int32)[None, :, None]).astype(jnp.float32)
        initial_dev = jnp.einsum('sc,dsa->dca', embed, onehot, precision=HIGHEST)
        source = jnp.concatenate([pos_dev, initial_dev], axis=1)

        def short_range(items):
            device, coords, slots = items
            row_index = device // N_GY
            col_index = device % N_GY
            pieces = []
            for table, directions in ((face_dev, FACE_DIRS), (corner_dev, CORNER_DIRS)):
                for number, (step_x, step_y) in enumerate(directions):
                    other = (row_index + step_x) % N_GX * N_GY + (col_index + step_y) % N_GY
                    piece = source[other][:, table[other, number]]
                    shift_vec = jnp.array([step_x * DOMAIN, step_y * DOMAIN, 0.0], dtype=jnp.float32)[:, None]
                    pieces.append(jnp.concatenate([piece[:3] + shift_vec, piece[3:]], axis=0))
            halo_rows = jnp.concatenate(pieces, axis=1)
            initial = initial_dev[device]
            invariants = edge_features(coords, halo_rows[:3], initial, halo_rows[3:], radial, slots)
            updated = initial + product(w_up.T, jax.nn.silu(invariants))
            charges = product(w_charge.T, updated)
            return (updated, charges)
        updated_dev, charge_dev = lax.map(jax.checkpoint(short_range), (dev_ids, pos_dev, nbr_dev))

        def accumulate(total, items):
            device, coords, charges = items
            cosine, sine = phase_block(global_pos(device, coords), kvec)
            return ((total[0] + product(cosine, charges.T), total[1] + product(sine, charges.T)), None)
        start = (jnp.zeros((KVEC, C), jnp.float32), jnp.zeros((KVEC, C), jnp.float32))
        (cos_factor, sin_factor), _ = lax.scan(jax.checkpoint(accumulate), start, (dev_ids, pos_dev, charge_dev))

        def long_range(items):
            device, coords, updated = items
            cosine, sine = phase_block(global_pos(device, coords), kvec)
            potential = scale * (product((kfilter * cos_factor).T, cosine) + product((kfilter * sin_factor).T, sine))
            combined = updated + potential
            return product(read[None, :], jax.nn.silu(combined))[0]
        return lax.map(jax.checkpoint(long_range), (dev_ids, pos_dev, updated_dev))
    energy_dev, pullback = jax.vjp(energies, pos_dev, embed, radial, w_up, w_charge, kfilter, read)
    grads = pullback(jnp.ones_like(energy_dev))
    grad_pos, grad_embed, grad_radial, grad_up, grad_charge, grad_filter, grad_read = grads
    atom_energy = energy_dev.reshape(ATOMS)
    forces = -grad_pos.transpose(1, 0, 2).reshape(3, ATOMS)
    return (atom_energy, forces, grad_embed / ATOMS, grad_radial / ATOMS, grad_up / ATOMS, grad_charge / ATOMS, grad_filter, grad_read / ATOMS)
```

```python
import functools
import math

import jax
import jax.numpy as jnp
from jax import lax
from jax.experimental import pallas as pl
from jax.experimental.pallas import tpu as pltpu
from jax.sharding import Mesh
from jax.sharding import PartitionSpec as P

CUTOFF = 5.0
SOFTEN = 0.01
WIDTH_GAUSS = 2.0
DOMAIN = 8.8
N = 128
SLOTS = 64
KINDS = 6
BASIS = 8
WAVES = 2048
ATOMS = 32768
SHARD = 256
HIGHEST = lax.Precision.HIGHEST
SCALE = 1.0 / math.sqrt(ATOMS * WAVES)

GX = ("y", "zh", "c")
GY = ("zl", "x")
ALL = GX + GY
GROUP = ("c", "x")
CROSS = ("y", "zh", "zl")
MEMBERS = 8
CROSSES = 32

COS_POLY = None
SIN_POLY = None


def _fit():
    import numpy as np

    count = 9
    points = (1.0 + np.cos(np.pi * (np.arange(200) + 0.5) / 200)) / 8.0
    root = np.sqrt(points)
    matrix = np.vander(points * 4.0, count, increasing=True)
    cosine = np.linalg.lstsq(matrix, np.cos(2 * np.pi * root), rcond=None)[0]
    sine = np.linalg.lstsq(matrix, np.sin(2 * np.pi * root) / root, rcond=None)[0]
    powers = 4.0 ** np.arange(count)
    return ([float(v) for v in cosine * powers], [float(v) for v in sine * powers])


COS_POLY, SIN_POLY = _fit()


def dims(left, right):
    return (((left,), (right,)), ((), ()))


def dot(left, right, left_dim=1, right_dim=0, precision=HIGHEST):
    return lax.dot_general(
        left,
        right,
        dims(left_dim, right_dim),
        precision=precision,
        preferred_element_type=jnp.float32,
    )


def half_dot(left, right, left_dim=1, right_dim=0):
    return lax.dot_general(
        left, right, dims(left_dim, right_dim), preferred_element_type=jnp.float32
    )


def split(value):
    high = value.astype(jnp.bfloat16)
    return high, (value - high.astype(jnp.float32)).astype(jnp.bfloat16)


def dot_three(left, right, left_dim=1, right_dim=0):
    left_high, left_low = left
    right_high, right_low = right
    return (
        half_dot(left_high, right_high, left_dim, right_dim)
        + half_dot(left_high, right_low, left_dim, right_dim)
        + half_dot(left_low, right_high, left_dim, right_dim)
    )


def sigmoid(value):
    return 1.0 / (1.0 + jnp.exp(-value))


def lane(shape):
    return lax.broadcasted_iota(jnp.int32, shape, 1)


def row_of(shape):
    return lax.broadcasted_iota(jnp.int32, shape, 0)


def call(kernel, out_shape, *args, scratch=(), vmem=32):
    return pl.pallas_call(
        kernel,
        out_shape=out_shape,
        scratch_shapes=list(scratch),
        compiler_params=pltpu.CompilerParams(vmem_limit_bytes=vmem * 1024 * 1024),
    )(*args)


def f32(*shape):
    return jax.ShapeDtypeStruct(shape, jnp.float32)


def take(row, index):
    return jnp.take_along_axis(
        jnp.broadcast_to(row, index.shape), index, axis=1, mode="promise_in_bounds"
    )


def pack_kernel(pos, species, index, to_minus, to_plus, own):
    rows = [pos[0:1, :], pos[1:2, :], pos[2:3, :], species[...].astype(jnp.float32)]
    where_from = index[...]
    for number, row in enumerate(rows):
        got = take(row, where_from)
        to_minus[number : number + 1, :] = got[0:1, :]
        to_plus[number : number + 1, :] = got[1:2, :]
        own[number : number + 1, :] = got[2:3, :]
    zero = jnp.zeros((4, N), jnp.float32)
    to_minus[4:8, :] = zero
    to_plus[4:8, :] = zero
    own[4:8, :] = zero


def relay_kernel(own, first, second, one, two):
    at = lane((8, N))
    a, b, d = own[...], first[...], second[...]
    one[...] = jnp.where(at < 64, a, jnp.where(at < 96, b, pltpu.roll(d, 32, 1)))
    two[...] = jnp.where(at < 64, pltpu.roll(a, 64, 1), jnp.where(at < 96, pltpu.roll(b, 96, 1), d))


def relay(own, first, second):
    return call(relay_kernel, (f32(8, N), f32(8, N)), own, first, second)


def moved(value, axes, steps):
    count = 1
    for axis in axes:
        count *= lax.axis_size(axis)
    return lax.ppermute(value, axes, [(s, (s + steps) % count) for s in range(count)])


def pair_weights(embed, radial):
    scalar, vector = [], []
    for kind in range(KINDS):
        row = embed[kind : kind + 1, :]
        scalar.append(radial[0] * row * 0.25)
        vector.append(radial[1] * row * 0.05)
    return jnp.concatenate(scalar, axis=0), jnp.concatenate(vector, axis=0)


def basis_centers():
    return row_of((BASIS, N)).astype(jnp.float32) * (CUTOFF / (BASIS - 1))


def edge_kernel(
    pos, species, nbr, from_plus_x, from_minus_x, from_plus_y, from_minus_y, embed, radial,
    shared, active, invariants, vectors, sums, edges, places,
):
    at = lane((8, N))
    own = [pos[0:1, :], pos[1:2, :], pos[2:3, :], species[...].astype(jnp.float32)]
    first, second = from_plus_x[...], from_minus_x[...]
    third = jnp.where(at < 64, from_plus_y[...], pltpu.roll(from_minus_y[...], 64, 1))
    line = lane((1, N))
    corner_y = jnp.where(line < 64, 0.0, jnp.where(line < 96, DOMAIN, -DOMAIN))
    tables = [
        own,
        [first[0:1] + DOMAIN, first[1:2] + corner_y, first[2:3], first[3:4]],
        [second[0:1] - DOMAIN, second[1:2] + corner_y, second[2:3], second[3:4]],
        [third[0:1], third[1:2] + jnp.where(line < 64, DOMAIN, -DOMAIN), third[2:3], third[3:4]],
    ]
    for group in range(SLOTS // 8):
        rows = slice(8 * group, 8 * group + 8)
        slot = nbr[rows, :]
        block = lax.shift_right_logical(slot, 6)
        table = jnp.where(
            block < 2,
            0,
            jnp.where(
                (block == 4) | (block == 5), 3, jnp.where((block & 1) == 0, 1, 2)
            ),
        )
        table = jnp.where(block == 8, 4, table)
        half = jnp.where((block == 1) | ((block >= 5) & (block < 8)), 64, 0)
        place = (slot & 63) + half
        found = []
        for number in range(4):
            value = take(tables[0][number], place)
            for other in range(1, 4):
                value = jnp.where(table == other, take(tables[other][number], place), value)
            found.append(value)
        offset = [found[d] - own[d] for d in range(3)]
        dist_sq = offset[0] * offset[0] + offset[1] * offset[1] + offset[2] * offset[2]
        valid = (table < 4).astype(jnp.float32)
        ramp = jnp.maximum(1.0 - dist_sq / (CUTOFF * CUTOFF), 0.0)
        edges[0, rows, :] = offset[0]
        edges[1, rows, :] = offset[1]
        edges[2, rows, :] = offset[2]
        edges[3, rows, :] = found[3]
        edges[4, rows, :] = jnp.sqrt(dist_sq + SOFTEN)
        edges[5, rows, :] = ramp * ramp * valid
        edges[6, rows, :] = (-2.0 / (CUTOFF * CUTOFF)) * ramp * valid
        places[0, rows, :] = table
        places[1, rows, :] = place
    centers = basis_centers()

    def step(slot, carry):
        row = pl.ds(slot, 1)
        away = edges[4, row, :] - centers
        basis = jnp.exp(-WIDTH_GAUSS * away * away) * edges[5, row, :]
        parts = [basis] + [basis * edges[d, row, :] for d in range(3)]
        kind_row = jnp.broadcast_to(edges[3, row, :], (BASIS, N))
        out = []
        for kind in range(KINDS):
            mask = kind_row == float(kind)
            for number in range(4):
                out.append(carry[4 * kind + number] + jnp.where(mask, parts[number], 0.0))
        return tuple(out)

    zero = jnp.zeros((BASIS, N), jnp.float32)
    total = lax.fori_loop(0, SLOTS, step, (zero,) * (4 * KINDS), unroll=4)
    for number in range(4):
        sums[number, :, :] = jnp.concatenate(
            [total[4 * kind + number] for kind in range(KINDS)], axis=0
        )
    scalar_w, vector_w = pair_weights(embed, radial)
    value = dot(sums[0], scalar_w, 0, 0)
    for d in range(3):
        vector = dot(sums[1 + d], vector_w, 0, 0)
        vectors[d, :, :] = vector
        value = value + vector * vector
    invariants[...] = value
    result = value * sigmoid(value)
    active[...] = result
    anchor_x = lax.convert_element_type(lax.axis_index(GX), jnp.float32) * DOMAIN
    anchor_y = lax.convert_element_type(lax.axis_index(GY), jnp.float32) * DOMAIN
    zero_row = jnp.zeros((1, N), jnp.float32)
    tail = jnp.concatenate(
        [own[0] + anchor_x, own[1] + anchor_y, own[2], own[3]] + [zero_row] * 4, axis=0
    )
    for member in range(MEMBERS):
        shared[member, 0:N, :] = result
        shared[member, N : N + 8, :] = tail


def edge_back_kernel(
    tiles, common, active, invariants, vectors, sums, edges, places, embed, radial, w_up, w_charge,
    species, grad_out, read_row,
    payload, charge_piece, own_grad, to_one, to_two, to_three,
):
    total = tiles[0]
    for member in range(1, MEMBERS):
        total = total + tiles[member]
    grad_charges = jnp.transpose(total[0:N, :])
    updated = grad_out[...] + dot(grad_charges, w_charge[...], 1, 1)
    value = invariants[...]
    logistic = sigmoid(value)
    slope = logistic * (1.0 + value * (1.0 - logistic))
    grad_inv = dot(updated, w_up[...], 1, 1) * slope
    scalar_w, vector_w = pair_weights(embed, radial)
    pulls = [dot(scalar_w, grad_inv, 1, 1)]
    grad_scalar = dot(sums[0], grad_inv)
    grad_vector = jnp.zeros((KINDS * BASIS, N), jnp.float32)
    for d in range(3):
        along = 2.0 * vectors[d] * grad_inv
        pulls.append(dot(vector_w, along, 1, 1))
        grad_vector = grad_vector + dot(sums[1 + d], along)
    onehot = (row_of((8, N)) == species[...]).astype(jnp.float32)
    grad_table = dot(onehot, updated)
    radial_zero = jnp.zeros((BASIS, N), jnp.float32)
    radial_one = jnp.zeros((BASIS, N), jnp.float32)
    table_rows = []
    for kind in range(KINDS):
        rows = slice(kind * BASIS, (kind + 1) * BASIS)
        row = embed[kind : kind + 1, :]
        part_zero, part_one = grad_scalar[rows] * 0.25, grad_vector[rows] * 0.05
        radial_zero = radial_zero + part_zero * row
        radial_one = radial_one + part_one * row
        table_rows.append(
            grad_table[kind : kind + 1]
            + jnp.sum(radial[0] * part_zero + radial[1] * part_one, axis=0, keepdims=True)
        )
    rest = jnp.concatenate(
        [radial_zero, radial_one] + table_rows + [read_row[...], jnp.zeros((1, N), jnp.float32)],
        axis=0,
    )
    up_piece = total[N + 24 : N + 40, :]
    charge_piece[...] = total[N + 8 : N + 24, :]
    for other in range(CROSSES):
        payload[other, 0:16, :] = up_piece
        payload[other, 16:40, :] = rest
    centers = basis_centers()
    sub = row_of((8, N))
    sub_table = sub & 3
    high_rows = sub < 4
    lane_rows = row_of((N, N))
    pull = [
        [pulls[number][kind * BASIS : (kind + 1) * BASIS] for number in range(4)]
        for kind in range(KINDS)
    ]

    def step(slot, carry):
        row = pl.ds(slot, 1)
        kind_row = jnp.broadcast_to(edges[3, row, :], (BASIS, N))
        own_pull = list(pull[KINDS - 1])
        for kind in range(KINDS - 1):
            mask = kind_row == float(kind)
            own_pull = [jnp.where(mask, pull[kind][n], own_pull[n]) for n in range(4)]
        radius = edges[4, row, :]
        envelope = edges[5, row, :]
        away = radius - centers
        bell = jnp.exp(-WIDTH_GAUSS * away * away)
        offset = [jnp.broadcast_to(edges[d, row, :], (BASIS, N)) for d in range(3)]
        by_basis = own_pull[0]
        for d in range(3):
            by_basis = by_basis + offset[d] * own_pull[1 + d]
        by_square = by_basis * bell * (edges[6, row, :] - (2.0 * envelope / radius) * away)
        basis = bell * envelope
        table = jnp.broadcast_to(places[0, row, :], (8, N)) == sub_table
        place = lane_rows == places[1, row, :]
        onehot = jnp.where(place, 1.0, 0.0).astype(jnp.bfloat16)
        centre, pieces = [], []
        for d in range(3):
            part = basis * own_pull[1 + d] + 2.0 * offset[d] * by_square
            centre.append(carry[d] + part)
            whole = jnp.broadcast_to(jnp.sum(part, axis=0, keepdims=True), (8, N))
            high = whole.astype(jnp.bfloat16).astype(jnp.float32)
            pieces.append(jnp.where(table, jnp.where(high_rows, high, whole - high), 0.0))
        rows = jnp.concatenate(pieces, axis=0).astype(jnp.bfloat16)
        return (*centre, carry[3] + half_dot(rows, onehot, 1, 1))

    zero = jnp.zeros((8, N), jnp.float32)
    out = lax.fori_loop(
        0, SLOTS, step, (zero, zero, zero, jnp.zeros((24, N), jnp.float32)), unroll=4
    )
    scattered = out[3]
    waves = total[N : N + 8, :]
    own_rows, one_rows, two_rows, three_rows = [], [], [], []
    for d in range(3):
        both = scattered[8 * d : 8 * d + 4] + scattered[8 * d + 4 : 8 * d + 8]
        centre = jnp.sum(out[d], axis=0, keepdims=True)
        own_rows.append(both[0:1] - centre + waves[d : d + 1])
        one_rows.append(both[1:2])
        two_rows.append(both[2:3])
        three_rows.append(both[3:4])
    pad = [jnp.zeros((5, N), jnp.float32)]
    own_grad[...] = jnp.concatenate(own_rows + pad, axis=0)
    to_one[...] = jnp.concatenate(one_rows + pad, axis=0)
    to_two[...] = jnp.concatenate(two_rows + pad, axis=0)
    to_three[...] = jnp.concatenate(three_rows + pad, axis=0)


def force_kernel(own_grad, from_minus_x, from_plus_x, from_minus_y, from_plus_y, index, forces):
    at = lane((8, N))
    faces = jnp.where(at < 64, from_minus_x[...], pltpu.roll(from_plus_x[...], 64, 1))
    total = own_grad[...]
    lane_rows = row_of((N, N))
    for number, piece in enumerate((from_minus_y[...], from_plus_y[...], faces)):
        onehot = jnp.where(lane_rows == index[number : number + 1, :], 1.0, 0.0)
        total = total + dot(piece, onehot, 1, 1)
    forces[...] = -total[0:3, :]


def structure_kernel(shared, kvec, embed, w_up, w_charge, factor, wave_high, wave_low, charges,
                     feature_high, feature_low):
    me = lax.axis_index(GROUP)
    at = pl.multiple_of(me * SHARD, SHARD)
    rows = jnp.concatenate(
        [kvec[:, pl.ds(at, SHARD)], jnp.zeros((5, SHARD), jnp.float32)], axis=0
    )
    turns = jnp.transpose(rows * (1.0 / (2.0 * math.pi)))
    table = jnp.concatenate([embed[...], jnp.zeros((2, N), jnp.float32)], axis=0)
    up = split(w_up[...])
    charge_w = split(w_charge[...])
    for member in range(MEMBERS):
        part = slice(member * N, (member + 1) * N)
        tail = shared[member, N : N + 8, :]
        onehot = (row_of((8, N)).astype(jnp.float32) == tail[3:4, :]).astype(jnp.float32)
        feature = dot(onehot, table, 0, 0) + dot_three(split(shared[member, 0:N, :]), up)
        high, low = split(feature)
        feature_high[part, :] = high
        feature_low[part, :] = low
        charges[part, :] = dot_three((high, low), charge_w)
        for chunk in range(SHARD // 64):
            waves = slice(chunk * 64, chunk * 64 + 64)
            angle = (
                turns[waves, 0:1] * tail[0:1, :]
                + turns[waves, 1:2] * tail[1:2, :]
                + turns[waves, 2:3] * tail[2:3, :]
            )
            angle = angle - jnp.round(angle)
            square = angle * angle
            cosine = jnp.full(square.shape, COS_POLY[-1], jnp.float32)
            for value in COS_POLY[-2::-1]:
                cosine = cosine * square + value
            sine = jnp.full(square.shape, SIN_POLY[-1], jnp.float32)
            for value in SIN_POLY[-2::-1]:
                sine = sine * square + value
            sine = sine * angle
            high, low = split(cosine)
            wave_high[waves, part] = high
            wave_low[waves, part] = low
            high, low = split(sine)
            waves = slice(SHARD + chunk * 64, SHARD + chunk * 64 + 64)
            wave_high[waves, part] = high
            wave_low[waves, part] = low
    project(wave_high, wave_low, feature_high[...], feature_low[...], factor)


def project(wave_high, wave_low, high, low, out):
    both = jnp.concatenate([high, low], axis=1)
    wide = half_dot(wave_high[...], both)
    total = wide[:, 0:N] + wide[:, N:] + half_dot(wave_low[...], high)
    out[...] = total.reshape(CROSSES, 16, N)


def projection_kernel(gathered, wave_high, wave_low, out):
    high, low = split(gathered[...].reshape(MEMBERS * N, N))
    project(wave_high, wave_low, high, low, out)


def sum_kernel(tiles, out):
    total = jnp.sum(tiles[...], axis=0)
    for other in range(out.shape[0]):
        out[other, :, :] = total


def filter_of(kfilter):
    me = lax.axis_index(GROUP)
    return kfilter[pl.ds(pl.multiple_of(me * SHARD, SHARD), SHARD), :] * SCALE


def waves_to_atoms(field, wave_high, wave_low):
    high, low = split(jnp.transpose(field))
    wide = half_dot(jnp.concatenate([high, low], axis=0), wave_high[...])
    return wide[0:N] + wide[N:] + half_dot(high, wave_low[...])


def potential_kernel(factor, w_charge, kfilter, wave_high, wave_low, out, weighted, charge_factor):
    scaled = filter_of(kfilter)
    charged = dot(factor[...], w_charge[...])
    charge_factor[...] = charged
    field = charged * jnp.concatenate([scaled, scaled], axis=0)
    weighted[...] = field
    total = waves_to_atoms(field, wave_high, wave_low)
    for member in range(MEMBERS):
        out[member, :, :] = total[:, member * N : (member + 1) * N]


def energy_kernel(tiles, active, species, embed, w_up, read,
                  shared, grad_out, energy, read_row, up_part):
    total = tiles[0]
    for member in range(1, MEMBERS):
        total = total + tiles[member]
    table = jnp.concatenate([embed[...], jnp.zeros((2, N), jnp.float32)], axis=0)
    onehot = (row_of((8, N)) == species[...]).astype(jnp.float32)
    act = active[...]
    combined = dot(onehot, table, 0, 0) + dot(act, w_up[...]) + jnp.transpose(total)
    logistic = sigmoid(combined)
    result = combined * logistic
    weights = read[...]
    energy[...] = dot(jnp.broadcast_to(weights, (8, N)), result, 1, 1)[0:1, :]
    read_row[...] = jnp.sum(result, axis=0, keepdims=True)
    grad = weights * (logistic * (1.0 + combined * (1.0 - logistic)))
    grad_out[...] = grad
    up_part[...] = dot(act, grad, 0, 0)
    for member in range(MEMBERS):
        shared[member, :, :] = grad


def wave_back_kernel(projected, factor, charge_factor, weighted, kfilter, kvec, wave_high, wave_low,
                     gathered, charges, shared, w_charge, up_part, out, grad_filter, phase):
    me = lax.axis_index(GROUP)
    at = pl.multiple_of(me * SHARD, SHARD)
    scaled = filter_of(kfilter)
    proj = projected[...]
    mixed = charge_factor[...] * proj
    grad_filter[...] = SCALE * (mixed[0:SHARD] + mixed[SHARD:])
    field = proj * jnp.concatenate([scaled, scaled], axis=0)
    by_charge = waves_to_atoms(field, wave_high, wave_low)
    charge_grad = dot(factor[...], field, 0, 0)
    active = jnp.concatenate([shared[member, 0:N, :] for member in range(MEMBERS)], axis=0)
    mix = dot_three(split(by_charge), split(active))
    up_grad = dot(mix, w_charge[...], 0, 1) + up_part[...]
    left = split(jnp.concatenate([weighted[...], field], axis=1))
    right = split(
        jnp.concatenate([gathered[...].reshape(MEMBERS * N, N), charges[...]], axis=1)
    )
    along = dot_three(left, right, 1, 1)
    cosine = wave_high[0:SHARD, :].astype(jnp.float32) + wave_low[0:SHARD, :].astype(jnp.float32)
    sine = wave_high[SHARD:, :].astype(jnp.float32) + wave_low[SHARD:, :].astype(jnp.float32)
    phase[...] = cosine * along[SHARD:] - sine * along[0:SHARD]
    rows = jnp.concatenate(
        [kvec[:, pl.ds(at, SHARD)], jnp.zeros((5, SHARD), jnp.float32)], axis=0
    )
    by_pos = dot(rows, phase[...])
    for member in range(MEMBERS):
        part = slice(member * N, (member + 1) * N)
        piece = slice(member * 16, (member + 1) * 16)
        out[member, 0:N, :] = by_charge[:, part]
        out[member, N : N + 8, :] = by_pos[:, part]
        out[member, N + 8 : N + 24, :] = charge_grad[piece]
        out[member, N + 24 : N + 40, :] = up_grad[piece]


def gather_sum_kernel(tiles, charge_piece, out):
    total = jnp.sum(tiles[...], axis=0)
    piece = charge_piece[...]
    for member in range(MEMBERS):
        out[member, 0:40, :] = total
        out[member, 40:56, :] = piece


def finish_kernel(tiles, grad_embed, grad_radial, grad_up, grad_charge, grad_read):
    mean = 1.0 / ATOMS
    total = tiles[0, 16:40, :]
    for member in range(1, MEMBERS):
        total = total + tiles[member, 16:40, :]
    total = total * mean
    for member in range(MEMBERS):
        grad_up[16 * member : 16 * member + 16, :] = tiles[member, 0:16, :] * mean
        grad_charge[16 * member : 16 * member + 16, :] = tiles[member, 40:56, :] * mean
    grad_radial[0, :, :] = total[0:8]
    grad_radial[1, :, :] = total[8:16]
    grad_embed[...] = total[16:22]
    grad_read[...] = total[22:23]


def body(
    positions, species, neighbours, face_sends, corner_sends,
    embed, radial, w_up, w_charge, kvec, kfilter, read,
):
    species = species.reshape(1, N)
    read = read.reshape(1, N)
    index = jnp.concatenate(
        [
            jnp.concatenate([face_sends[2], corner_sends[0], corner_sends[2]])[None],
            jnp.concatenate([face_sends[3], corner_sends[1], corner_sends[3]])[None],
            jnp.concatenate([face_sends[0], face_sends[1]])[None],
            jnp.zeros((5, N), jnp.int32),
        ],
        axis=0,
    )
    to_minus, to_plus, own_x = call(pack_kernel, (f32(8, N),) * 3, positions, species, index)
    from_plus_y = moved(to_minus, GY, -1)
    from_minus_y = moved(to_plus, GY, 1)
    to_minus, to_plus = relay(own_x, from_plus_y, from_minus_y)
    from_plus_x = moved(to_minus, GX, -1)
    from_minus_x = moved(to_plus, GX, 1)
    shared, active, invariants, vectors, sums, edges, places = call(
        edge_kernel,
        (
            f32(MEMBERS, N + 8, N), f32(N, N), f32(N, N), f32(3, N, N), f32(4, KINDS * BASIS, N),
            f32(7, SLOTS, N), jax.ShapeDtypeStruct((2, SLOTS, N), jnp.int32),
        ),
        positions, species, neighbours, from_plus_x, from_minus_x, from_plus_y, from_minus_y,
        embed, radial,
    )
    shared = lax.all_to_all(shared, GROUP, 0, 0)
    half = jax.ShapeDtypeStruct((2 * SHARD, MEMBERS * N), jnp.bfloat16)
    scratch = pltpu.VMEM((MEMBERS * N, N), jnp.bfloat16)
    factor, wave_high, wave_low, charges = call(
        structure_kernel,
        (f32(CROSSES, 16, N), half, half, f32(MEMBERS * N, N)),
        shared, kvec, embed, w_up, w_charge,
        scratch=(scratch, scratch),
    )

    def cross_sum(tiles):
        tiles = lax.all_to_all(tiles, CROSS, 0, 0)
        tiles = call(sum_kernel, f32(CROSSES, 16, N), tiles)
        return lax.all_to_all(tiles, CROSS, 0, 0).reshape(2 * SHARD, N)

    factor = cross_sum(factor)
    potential, weighted, charge_factor = call(
        potential_kernel,
        (f32(MEMBERS, N, N), f32(2 * SHARD, N), f32(2 * SHARD, N)),
        factor, w_charge, kfilter, wave_high, wave_low,
    )
    potential = lax.all_to_all(potential, GROUP, 0, 0)
    gathered, grad_out, energy, read_row, up_part = call(
        energy_kernel,
        (f32(MEMBERS, N, N), f32(N, N), f32(1, N), f32(1, N), f32(N, N)),
        potential, active, species, embed, w_up, read,
    )
    gathered = lax.all_to_all(gathered, GROUP, 0, 0)
    projected = cross_sum(
        call(projection_kernel, f32(CROSSES, 16, N), gathered, wave_high, wave_low)
    )
    tiles, grad_filter = call(
        wave_back_kernel,
        (f32(MEMBERS, N + 40, N), f32(SHARD, N)),
        projected, factor, charge_factor, weighted, kfilter, kvec, wave_high, wave_low,
        gathered, charges, shared, w_charge, up_part,
        scratch=(pltpu.VMEM((SHARD, MEMBERS * N), jnp.float32),),
    )
    grad_filter = lax.all_gather(grad_filter, GROUP, axis=0, tiled=True)
    tiles = lax.all_to_all(tiles, GROUP, 0, 0)
    payload, charge_piece, own_grad, to_one, to_two, to_three = call(
        edge_back_kernel,
        (f32(CROSSES, 40, N), f32(16, N)) + (f32(8, N),) * 4,
        tiles, shared, active, invariants, vectors, sums, edges, places, embed, radial, w_up,
        w_charge, species, grad_out, read_row,
    )
    back_minus_x = moved(to_one, GX, 1)
    back_plus_x = moved(to_two, GX, -1)
    to_plus, to_minus = relay(to_three, back_minus_x, back_plus_x)
    back_minus_y = moved(to_plus, GY, 1)
    back_plus_y = moved(to_minus, GY, -1)
    forces = call(
        force_kernel, f32(3, N),
        own_grad, back_minus_x, back_plus_x, back_minus_y, back_plus_y, index,
    )
    payload = lax.all_to_all(payload, CROSS, 0, 0)
    payload = call(gather_sum_kernel, f32(MEMBERS, 56, N), payload, charge_piece)
    payload = lax.all_to_all(payload, GROUP, 0, 0)
    grad_embed, grad_radial, grad_up, grad_charge, grad_read = call(
        finish_kernel,
        (f32(KINDS, N), f32(2, BASIS, N), f32(N, N), f32(N, N), f32(1, N)),
        payload,
    )
    return (
        energy.reshape(N), forces, grad_embed, grad_radial, grad_up, grad_charge, grad_filter,
        grad_read.reshape(N),
    )


def solution(mesh):
    fine = Mesh(mesh.devices.reshape(4, 4, 2, 2, 4), ALL)
    atoms = P(ALL)
    rows = P(None, ALL)
    return jax.shard_map(
        body,
        mesh=fine,
        in_specs=(rows, atoms, rows, rows, rows) + (P(),) * 7,
        out_specs=(atoms, rows) + (P(),) * 6,
        check_vma=False,
    )
```

```python
import functools
import math

import jax
import jax.numpy as jnp
from jax import lax
from jax.experimental import pallas as pl
from jax.experimental.pallas import tpu as pltpu
from jax.sharding import Mesh
from jax.sharding import PartitionSpec as P

CUTOFF = 5.0
SOFTEN = 0.01
WIDTH_GAUSS = 2.0
DOMAIN = 8.8
N = 128
SLOTS = 64
KINDS = 6
BASIS = 8
WAVES = 2048
ATOMS = 32768
SHARD = 256
HIGHEST = lax.Precision.HIGHEST
SCALE = 1.0 / math.sqrt(ATOMS * WAVES)

GX = ("y", "zh", "c")
GY = ("zl", "x")
ALL = GX + GY
GROUP = ("c", "x")
CROSS = ("y", "zh", "zl")
MEMBERS = 8
CROSSES = 32
DEPTH = ("zh", "zl")
PLANE = ("y", "x")

COS_POLY = None
SIN_POLY = None


def _fit():
    import numpy as np

    points = (1.0 + np.cos(np.pi * (np.arange(200) + 0.5) / 200)) / 8.0
    root = np.sqrt(points)
    found = []
    for count, value in ((7, np.cos(2 * np.pi * root)), (6, np.sin(2 * np.pi * root) / root)):
        matrix = np.vander(points * 4.0, count, increasing=True)
        terms = np.linalg.lstsq(matrix, value, rcond=None)[0] * 4.0 ** np.arange(count)
        found.append([float(term) for term in terms])
    return found


COS_POLY, SIN_POLY = _fit()


def dims(left, right):
    return (((left,), (right,)), ((), ()))


def dot(left, right, left_dim=1, right_dim=0, precision=HIGHEST):
    return lax.dot_general(
        left,
        right,
        dims(left_dim, right_dim),
        precision=precision,
        preferred_element_type=jnp.float32,
    )


def half_dot(left, right, left_dim=1, right_dim=0):
    return lax.dot_general(
        left, right, dims(left_dim, right_dim), preferred_element_type=jnp.float32
    )


def split(value):
    high = value.astype(jnp.bfloat16)
    return high, (value - high.astype(jnp.float32)).astype(jnp.bfloat16)


def dot_three(left, right, left_dim=1, right_dim=0):
    left_high, left_low = left
    right_high, right_low = right
    return (
        half_dot(left_high, right_high, left_dim, right_dim)
        + half_dot(left_high, right_low, left_dim, right_dim)
        + half_dot(left_low, right_high, left_dim, right_dim)
    )


def sigmoid(value):
    return 1.0 / (1.0 + jnp.exp(-value))


def lane(shape):
    return lax.broadcasted_iota(jnp.int32, shape, 1)


def row_of(shape):
    return lax.broadcasted_iota(jnp.int32, shape, 0)


def call(kernel, out_shape, *args, scratch=(), vmem=32):
    return pl.pallas_call(
        kernel,
        out_shape=out_shape,
        scratch_shapes=list(scratch),
        compiler_params=pltpu.CompilerParams(vmem_limit_bytes=vmem * 1024 * 1024),
    )(*args)


def f32(*shape):
    return jax.ShapeDtypeStruct(shape, jnp.float32)


def take(row, index):
    return jnp.take_along_axis(
        jnp.broadcast_to(row, index.shape), index, axis=1, mode="promise_in_bounds"
    )


def joined(face, corner, faces, corners):
    return jnp.concatenate(
        [face[f : f + 1, :] for f in faces] + [corner[f : f + 1, :] for f in corners], axis=1
    )


def pack_kernel(pos, species, face, corner, near, far, own):
    even = lax.axis_index("x") % 2 == 0
    rows = [pos[0:1, :], pos[1:2, :], pos[2:3, :], species[...].astype(jnp.float32)]
    where_from = jnp.concatenate(
        [
            joined(face, corner, (2,), (0, 2)),
            joined(face, corner, (3,), (1, 3)),
            joined(face, corner, (0, 1), ()),
            jnp.zeros((5, N), jnp.int32),
        ],
        axis=0,
    )
    for number, row in enumerate(rows):
        got = take(row, where_from)
        near[number : number + 1, :] = jnp.where(even, got[1:2, :], got[0:1, :])
        far[number : number + 1, :] = jnp.where(even, got[0:1, :], got[1:2, :])
        own[number : number + 1, :] = got[2:3, :]
    zero = jnp.zeros((4, N), jnp.float32)
    near[4:8, :] = zero
    far[4:8, :] = zero
    own[4:8, :] = zero


def swapped(value, axes, odd):
    count = math.prod(lax.axis_size(axis) for axis in axes)
    places = [(at, ((((at + odd) % count) ^ 1) - odd) % count) for at in range(count)]
    return lax.ppermute(value, axes, places)


def relay_kernel(own, near, far, one, two):
    at = lane((8, N))
    even = lax.axis_index("x") % 2 == 0
    a = own[...]
    b = jnp.where(even, near[...], far[...])
    d = jnp.where(even, far[...], near[...])
    to_minus = jnp.where(at < 64, a, jnp.where(at < 96, b, pltpu.roll(d, 32, 1)))
    to_plus = jnp.where(
        at < 64, pltpu.roll(a, 64, 1), jnp.where(at < 96, pltpu.roll(b, 96, 1), d)
    )
    first = lax.axis_index("c") == 0
    one[...] = jnp.where(first, to_plus, to_minus)
    two[...] = jnp.where(first, to_minus, to_plus)


def pair_weights(embed, radial):
    scalar, vector = [], []
    for kind in range(KINDS):
        row = embed[kind : kind + 1, :]
        scalar.append(radial[0] * row * 0.25)
        vector.append(radial[1] * row * 0.05)
    return jnp.concatenate(scalar, axis=0), jnp.concatenate(vector, axis=0)


def basis_centers():
    return row_of((BASIS, N)).astype(jnp.float32) * (CUTOFF / (BASIS - 1))


def edge_kernel(
    pos, species, nbr, near_x, far_x, near_y, far_y, embed, radial,
    shared, active, invariants, vectors, sums, edges, places,
):
    at = lane((8, N))
    own = [pos[0:1, :], pos[1:2, :], pos[2:3, :], species[...].astype(jnp.float32)]
    core_zero = lax.axis_index("c") == 0
    even = lax.axis_index("x") % 2 == 0
    first = jnp.where(core_zero, near_x[...], far_x[...])
    second = jnp.where(core_zero, far_x[...], near_x[...])
    plus_y = jnp.where(even, near_y[...], far_y[...])
    minus_y = jnp.where(even, far_y[...], near_y[...])
    third = jnp.where(at < 64, plus_y, pltpu.roll(minus_y, 64, 1))
    line = lane((1, N))
    corner_y = jnp.where(line < 64, 0.0, jnp.where(line < 96, DOMAIN, -DOMAIN))
    tables = [
        own,
        [first[0:1] + DOMAIN, first[1:2] + corner_y, first[2:3], first[3:4]],
        [second[0:1] - DOMAIN, second[1:2] + corner_y, second[2:3], second[3:4]],
        [third[0:1], third[1:2] + jnp.where(line < 64, DOMAIN, -DOMAIN), third[2:3], third[3:4]],
    ]
    for group in range(SLOTS // 8):
        rows = slice(8 * group, 8 * group + 8)
        slot = nbr[rows, :]
        block = lax.shift_right_logical(slot, 6)
        table = jnp.where(
            block < 2,
            0,
            jnp.where(
                (block == 4) | (block == 5), 3, jnp.where((block & 1) == 0, 1, 2)
            ),
        )
        table = jnp.where(block == 8, 4, table)
        half = jnp.where((block == 1) | ((block >= 5) & (block < 8)), 64, 0)
        place = (slot & 63) + half
        found = []
        for number in range(4):
            value = take(tables[0][number], place)
            for other in range(1, 4):
                value = jnp.where(table == other, take(tables[other][number], place), value)
            found.append(value)
        offset = [found[d] - own[d] for d in range(3)]
        dist_sq = offset[0] * offset[0] + offset[1] * offset[1] + offset[2] * offset[2]
        valid = (table < 4).astype(jnp.float32)
        ramp = jnp.maximum(1.0 - dist_sq / (CUTOFF * CUTOFF), 0.0)
        edges[0, rows, :] = offset[0]
        edges[1, rows, :] = offset[1]
        edges[2, rows, :] = offset[2]
        edges[3, rows, :] = found[3]
        edges[4, rows, :] = jnp.sqrt(dist_sq + SOFTEN)
        edges[5, rows, :] = ramp * ramp * valid
        edges[6, rows, :] = (-2.0 / (CUTOFF * CUTOFF)) * ramp * valid
        places[0, rows, :] = table
        places[1, rows, :] = place
    centers = basis_centers()

    def step(slot, carry):
        row = pl.ds(slot, 1)
        away = edges[4, row, :] - centers
        basis = jnp.exp(-WIDTH_GAUSS * away * away) * edges[5, row, :]
        parts = [basis] + [basis * edges[d, row, :] for d in range(3)]
        kind_row = jnp.broadcast_to(edges[3, row, :], (BASIS, N))
        out = []
        for kind in range(KINDS):
            mask = kind_row == float(kind)
            for number in range(4):
                out.append(carry[4 * kind + number] + jnp.where(mask, parts[number], 0.0))
        return tuple(out)

    zero = jnp.zeros((BASIS, N), jnp.float32)
    total = lax.fori_loop(0, SLOTS, step, (zero,) * (4 * KINDS), unroll=4)
    for number in range(4):
        sums[number, :, :] = jnp.concatenate(
            [total[4 * kind + number] for kind in range(KINDS)], axis=0
        )
    scalar_w, vector_w = pair_weights(embed, radial)
    value = dot(sums[0], scalar_w, 0, 0)
    for d in range(3):
        vector = dot(sums[1 + d], vector_w, 0, 0)
        vectors[d, :, :] = vector
        value = value + vector * vector
    invariants[...] = value
    result = value * sigmoid(value)
    active[...] = result
    anchor_x = lax.convert_element_type(lax.axis_index(GX), jnp.float32) * DOMAIN
    anchor_y = lax.convert_element_type(lax.axis_index(GY), jnp.float32) * DOMAIN
    zero_row = jnp.zeros((1, N), jnp.float32)
    tail = jnp.concatenate(
        [own[0] + anchor_x, own[1] + anchor_y, own[2], own[3]] + [zero_row] * 4, axis=0
    )
    for member in range(MEMBERS):
        shared[member, 0:N, :] = result
        shared[member, N : N + 8, :] = tail


def edge_back_kernel(
    tiles, active, invariants, vectors, sums, edges, places, embed, radial, w_up, w_charge,
    species, grad_out, read_row,
    payload, own_grad, charge_piece,
):
    total = tiles[0]
    for member in range(1, MEMBERS):
        total = total + tiles[member]
    grad_charges = jnp.transpose(total[0:N, :])
    updated = grad_out[...] + dot(grad_charges, w_charge[...], 1, 1)
    value = invariants[...]
    logistic = sigmoid(value)
    slope = logistic * (1.0 + value * (1.0 - logistic))
    grad_inv = dot(updated, w_up[...], 1, 1) * slope
    scalar_w, vector_w = pair_weights(embed, radial)
    pulls = [dot(scalar_w, grad_inv, 1, 1)]
    grad_scalar = dot(sums[0], grad_inv)
    grad_vector = jnp.zeros((KINDS * BASIS, N), jnp.float32)
    for d in range(3):
        along = 2.0 * vectors[d] * grad_inv
        pulls.append(dot(vector_w, along, 1, 1))
        grad_vector = grad_vector + dot(sums[1 + d], along)
    onehot = (row_of((8, N)) == species[...]).astype(jnp.float32)
    grad_table = dot(onehot, updated)
    radial_zero = jnp.zeros((BASIS, N), jnp.float32)
    radial_one = jnp.zeros((BASIS, N), jnp.float32)
    table_rows = []
    for kind in range(KINDS):
        rows = slice(kind * BASIS, (kind + 1) * BASIS)
        row = embed[kind : kind + 1, :]
        part_zero, part_one = grad_scalar[rows] * 0.25, grad_vector[rows] * 0.05
        radial_zero = radial_zero + part_zero * row
        radial_one = radial_one + part_one * row
        table_rows.append(
            grad_table[kind : kind + 1]
            + jnp.sum(radial[0] * part_zero + radial[1] * part_one, axis=0, keepdims=True)
        )
    rest = jnp.concatenate(
        [radial_zero, radial_one] + table_rows + [read_row[...], jnp.zeros((1, N), jnp.float32)],
        axis=0,
    )
    up_piece = total[N + 8 : N + 24, :]
    charge_piece[...] = total[N + 24 : N + 40, :]
    centers = basis_centers()
    sub = row_of((8, N))
    sub_table = sub & 3
    high_rows = sub < 4
    lane_rows = row_of((N, N))
    pull = [
        [pulls[number][kind * BASIS : (kind + 1) * BASIS] for number in range(4)]
        for kind in range(KINDS)
    ]

    def step(slot, carry):
        row = pl.ds(slot, 1)
        kind_row = jnp.broadcast_to(edges[3, row, :], (BASIS, N))
        own_pull = list(pull[KINDS - 1])
        for kind in range(KINDS - 1):
            mask = kind_row == float(kind)
            own_pull = [jnp.where(mask, pull[kind][n], own_pull[n]) for n in range(4)]
        radius = edges[4, row, :]
        envelope = edges[5, row, :]
        away = radius - centers
        bell = jnp.exp(-WIDTH_GAUSS * away * away)
        offset = [jnp.broadcast_to(edges[d, row, :], (BASIS, N)) for d in range(3)]
        by_basis = own_pull[0]
        for d in range(3):
            by_basis = by_basis + offset[d] * own_pull[1 + d]
        by_square = by_basis * bell * (edges[6, row, :] - (2.0 * envelope / radius) * away)
        basis = bell * envelope
        table = jnp.broadcast_to(places[0, row, :], (8, N)) == sub_table
        place = lane_rows == places[1, row, :]
        onehot = jnp.where(place, 1.0, 0.0).astype(jnp.bfloat16)
        centre, pieces = [], []
        for d in range(3):
            part = basis * own_pull[1 + d] + 2.0 * offset[d] * by_square
            centre.append(carry[d] + part)
            whole = jnp.broadcast_to(jnp.sum(part, axis=0, keepdims=True), (8, N))
            high = whole.astype(jnp.bfloat16).astype(jnp.float32)
            pieces.append(jnp.where(table, jnp.where(high_rows, high, whole - high), 0.0))
        rows = jnp.concatenate(pieces, axis=0).astype(jnp.bfloat16)
        return (*centre, carry[3] + half_dot(rows, onehot, 1, 1))

    zero = jnp.zeros((8, N), jnp.float32)
    out = lax.fori_loop(
        0, SLOTS, step, (zero, zero, zero, jnp.zeros((24, N), jnp.float32)), unroll=4
    )
    scattered = out[3]
    waves = total[N : N + 8, :]
    own_rows, one_rows, two_rows, three_rows = [], [], [], []
    for d in range(3):
        both = scattered[8 * d : 8 * d + 4] + scattered[8 * d + 4 : 8 * d + 8]
        centre = jnp.sum(out[d], axis=0, keepdims=True)
        own_rows.append(both[0:1] - centre + waves[d : d + 1])
        one_rows.append(both[1:2])
        two_rows.append(both[2:3])
        three_rows.append(both[3:4])
    pad = [jnp.zeros((5, N), jnp.float32)]
    own_grad[...] = jnp.concatenate(own_rows + pad, axis=0)
    depth_of = [depth_after(step_x, step_y) for step_x, step_y in TABLE_DIRS]
    line = lane((8, N))
    ones = jnp.concatenate(one_rows + pad, axis=0)
    twos = jnp.concatenate(two_rows + pad, axis=0)
    threes = jnp.concatenate(three_rows + pad, axis=0)
    home_one = segments(line, depth_of[0:3])
    home_two = segments(line, depth_of[3:6])
    home_three = jnp.where(line < 64, depth_of[6], depth_of[7])
    for other in range(8):
        payload[other, 0:16, :] = up_piece
        payload[other, 16:40, :] = rest
        payload[other, 40:48, :] = pack_six(
            jnp.where(home_one == other, ones, 0.0), jnp.where(home_two == other, twos, 0.0)
        )
        payload[other, 48:56, :] = jnp.where(home_three == other, threes, 0.0)


TABLE_DIRS = ((1, 0), (1, 1), (1, -1), (-1, 0), (-1, 1), (-1, -1), (0, 1), (0, -1))


def segments(line, values):
    return jnp.where(line < 64, values[0], jnp.where(line < 96, values[1], values[2]))


def pack_six(one, two):
    return jnp.where(row_of((8, N)) < 4, one, pltpu.roll(two, 4, 0))


def depth_after(step_x, step_y):
    core, high = lax.axis_index("c"), lax.axis_index("zh")
    low, column = lax.axis_index("zl"), lax.axis_index("x")
    if step_x == 1:
        high = jnp.where(core == 1, (high + 1) % 4, high)
    if step_x == -1:
        high = jnp.where(core == 0, (high + 3) % 4, high)
    if step_y == 1:
        low = jnp.where(column == 3, 1 - low, low)
    if step_y == -1:
        low = jnp.where(column == 0, 1 - low, low)
    return high * 2 + low


def plane_after(step_x, step_y):
    core, high = lax.axis_index("c"), lax.axis_index("zh")
    row, column = lax.axis_index("y"), lax.axis_index("x")
    if step_x == 1:
        row = jnp.where((core == 1) & (high == 0), (row + 1) % 4, row)
    if step_x == -1:
        row = jnp.where((core == 0) & (high == 3), (row + 3) % 4, row)
    return row * 4 + (column + step_y + 4) % 4


def depth_sum_kernel(tiles, charge_piece, out):
    total = jnp.sum(tiles[...], axis=0)
    place_of = [plane_after(step_x, step_y) for step_x, step_y in TABLE_DIRS]
    line = lane((8, N))
    home = jnp.where(
        row_of((8, N)) < 4, segments(line, place_of[0:3]), segments(line, place_of[3:6])
    )
    home_three = jnp.where(line < 64, place_of[6], place_of[7])
    sixes, threes = total[40:48], total[48:56]
    row = lax.axis_index("y")
    quarter = charge_piece[0:4, :]
    for number in range(1, 4):
        quarter = jnp.where(row == number, charge_piece[4 * number : 4 * number + 4, :], quarter)
    for other in range(16):
        out[other, 0:40, :] = total[0:40]
        out[other, 40:48, :] = jnp.where(home == other, sixes, 0.0)
        out[other, 48:56, :] = jnp.where(home_three == other, threes, 0.0)
        out[other, 52:56, :] = quarter


def plane_sum_kernel(tiles, swap, threes):
    for column in range(4):
        total = tiles[column, 0:16, :]
        for row in range(1, 4):
            total = total + tiles[4 * row + column, 0:16, :]
        swap[16 * column : 16 * column + 16, :] = total
        for row in range(4):
            at = 96 + 16 * column + 4 * row
            swap[at : at + 4, :] = tiles[4 * row + column, 52:56, :]
    rest = tiles[0, 16:56, :]
    for other in range(1, 16):
        rest = rest + tiles[other, 16:56, :]
    swap[64:96, :] = rest[0:32]
    threes[...] = jnp.where(row_of((8, N)) < 4, rest[32:40], 0.0)


def finish_kernel(own, other, threes, own_grad, face, corner, forces, grad_embed, grad_radial, grad_up,
                  grad_charge, grad_read):
    mean = 1.0 / ATOMS
    core = lax.axis_index("c")
    mine = pl.ds(pl.multiple_of(core * 64, 64), 64)
    theirs = pl.ds(pl.multiple_of((1 - core) * 64, 64), 64)
    grad_up[mine, :] = own[0:64, :] * mean
    grad_up[theirs, :] = other[0:64, :] * mean
    grad_charge[mine, :] = own[96:160, :] * mean
    grad_charge[theirs, :] = other[96:160, :] * mean
    total = (own[64:88, :] + other[64:88, :]) * mean
    grad_radial[0, :, :] = total[0:8]
    grad_radial[1, :, :] = total[8:16]
    grad_embed[...] = total[16:22]
    grad_read[...] = total[22:23]
    sixes = other[88:96, :]
    grad = own_grad[...]
    lane_rows = row_of((N, N))
    for piece, faces, corners in (
        (sixes, (0,), (0, 1)),
        (pltpu.roll(sixes, 4, 0), (1,), (2, 3)),
        (threes[...], (2, 3), ()),
    ):
        onehot = jnp.where(lane_rows == joined(face, corner, faces, corners), 1.0, 0.0)
        grad = grad + dot(piece, onehot, 1, 1)
    forces[...] = -grad[0:3, :]


def spread_kernel(*refs):
    out = refs[-1]
    core, column = lax.axis_index("c"), lax.axis_index("x")
    for number, shard in enumerate(refs[:-1]):
        source = (column + 4 - number % 4) % 4
        member = jnp.where(number < 4, core, 1 - core) * 4 + source
        out[pl.ds(pl.multiple_of(member * SHARD, SHARD), SHARD), :] = shard[...]


def structure_kernel(shared, kvec, embed, w_up, w_charge, factor, wave_high, wave_low, charges,
                     feature_high, feature_low):
    me = lax.axis_index(GROUP)
    at = pl.multiple_of(me * SHARD, SHARD)
    rows = jnp.concatenate(
        [kvec[:, pl.ds(at, SHARD)], jnp.zeros((5, SHARD), jnp.float32)], axis=0
    )
    turns = jnp.transpose(rows * (1.0 / (2.0 * math.pi)))
    table = jnp.concatenate([embed[...], jnp.zeros((2, N), jnp.float32)], axis=0)
    up = split(w_up[...])
    charge_w = split(w_charge[...])
    for member in range(MEMBERS):
        part = slice(member * N, (member + 1) * N)
        tail = shared[member, N : N + 8, :]
        onehot = (row_of((8, N)).astype(jnp.float32) == tail[3:4, :]).astype(jnp.float32)
        feature = dot(onehot, table, 0, 0) + dot_three(split(shared[member, 0:N, :]), up)
        high, low = split(feature)
        feature_high[part, :] = high
        feature_low[part, :] = low
        charges[part, :] = dot_three((high, low), charge_w)
        for chunk in range(SHARD // 64):
            waves = slice(chunk * 64, chunk * 64 + 64)
            angle = (
                turns[waves, 0:1] * tail[0:1, :]
                + turns[waves, 1:2] * tail[1:2, :]
                + turns[waves, 2:3] * tail[2:3, :]
            )
            angle = angle - jnp.round(angle)
            square = angle * angle
            cosine = jnp.full(square.shape, COS_POLY[-1], jnp.float32)
            for value in COS_POLY[-2::-1]:
                cosine = cosine * square + value
            sine = jnp.full(square.shape, SIN_POLY[-1], jnp.float32)
            for value in SIN_POLY[-2::-1]:
                sine = sine * square + value
            sine = sine * angle
            high, low = split(cosine)
            wave_high[waves, part] = high
            wave_low[waves, part] = low
            high, low = split(sine)
            waves = slice(SHARD + chunk * 64, SHARD + chunk * 64 + 64)
            wave_high[waves, part] = high
            wave_low[waves, part] = low
    project(wave_high, wave_low, feature_high[...], feature_low[...], factor)


def project(wave_high, wave_low, high, low, out):
    both = jnp.concatenate([high, low], axis=1)
    wide = half_dot(wave_high[...], both)
    total = wide[:, 0:N] + wide[:, N:] + half_dot(wave_low[...], high)
    out[...] = total.reshape(CROSSES, 16, N)


def projection_kernel(gathered, wave_high, wave_low, out):
    high, low = split(gathered[...].reshape(MEMBERS * N, N))
    project(wave_high, wave_low, high, low, out)


def sum_kernel(tiles, out):
    total = jnp.sum(tiles[...], axis=0)
    for other in range(out.shape[0]):
        out[other, :, :] = total


def filter_of(kfilter):
    me = lax.axis_index(GROUP)
    return kfilter[pl.ds(pl.multiple_of(me * SHARD, SHARD), SHARD), :] * SCALE


def waves_to_atoms(field, wave_high, wave_low):
    high, low = split(jnp.transpose(field))
    wide = half_dot(jnp.concatenate([high, low], axis=0), wave_high[...])
    return wide[0:N] + wide[N:] + half_dot(high, wave_low[...])


def potential_kernel(factor, w_charge, kfilter, wave_high, wave_low, out, weighted, charge_factor):
    scaled = filter_of(kfilter)
    charged = dot(factor[...], w_charge[...])
    charge_factor[...] = charged
    field = charged * jnp.concatenate([scaled, scaled], axis=0)
    weighted[...] = field
    total = waves_to_atoms(field, wave_high, wave_low)
    for member in range(MEMBERS):
        out[member, :, :] = total[:, member * N : (member + 1) * N]


def energy_kernel(tiles, active, species, embed, w_up, read,
                  shared, grad_out, energy, read_row, up_part):
    total = tiles[0]
    for member in range(1, MEMBERS):
        total = total + tiles[member]
    table = jnp.concatenate([embed[...], jnp.zeros((2, N), jnp.float32)], axis=0)
    onehot = (row_of((8, N)) == species[...]).astype(jnp.float32)
    act = active[...]
    combined = dot(onehot, table, 0, 0) + dot(act, w_up[...]) + jnp.transpose(total)
    logistic = sigmoid(combined)
    result = combined * logistic
    weights = read[...]
    energy[...] = dot(jnp.broadcast_to(weights, (8, N)), result, 1, 1)[0:1, :]
    read_row[...] = jnp.sum(result, axis=0, keepdims=True)
    grad = weights * (logistic * (1.0 + combined * (1.0 - logistic)))
    grad_out[...] = grad
    up_part[...] = dot(act, grad, 0, 0)
    for member in range(MEMBERS):
        shared[member, :, :] = grad


def wave_trig(wave_high, wave_low):
    cosine = wave_high[0:SHARD, :].astype(jnp.float32) + wave_low[0:SHARD, :].astype(jnp.float32)
    sine = wave_high[SHARD:, :].astype(jnp.float32) + wave_low[SHARD:, :].astype(jnp.float32)
    return cosine, sine


def by_position(fields, atoms, kvec, wave_high, wave_low):
    along = dot_three(split(fields), split(atoms), 1, 1)
    cosine, sine = wave_trig(wave_high, wave_low)
    phase = cosine * along[SHARD:] - sine * along[0:SHARD]
    me = lax.axis_index(GROUP)
    rows = jnp.concatenate(
        [
            kvec[:, pl.ds(pl.multiple_of(me * SHARD, SHARD), SHARD)],
            jnp.zeros((5, SHARD), jnp.float32),
        ],
        axis=0,
    )
    return dot_three(split(rows), split(phase))


def wave_back_kernel(projected, factor, charge_factor, weighted, kfilter, kvec, wave_high, wave_low,
                     gathered, charges, shared, w_charge, up_part, out, grad_filter):
    scaled = filter_of(kfilter)
    proj = projected[...]
    mixed = charge_factor[...] * proj
    grad_filter[...] = SCALE * (mixed[0:SHARD] + mixed[SHARD:])
    field = proj * jnp.concatenate([scaled, scaled], axis=0)
    charge_grad = dot_three(split(factor[...]), split(field), 0, 0)
    by_charge = waves_to_atoms(field, wave_high, wave_low)
    active = jnp.concatenate([shared[member, 0:N, :] for member in range(MEMBERS)], axis=0)
    mix = dot_three(split(by_charge), split(active))
    up_grad = dot(mix, w_charge[...], 0, 1) + up_part[...]
    by_pos = by_position(
        jnp.concatenate([weighted[...], field], axis=1),
        jnp.concatenate([gathered[...].reshape(MEMBERS * N, N), charges[...]], axis=1),
        kvec, wave_high, wave_low,
    )
    for member in range(MEMBERS):
        part = slice(member * N, (member + 1) * N)
        out[member, 0:N, :] = by_charge[:, part]
        out[member, N : N + 8, :] = by_pos[:, part]
        out[member, N + 8 : N + 24, :] = up_grad[member * 16 : (member + 1) * 16]
        out[member, N + 24 : N + 40, :] = charge_grad[member * 16 : (member + 1) * 16]


def body(
    positions, species, neighbours, face_sends, corner_sends,
    embed, radial, w_up, w_charge, kvec, kfilter, read,
):
    species = species.reshape(1, N)
    read = read.reshape(1, N)
    near, far, own_x = call(
        pack_kernel, (f32(8, N),) * 3, positions, species, face_sends, corner_sends
    )
    near_y, far_y = swapped(near, GY, 0), swapped(far, GY, 1)
    near, far = call(relay_kernel, (f32(8, N),) * 2, own_x, near_y, far_y)
    near_x, far_x = swapped(near, GX, 0), swapped(far, GX, 1)
    shared, active, invariants, vectors, sums, edges, places = call(
        edge_kernel,
        (
            f32(MEMBERS, N + 8, N), f32(N, N), f32(N, N), f32(3, N, N), f32(4, KINDS * BASIS, N),
            f32(7, SLOTS, N), jax.ShapeDtypeStruct((2, SLOTS, N), jnp.int32),
        ),
        positions, species, neighbours, near_x, far_x, near_y, far_y, embed, radial,
    )
    shared = lax.all_to_all(shared, GROUP, 0, 0)
    half = jax.ShapeDtypeStruct((2 * SHARD, MEMBERS * N), jnp.bfloat16)
    scratch = pltpu.VMEM((MEMBERS * N, N), jnp.bfloat16)
    factor, wave_high, wave_low, charges = call(
        structure_kernel,
        (f32(CROSSES, 16, N), half, half, f32(MEMBERS * N, N)),
        shared, kvec, embed, w_up, w_charge,
        scratch=(scratch, scratch),
    )

    def cross_sum(tiles):
        tiles = lax.all_to_all(tiles, CROSS, 0, 0)
        tiles = call(sum_kernel, f32(CROSSES, 16, N), tiles)
        return lax.all_to_all(tiles, CROSS, 0, 0).reshape(2 * SHARD, N)

    factor = cross_sum(factor)
    potential, weighted, charge_factor = call(
        potential_kernel,
        (f32(MEMBERS, N, N), f32(2 * SHARD, N), f32(2 * SHARD, N)),
        factor, w_charge, kfilter, wave_high, wave_low,
    )
    potential = lax.all_to_all(potential, GROUP, 0, 0)
    gathered, grad_out, energy, read_row, up_part = call(
        energy_kernel,
        (f32(MEMBERS, N, N), f32(N, N), f32(1, N), f32(1, N), f32(N, N)),
        potential, active, species, embed, w_up, read,
    )
    gathered = lax.all_to_all(gathered, GROUP, 0, 0)
    projected = call(projection_kernel, f32(CROSSES, 16, N), gathered, wave_high, wave_low)
    projected = cross_sum(projected)
    tiles, shard = call(
        wave_back_kernel,
        (f32(MEMBERS, N + 40, N), f32(SHARD, N)),
        projected, factor, charge_factor, weighted, kfilter, kvec, wave_high, wave_low,
        gathered, charges, shared, w_charge, up_part,
    )
    swap = [(0, 1), (1, 0)]
    shards = [shard] + [
        lax.ppermute(shard, "x", [(at, (at + step) % 4) for at in range(4)]) for step in (1, 2, 3)
    ]
    shards += [lax.ppermute(value, "c", swap) for value in shards]
    tiles = lax.all_to_all(tiles, GROUP, 0, 0)
    payload, own_grad, charge_piece = call(
        edge_back_kernel,
        (f32(8, 56, N), f32(8, N), f32(16, N)),
        tiles, active, invariants, vectors, sums, edges, places, embed, radial, w_up,
        w_charge, species, grad_out, read_row,
    )
    payload = lax.all_to_all(payload, DEPTH, 0, 0)
    payload = call(depth_sum_kernel, f32(16, 56, N), payload, charge_piece)
    payload = lax.all_to_all(payload, PLANE, 0, 0)
    payload, threes = call(plane_sum_kernel, (f32(160, N), f32(8, N)), payload)
    other = lax.ppermute(payload, "c", swap)
    grad_filter = call(spread_kernel, f32(WAVES, N), *shards)
    forces, grad_embed, grad_radial, grad_up, grad_charge, grad_read = call(
        finish_kernel,
        (f32(3, N), f32(KINDS, N), f32(2, BASIS, N), f32(N, N), f32(N, N), f32(1, N)),
        payload, other, threes, own_grad, face_sends, corner_sends,
    )
    return (
        energy.reshape(N), forces, grad_embed, grad_radial, grad_up, grad_charge, grad_filter,
        grad_read.reshape(N),
    )


def solution(mesh):
    fine = Mesh(mesh.devices.reshape(4, 4, 2, 2, 4), ALL)
    atoms = P(ALL)
    rows = P(None, ALL)
    return jax.shard_map(
        body,
        mesh=fine,
        in_specs=(rows, atoms, rows, rows, rows) + (P(),) * 7,
        out_specs=(atoms, rows) + (P(),) * 6,
        check_vma=False,
    )
```

```python
import functools
import math

import jax
import jax.numpy as jnp
from jax import lax
from jax.experimental import pallas as pl
from jax.experimental.pallas import tpu as pltpu
from jax.sharding import Mesh
from jax.sharding import PartitionSpec as P

CUTOFF = 5.0
SOFTEN = 0.01
WIDTH_GAUSS = 2.0
DOMAIN = 8.8
N = 128
SLOTS = 64
KINDS = 6
BASIS = 8
WAVES = 2048
ATOMS = 32768
SHARD = 256
HIGHEST = lax.Precision.HIGHEST
SCALE = 1.0 / math.sqrt(ATOMS * WAVES)

GX = ("y", "zh", "c")
GY = ("zl", "x")
ALL = GX + GY
GROUP = ("c", "x")
CROSS = ("y", "zh", "zl")
MEMBERS = 8
CROSSES = 32
DEPTH = ("zh", "zl")
PLANE = ("y", "x")

COS_POLY = None
SIN_POLY = None


def _fit():
    import numpy as np

    points = (1.0 + np.cos(np.pi * (np.arange(200) + 0.5) / 200)) / 8.0
    root = np.sqrt(points)
    found = []
    for count, value in ((7, np.cos(2 * np.pi * root)), (6, np.sin(2 * np.pi * root) / root)):
        matrix = np.vander(points * 4.0, count, increasing=True)
        terms = np.linalg.lstsq(matrix, value, rcond=None)[0] * 4.0 ** np.arange(count)
        found.append([float(term) for term in terms])
    return found


COS_POLY, SIN_POLY = _fit()


def dims(left, right):
    return (((left,), (right,)), ((), ()))


def dot(left, right, left_dim=1, right_dim=0, precision=HIGHEST):
    return lax.dot_general(
        left,
        right,
        dims(left_dim, right_dim),
        precision=precision,
        preferred_element_type=jnp.float32,
    )


def half_dot(left, right, left_dim=1, right_dim=0):
    return lax.dot_general(
        left, right, dims(left_dim, right_dim), preferred_element_type=jnp.float32
    )


def split(value):
    high = value.astype(jnp.bfloat16)
    return high, (value - high.astype(jnp.float32)).astype(jnp.bfloat16)


def dot_three(left, right, left_dim=1, right_dim=0):
    left_high, left_low = left
    right_high, right_low = right
    return (
        half_dot(left_high, right_high, left_dim, right_dim)
        + half_dot(left_high, right_low, left_dim, right_dim)
        + half_dot(left_low, right_high, left_dim, right_dim)
    )


def sigmoid(value):
    return 1.0 / (1.0 + jnp.exp(-value))


def lane(shape):
    return lax.broadcasted_iota(jnp.int32, shape, 1)


def row_of(shape):
    return lax.broadcasted_iota(jnp.int32, shape, 0)


def call(kernel, out_shape, *args, scratch=(), vmem=32, far=False, cost=None):
    more = {"in_specs": [pl.BlockSpec(memory_space=pltpu.HBM)] * len(args)} if far else {}
    return pl.pallas_call(
        kernel,
        out_shape=out_shape,
        scratch_shapes=list(scratch),
        cost_estimate=cost,
        **more,
        compiler_params=pltpu.CompilerParams(vmem_limit_bytes=vmem * 1024 * 1024),
    )(*args)


def f32(*shape):
    return jax.ShapeDtypeStruct(shape, jnp.float32)


def i32(*shape):
    return jax.ShapeDtypeStruct(shape, jnp.int32)


def take(row, index):
    return jnp.take_along_axis(
        jnp.broadcast_to(row, index.shape), index, axis=1, mode="promise_in_bounds"
    )


def joined(face, corner, faces, corners):
    return jnp.concatenate(
        [face[f : f + 1, :] for f in faces] + [corner[f : f + 1, :] for f in corners], axis=1
    )


def pack_kernel(pos_in, species_in, face_in, corner_in, nbr_in, embed_in, radial_in, read_in,
                near, far, own, home, pos, species, nbr, embed, radial, read, face, corner, sems):
    pairs = (
        (pos_in, pos), (species_in, species), (face_in, face), (corner_in, corner),
        (nbr_in, nbr), (embed_in, embed), (radial_in, radial), (read_in, read),
    )
    copies = [
        pltpu.make_async_copy(source, target, sems.at[number])
        for number, (source, target) in enumerate(pairs)
    ]
    for copy in copies:
        copy.start()
    for copy in copies:
        copy.wait()
    even = lax.axis_index("x") % 2 == 0
    rows = [pos[0:1, :], pos[1:2, :], pos[2:3, :], species[...].astype(jnp.float32)]
    padding = jnp.zeros((5, N), jnp.int32)
    where_from = jnp.concatenate(
        [
            joined(face, corner, (2,), (0, 2)),
            joined(face, corner, (3,), (1, 3)),
            joined(face, corner, (0, 1), ()),
            padding,
        ],
        axis=0,
    )
    home[...] = jnp.concatenate(
        [
            joined(face, corner, (0,), (0, 1)),
            joined(face, corner, (1,), (2, 3)),
            joined(face, corner, (2, 3), ()),
            padding,
        ],
        axis=0,
    )
    for number, row in enumerate(rows):
        got = take(row, where_from)
        near[number : number + 1, :] = jnp.where(even, got[1:2, :], got[0:1, :])
        far[number : number + 1, :] = jnp.where(even, got[0:1, :], got[1:2, :])
        own[number : number + 1, :] = got[2:3, :]
    zero = jnp.zeros((4, N), jnp.float32)
    near[4:8, :] = zero
    far[4:8, :] = zero
    own[4:8, :] = zero


def swapped(value, axes, odd):
    count = math.prod(lax.axis_size(axis) for axis in axes)
    places = [(at, ((((at + odd) % count) ^ 1) - odd) % count) for at in range(count)]
    return lax.ppermute(value, axes, places)


def relay_kernel(own, near, far, one, two):
    at = lane((8, N))
    even = lax.axis_index("x") % 2 == 0
    a = own[...]
    b = jnp.where(even, near[...], far[...])
    d = jnp.where(even, far[...], near[...])
    to_minus = jnp.where(at < 64, a, jnp.where(at < 96, b, pltpu.roll(d, 32, 1)))
    to_plus = jnp.where(
        at < 64, pltpu.roll(a, 64, 1), jnp.where(at < 96, pltpu.roll(b, 96, 1), d)
    )
    first = lax.axis_index("c") == 0
    one[...] = jnp.where(first, to_plus, to_minus)
    two[...] = jnp.where(first, to_minus, to_plus)


def pair_weights(embed, radial):
    scalar, vector = [], []
    for kind in range(KINDS):
        row = embed[kind : kind + 1, :]
        scalar.append(radial[0] * row * 0.25)
        vector.append(radial[1] * row * 0.05)
    return jnp.concatenate(scalar, axis=0), jnp.concatenate(vector, axis=0)


def basis_centers():
    return row_of((BASIS, N)).astype(jnp.float32) * (CUTOFF / (BASIS - 1))


def edge_kernel(
    pos, species, nbr, near_x, far_x, near_y, far_y, embed, radial,
    shared, active, invariants, vectors, sums, edges, places,
):
    at = lane((8, N))
    own = [pos[0:1, :], pos[1:2, :], pos[2:3, :], species[...].astype(jnp.float32)]
    core_zero = lax.axis_index("c") == 0
    even = lax.axis_index("x") % 2 == 0
    first = jnp.where(core_zero, near_x[...], far_x[...])
    second = jnp.where(core_zero, far_x[...], near_x[...])
    plus_y = jnp.where(even, near_y[...], far_y[...])
    minus_y = jnp.where(even, far_y[...], near_y[...])
    third = jnp.where(at < 64, plus_y, pltpu.roll(minus_y, 64, 1))
    line = lane((1, N))
    corner_y = jnp.where(line < 64, 0.0, jnp.where(line < 96, DOMAIN, -DOMAIN))
    tables = [
        own,
        [first[0:1] + DOMAIN, first[1:2] + corner_y, first[2:3], first[3:4]],
        [second[0:1] - DOMAIN, second[1:2] + corner_y, second[2:3], second[3:4]],
        [third[0:1], third[1:2] + jnp.where(line < 64, DOMAIN, -DOMAIN), third[2:3], third[3:4]],
    ]
    for group in range(SLOTS // 8):
        rows = slice(8 * group, 8 * group + 8)
        slot = nbr[rows, :]
        block = lax.shift_right_logical(slot, 6)
        table = jnp.where(
            block < 2,
            0,
            jnp.where(
                (block == 4) | (block == 5), 3, jnp.where((block & 1) == 0, 1, 2)
            ),
        )
        table = jnp.where(block == 8, 4, table)
        half = jnp.where((block == 1) | ((block >= 5) & (block < 8)), 64, 0)
        place = (slot & 63) + half
        found = []
        for number in range(4):
            value = take(tables[0][number], place)
            for other in range(1, 4):
                value = jnp.where(table == other, take(tables[other][number], place), value)
            found.append(value)
        offset = [found[d] - own[d] for d in range(3)]
        dist_sq = offset[0] * offset[0] + offset[1] * offset[1] + offset[2] * offset[2]
        valid = (table < 4).astype(jnp.float32)
        ramp = jnp.maximum(1.0 - dist_sq / (CUTOFF * CUTOFF), 0.0)
        edges[0, rows, :] = offset[0]
        edges[1, rows, :] = offset[1]
        edges[2, rows, :] = offset[2]
        edges[3, rows, :] = found[3]
        edges[4, rows, :] = jnp.sqrt(dist_sq + SOFTEN)
        edges[5, rows, :] = ramp * ramp * valid
        edges[6, rows, :] = (-2.0 / (CUTOFF * CUTOFF)) * ramp * valid
        places[0, rows, :] = table
        places[1, rows, :] = place
    centers = basis_centers()

    def step(slot, carry):
        row = pl.ds(slot, 1)
        away = edges[4, row, :] - centers
        basis = jnp.exp(-WIDTH_GAUSS * away * away) * edges[5, row, :]
        parts = [basis] + [basis * edges[d, row, :] for d in range(3)]
        kind_row = jnp.broadcast_to(edges[3, row, :], (BASIS, N))
        out = []
        for kind in range(KINDS):
            mask = kind_row == float(kind)
            for number in range(4):
                out.append(carry[4 * kind + number] + jnp.where(mask, parts[number], 0.0))
        return tuple(out)

    zero = jnp.zeros((BASIS, N), jnp.float32)
    total = lax.fori_loop(0, SLOTS, step, (zero,) * (4 * KINDS), unroll=4)
    for number in range(4):
        sums[number, :, :] = jnp.concatenate(
            [total[4 * kind + number] for kind in range(KINDS)], axis=0
        )
    scalar_w, vector_w = pair_weights(embed, radial)
    value = dot(sums[0], scalar_w, 0, 0)
    for d in range(3):
        vector = dot(sums[1 + d], vector_w, 0, 0)
        vectors[d, :, :] = vector
        value = value + vector * vector
    invariants[...] = value
    result = value * sigmoid(value)
    active[...] = result
    anchor_x = lax.convert_element_type(lax.axis_index(GX), jnp.float32) * DOMAIN
    anchor_y = lax.convert_element_type(lax.axis_index(GY), jnp.float32) * DOMAIN
    zero_row = jnp.zeros((1, N), jnp.float32)
    tail = jnp.concatenate(
        [own[0] + anchor_x, own[1] + anchor_y, own[2], own[3]] + [zero_row] * 4, axis=0
    )
    for member in range(4):
        shared[member, 0:N, :] = result
        shared[member, N : N + 8, :] = tail


def edge_back_kernel(
    tiles, active, invariants, vectors, sums, edges, places, embed, radial, w_up, w_charge,
    species, grad_out, read_row,
    payload, own_grad, charge_piece,
):
    total = tiles[0]
    for member in range(1, 4):
        total = total + tiles[member]
    grad_charges = jnp.transpose(total[0:N, :])
    updated = grad_out[...] + dot(grad_charges, w_charge[...], 1, 1)
    value = invariants[...]
    logistic = sigmoid(value)
    slope = logistic * (1.0 + value * (1.0 - logistic))
    grad_inv = dot(updated, w_up[...], 1, 1) * slope
    scalar_w, vector_w = pair_weights(embed, radial)
    pulls = [dot(scalar_w, grad_inv, 1, 1)]
    grad_scalar = dot(sums[0], grad_inv)
    grad_vector = jnp.zeros((KINDS * BASIS, N), jnp.float32)
    for d in range(3):
        along = 2.0 * vectors[d] * grad_inv
        pulls.append(dot(vector_w, along, 1, 1))
        grad_vector = grad_vector + dot(sums[1 + d], along)
    onehot = (row_of((8, N)) == species[...]).astype(jnp.float32)
    grad_table = dot(onehot, updated)
    radial_zero = jnp.zeros((BASIS, N), jnp.float32)
    radial_one = jnp.zeros((BASIS, N), jnp.float32)
    table_rows = []
    for kind in range(KINDS):
        rows = slice(kind * BASIS, (kind + 1) * BASIS)
        row = embed[kind : kind + 1, :]
        part_zero, part_one = grad_scalar[rows] * 0.25, grad_vector[rows] * 0.05
        radial_zero = radial_zero + part_zero * row
        radial_one = radial_one + part_one * row
        table_rows.append(
            grad_table[kind : kind + 1]
            + jnp.sum(radial[0] * part_zero + radial[1] * part_one, axis=0, keepdims=True)
        )
    rest = jnp.concatenate(
        [radial_zero, radial_one] + table_rows + [read_row[...], jnp.zeros((1, N), jnp.float32)],
        axis=0,
    )
    up_piece = total[N + 8 : N + 24, :]
    charge_piece[...] = total[N + 24 : N + 40, :]
    centers = basis_centers()
    sub = row_of((8, N))
    sub_table = sub & 3
    high_rows = sub < 4
    lane_rows = row_of((N, N))
    pull = [
        [pulls[number][kind * BASIS : (kind + 1) * BASIS] for number in range(4)]
        for kind in range(KINDS)
    ]

    def step(slot, carry):
        row = pl.ds(slot, 1)
        kind_row = jnp.broadcast_to(edges[3, row, :], (BASIS, N))
        own_pull = list(pull[KINDS - 1])
        for kind in range(KINDS - 1):
            mask = kind_row == float(kind)
            own_pull = [jnp.where(mask, pull[kind][n], own_pull[n]) for n in range(4)]
        radius = edges[4, row, :]
        envelope = edges[5, row, :]
        away = radius - centers
        bell = jnp.exp(-WIDTH_GAUSS * away * away)
        offset = [jnp.broadcast_to(edges[d, row, :], (BASIS, N)) for d in range(3)]
        by_basis = own_pull[0]
        for d in range(3):
            by_basis = by_basis + offset[d] * own_pull[1 + d]
        by_square = by_basis * bell * (edges[6, row, :] - (2.0 * envelope / radius) * away)
        basis = bell * envelope
        table = jnp.broadcast_to(places[0, row, :], (8, N)) == sub_table
        place = lane_rows == places[1, row, :]
        onehot = jnp.where(place, 1.0, 0.0).astype(jnp.bfloat16)
        centre, pieces = [], []
        for d in range(3):
            part = basis * own_pull[1 + d] + 2.0 * offset[d] * by_square
            centre.append(carry[d] + part)
            whole = jnp.broadcast_to(jnp.sum(part, axis=0, keepdims=True), (8, N))
            high = whole.astype(jnp.bfloat16).astype(jnp.float32)
            pieces.append(jnp.where(table, jnp.where(high_rows, high, whole - high), 0.0))
        rows = jnp.concatenate(pieces, axis=0).astype(jnp.bfloat16)
        return (*centre, carry[3] + half_dot(rows, onehot, 1, 1))

    zero = jnp.zeros((8, N), jnp.float32)
    out = lax.fori_loop(
        0, SLOTS, step, (zero, zero, zero, jnp.zeros((24, N), jnp.float32)), unroll=4
    )
    scattered = out[3]
    waves = total[N : N + 8, :]
    own_rows, one_rows, two_rows, three_rows = [], [], [], []
    for d in range(3):
        both = scattered[8 * d : 8 * d + 4] + scattered[8 * d + 4 : 8 * d + 8]
        centre = jnp.sum(out[d], axis=0, keepdims=True)
        own_rows.append(both[0:1] - centre + waves[d : d + 1])
        one_rows.append(both[1:2])
        two_rows.append(both[2:3])
        three_rows.append(both[3:4])
    pad = [jnp.zeros((5, N), jnp.float32)]
    own_grad[...] = jnp.concatenate(own_rows + pad, axis=0)
    depth_of = [depth_after(step_x, step_y) for step_x, step_y in TABLE_DIRS]
    line = lane((8, N))
    ones = jnp.concatenate(one_rows + pad, axis=0)
    twos = jnp.concatenate(two_rows + pad, axis=0)
    threes = jnp.concatenate(three_rows + pad, axis=0)
    home_one = segments(line, depth_of[0:3])
    home_two = segments(line, depth_of[3:6])
    home_three = jnp.where(line < 64, depth_of[6], depth_of[7])
    for other in range(8):
        payload[other, 0:16, :] = up_piece
        payload[other, 16:40, :] = rest
        payload[other, 40:48, :] = pack_six(
            jnp.where(home_one == other, ones, 0.0), jnp.where(home_two == other, twos, 0.0)
        )
        payload[other, 48:56, :] = jnp.where(home_three == other, threes, 0.0)


TABLE_DIRS = ((1, 0), (1, 1), (1, -1), (-1, 0), (-1, 1), (-1, -1), (0, 1), (0, -1))


def segments(line, values):
    return jnp.where(line < 64, values[0], jnp.where(line < 96, values[1], values[2]))


def pack_six(one, two):
    return jnp.where(row_of((8, N)) < 4, one, pltpu.roll(two, 4, 0))


def depth_after(step_x, step_y):
    core, high = lax.axis_index("c"), lax.axis_index("zh")
    low, column = lax.axis_index("zl"), lax.axis_index("x")
    if step_x == 1:
        high = jnp.where(core == 1, (high + 1) % 4, high)
    if step_x == -1:
        high = jnp.where(core == 0, (high + 3) % 4, high)
    if step_y == 1:
        low = jnp.where(column == 3, 1 - low, low)
    if step_y == -1:
        low = jnp.where(column == 0, 1 - low, low)
    return high * 2 + low


def plane_after(step_x, step_y):
    core, high = lax.axis_index("c"), lax.axis_index("zh")
    row, column = lax.axis_index("y"), lax.axis_index("x")
    if step_x == 1:
        row = jnp.where((core == 1) & (high == 0), (row + 1) % 4, row)
    if step_x == -1:
        row = jnp.where((core == 0) & (high == 3), (row + 3) % 4, row)
    return row * 4 + (column + step_y + 4) % 4


def depth_sum_kernel(tiles, charge_piece, out):
    total = jnp.sum(tiles[...], axis=0)
    place_of = [plane_after(step_x, step_y) for step_x, step_y in TABLE_DIRS]
    line = lane((8, N))
    home = jnp.where(
        row_of((8, N)) < 4, segments(line, place_of[0:3]), segments(line, place_of[3:6])
    )
    home_three = jnp.where(line < 64, place_of[6], place_of[7])
    sixes, threes = total[40:48], total[48:56]
    row = lax.axis_index("y")
    quarter = charge_piece[0:4, :]
    for number in range(1, 4):
        quarter = jnp.where(row == number, charge_piece[4 * number : 4 * number + 4, :], quarter)
    for other in range(16):
        out[other, 0:40, :] = total[0:40]
        out[other, 40:48, :] = jnp.where(home == other, sixes, 0.0)
        out[other, 48:56, :] = jnp.where(home_three == other, threes, 0.0)
        out[other, 52:56, :] = quarter


def plane_sum_kernel(tiles, swap, threes):
    for column in range(4):
        total = tiles[column, 0:16, :]
        for row in range(1, 4):
            total = total + tiles[4 * row + column, 0:16, :]
        swap[16 * column : 16 * column + 16, :] = total
        for row in range(4):
            at = 96 + 16 * column + 4 * row
            swap[at : at + 4, :] = tiles[4 * row + column, 52:56, :]
    rest = tiles[0, 16:56, :]
    for other in range(1, 16):
        rest = rest + tiles[other, 16:56, :]
    swap[64:96, :] = rest[0:32]
    threes[...] = jnp.where(row_of((8, N)) < 4, rest[32:40], 0.0)


def finish_kernel(own, other, threes, own_grad, home, forces, grad_embed, grad_radial, grad_up,
                  grad_charge, grad_read):
    mean = 1.0 / ATOMS
    core = lax.axis_index("c")
    mine = pl.ds(pl.multiple_of(core * 64, 64), 64)
    theirs = pl.ds(pl.multiple_of((1 - core) * 64, 64), 64)
    grad_up[mine, :] = own[0:64, :] * mean
    grad_up[theirs, :] = other[0:64, :] * mean
    grad_charge[mine, :] = own[96:160, :] * mean
    grad_charge[theirs, :] = other[96:160, :] * mean
    total = (own[64:88, :] + other[64:88, :]) * mean
    grad_radial[0, :, :] = total[0:8]
    grad_radial[1, :, :] = total[8:16]
    grad_embed[...] = total[16:22]
    grad_read[...] = total[22:23]
    sixes = other[88:96, :]
    grad = own_grad[...]
    lane_rows = row_of((N, N))
    for number, piece in enumerate((sixes, pltpu.roll(sixes, 4, 0), threes[...])):
        onehot = jnp.where(lane_rows == home[number : number + 1, :], 1.0, 0.0)
        grad = grad + dot(piece, onehot, 1, 1)
    forces[...] = -grad[0:3, :]


def spread_kernel(*refs):
    out = refs[-1]
    core, column = lax.axis_index("c"), lax.axis_index("x")
    for number, shard in enumerate(refs[:-1]):
        source = (column + 4 - number % 4) % 4
        member = jnp.where(number < 4, core, 1 - core) * 4 + source
        out[pl.ds(pl.multiple_of(member * SHARD, SHARD), SHARD), :] = shard[...]


def structure_kernel(mine, other, kvec, embed, w_up, factor, wave_high, wave_low,
                     feature_high, feature_low):
    me = lax.axis_index(GROUP)
    at = pl.multiple_of(me * SHARD, SHARD)
    rows = jnp.concatenate(
        [kvec[:, pl.ds(at, SHARD)], jnp.zeros((5, SHARD), jnp.float32)], axis=0
    )
    turns = jnp.transpose(rows * (1.0 / (2.0 * math.pi)))
    table = jnp.concatenate([embed[...], jnp.zeros((2, N), jnp.float32)], axis=0)
    up = split(w_up[...])
    for member in range(MEMBERS):
        part = slice(member * N, (member + 1) * N)
        tile = (mine, other)[member // 4].at[member % 4]
        tail = tile[N : N + 8, :]
        onehot = (row_of((8, N)).astype(jnp.float32) == tail[3:4, :]).astype(jnp.float32)
        feature = dot(onehot, table, 0, 0) + dot_three(split(tile[0:N, :]), up)
        high, low = split(feature)
        feature_high[part, :] = high
        feature_low[part, :] = low
        for chunk in range(SHARD // 64):
            waves = slice(chunk * 64, chunk * 64 + 64)
            angle = (
                turns[waves, 0:1] * tail[0:1, :]
                + turns[waves, 1:2] * tail[1:2, :]
                + turns[waves, 2:3] * tail[2:3, :]
            )
            angle = angle - jnp.round(angle)
            square = angle * angle
            cosine = jnp.full(square.shape, COS_POLY[-1], jnp.float32)
            for value in COS_POLY[-2::-1]:
                cosine = cosine * square + value
            sine = jnp.full(square.shape, SIN_POLY[-1], jnp.float32)
            for value in SIN_POLY[-2::-1]:
                sine = sine * square + value
            sine = sine * angle
            high, low = split(cosine)
            wave_high[waves, part] = high
            wave_low[waves, part] = low
            high, low = split(sine)
            waves = slice(SHARD + chunk * 64, SHARD + chunk * 64 + 64)
            wave_high[waves, part] = high
            wave_low[waves, part] = low
    project(wave_high, wave_low, feature_high[...], feature_low[...], factor)


def whole(mine, other):
    return jnp.concatenate([mine[...].reshape(4 * N, N), other[...].reshape(4 * N, N)], axis=0)


def project(wave_high, wave_low, high, low, out):
    both = jnp.concatenate([high, low], axis=1)
    wide = half_dot(wave_high[...], both)
    total = wide[:, 0:N] + wide[:, N:] + half_dot(wave_low[...], high)
    out[...] = total.reshape(CROSSES, 16, N)


def projection_kernel(mine, other, wave_high, wave_low, out):
    high, low = split(whole(mine, other))
    project(wave_high, wave_low, high, low, out)


def sum_kernel(tiles, out):
    total = jnp.sum(tiles[...], axis=0)
    for other in range(out.shape[0]):
        out[other, :, :] = total


def filter_of(kfilter):
    me = lax.axis_index(GROUP)
    return kfilter[pl.ds(pl.multiple_of(me * SHARD, SHARD), SHARD), :] * SCALE


def waves_to_atoms(field, wave_high, wave_low):
    high, low = split(jnp.transpose(field))
    wide = half_dot(jnp.concatenate([high, low], axis=0), wave_high[...])
    return wide[0:N] + wide[N:] + half_dot(high, wave_low[...])


def potential_kernel(factor, w_charge, kfilter, wave_high, wave_low,
                     mine, other, weighted, charge_factor):
    scaled = filter_of(kfilter)
    charged = dot(factor[...], w_charge[...])
    charge_factor[...] = charged
    field = charged * jnp.concatenate([scaled, scaled], axis=0)
    weighted[...] = field
    total = waves_to_atoms(field, wave_high, wave_low)
    for member in range(MEMBERS):
        (mine, other)[member // 4][member % 4] = total[:, member * N : (member + 1) * N]


def energy_kernel(tiles, active, species, embed, w_up, read,
                  shared, grad_out, energy, read_row, up_part):
    total = tiles[0]
    for member in range(1, 4):
        total = total + tiles[member]
    table = jnp.concatenate([embed[...], jnp.zeros((2, N), jnp.float32)], axis=0)
    onehot = (row_of((8, N)) == species[...]).astype(jnp.float32)
    act = active[...]
    combined = dot(onehot, table, 0, 0) + dot(act, w_up[...]) + jnp.transpose(total)
    logistic = sigmoid(combined)
    result = combined * logistic
    weights = read[...]
    energy[...] = dot(jnp.broadcast_to(weights, (8, N)), result, 1, 1)[0:1, :]
    read_row[...] = jnp.sum(result, axis=0, keepdims=True)
    grad = weights * (logistic * (1.0 + combined * (1.0 - logistic)))
    grad_out[...] = grad
    up_part[...] = dot(act, grad, 0, 0)
    for member in range(4):
        shared[member, :, :] = grad


def wave_trig(wave_high, wave_low):
    cosine = wave_high[0:SHARD, :].astype(jnp.float32) + wave_low[0:SHARD, :].astype(jnp.float32)
    sine = wave_high[SHARD:, :].astype(jnp.float32) + wave_low[SHARD:, :].astype(jnp.float32)
    return cosine, sine


def wave_back_kernel(projected, factor, charge_factor, weighted, kfilter, kvec, wave_high, wave_low,
                     grad_mine, grad_other, feature_high, feature_low, shared_mine, shared_other,
                     w_charge, up_part, mine, other, grad_filter, up_grad, charge_grad):
    scaled = filter_of(kfilter)
    proj = projected[...]
    mixed = charge_factor[...] * proj
    grad_filter[...] = SCALE * (mixed[0:SHARD] + mixed[SHARD:])
    field = proj * jnp.concatenate([scaled, scaled], axis=0)
    pieces = split(field)
    by_charge = waves_to_atoms(field, wave_high, wave_low)
    charge_grad[...] = dot_three(split(factor[...]), pieces, 0, 0)
    active = whole(shared_mine.at[:, 0:N, :], shared_other.at[:, 0:N, :])
    mix = dot_three(split(by_charge), split(active))
    weights = split(w_charge[...])
    up_grad[...] = dot_three(split(mix), weights, 0, 1) + up_part[...]
    by_feature = dot_three(pieces, weights, 1, 1)
    grad_high, grad_low = split(whole(grad_mine, grad_other))
    along = dot_three(
        split(jnp.concatenate([weighted[...], by_feature], axis=1)),
        (
            jnp.concatenate([grad_high, feature_high[...]], axis=1),
            jnp.concatenate([grad_low, feature_low[...]], axis=1),
        ),
        1, 1,
    )
    cosine, sine = wave_trig(wave_high, wave_low)
    phase = cosine * along[SHARD:] - sine * along[0:SHARD]
    me = lax.axis_index(GROUP)
    rows = jnp.concatenate(
        [
            kvec[:, pl.ds(pl.multiple_of(me * SHARD, SHARD), SHARD)],
            jnp.zeros((5, SHARD), jnp.float32),
        ],
        axis=0,
    )
    by_pos = dot_three(split(rows), split(phase))
    core = lax.axis_index("c")
    for member in range(MEMBERS):
        part = slice(member * N, (member + 1) * N)
        out = (mine, other)[member // 4].at[member % 4]
        place = jnp.where(core == member // 4, member % 4, 4 + member % 4) * 16
        piece = pl.ds(pl.multiple_of(place, 16), 16)
        out[0:N, :] = by_charge[:, part]
        out[N : N + 8, :] = by_pos[:, part]
        out[N + 8 : N + 24, :] = up_grad[piece, :]
        out[N + 24 : N + 40, :] = charge_grad[piece, :]


def body(
    positions, species, neighbours, face_sends, corner_sends,
    embed, radial, w_up, w_charge, kvec, kfilter, read,
):
    near, far, own_x, home, positions, species, neighbours, embed, radial, read = call(
        pack_kernel,
        (f32(8, N),) * 3
        + (
            i32(8, N), f32(3, N), i32(1, N), i32(SLOTS, N), f32(KINDS, N), f32(2, BASIS, N),
            f32(1, N),
        ),
        positions, species.reshape(1, N), face_sends, corner_sends, neighbours, embed, radial,
        read.reshape(1, N),
        scratch=(
            pltpu.VMEM((4, N // 2), jnp.int32),
            pltpu.VMEM((4, N // 4), jnp.int32),
            pltpu.SemaphoreType.DMA((8,)),
        ),
        far=True,
    )
    near_y, far_y = swapped(near, GY, 0), swapped(far, GY, 1)
    near, far = call(relay_kernel, (f32(8, N),) * 2, own_x, near_y, far_y)
    near_x, far_x = swapped(near, GX, 0), swapped(far, GX, 1)
    shared, active, invariants, vectors, sums, edges, places = call(
        edge_kernel,
        (
            f32(4, N + 8, N), f32(N, N), f32(N, N), f32(3, N, N), f32(4, KINDS * BASIS, N),
            f32(7, SLOTS, N), i32(2, SLOTS, N),
        ),
        positions, species, neighbours, near_x, far_x, near_y, far_y, embed, radial,
    )
    swap = [(0, 1), (1, 0)]

    def other_core(value):
        return lax.ppermute(value, "c", swap)

    def row_exchange(tiles):
        return lax.all_to_all(tiles, "x", 0, 0)

    shared = row_exchange(shared)
    shared_other = other_core(shared)
    half = jax.ShapeDtypeStruct((2 * SHARD, MEMBERS * N), jnp.bfloat16)
    feature = jax.ShapeDtypeStruct((MEMBERS * N, N), jnp.bfloat16)
    factor, wave_high, wave_low, feature_high, feature_low = call(
        structure_kernel,
        (f32(CROSSES, 16, N), half, half, feature, feature),
        shared, shared_other, kvec, embed, w_up,
    )

    def cross_sum(tiles):
        tiles = lax.all_to_all(tiles, CROSS, 0, 0)
        tiles = call(sum_kernel, f32(CROSSES, 16, N), tiles)
        return lax.all_to_all(tiles, CROSS, 0, 0).reshape(2 * SHARD, N)

    factor = cross_sum(factor)
    mine, other, weighted, charge_factor = call(
        potential_kernel,
        (f32(4, N, N), f32(4, N, N), f32(2 * SHARD, N), f32(2 * SHARD, N)),
        factor, w_charge, kfilter, wave_high, wave_low,
    )
    potential = row_exchange(mine + other_core(other))
    grads, grad_out, energy, read_row, up_part = call(
        energy_kernel,
        (f32(4, N, N), f32(N, N), f32(1, N), f32(1, N), f32(N, N)),
        potential, active, species, embed, w_up, read,
    )
    grads = row_exchange(grads)
    grads_other = other_core(grads)
    projected = cross_sum(
        call(projection_kernel, f32(CROSSES, 16, N), grads, grads_other, wave_high, wave_low)
    )
    square = pltpu.VMEM((N, N), jnp.float32)
    mine, other, shard = call(
        wave_back_kernel,
        (f32(4, N + 40, N), f32(4, N + 40, N), f32(SHARD, N)),
        projected, factor, charge_factor, weighted, kfilter, kvec, wave_high, wave_low,
        grads, grads_other, feature_high, feature_low, shared, shared_other, w_charge, up_part,
        scratch=(square, square),
    )
    tiles = row_exchange(mine + other_core(other))
    shards = [shard] + [
        lax.ppermute(shard, "x", [(at, (at + step) % 4) for at in range(4)]) for step in (1, 2, 3)
    ]
    payload, own_grad, charge_piece = call(
        edge_back_kernel,
        (f32(8, 56, N), f32(8, N), f32(16, N)),
        tiles, active, invariants, vectors, sums, edges, places, embed, radial, w_up,
        w_charge, species, grad_out, read_row,
        cost=pl.CostEstimate(flops=10**9, bytes_accessed=10**7, transcendentals=10**5),
    )
    payload, *shards = lax.optimization_barrier((payload, *shards))
    payload = lax.all_to_all(payload, DEPTH, 0, 0)
    payload = call(depth_sum_kernel, f32(16, 56, N), payload, charge_piece)
    payload = lax.all_to_all(payload, PLANE, 0, 0)
    payload, threes = call(plane_sum_kernel, (f32(160, N), f32(8, N)), payload)
    shards += [other_core(value) for value in shards]
    payload_other = other_core(payload)
    grad_filter = call(spread_kernel, f32(WAVES, N), *shards)
    forces, grad_embed, grad_radial, grad_up, grad_charge, grad_read = call(
        finish_kernel,
        (f32(3, N), f32(KINDS, N), f32(2, BASIS, N), f32(N, N), f32(N, N), f32(1, N)),
        payload, payload_other, threes, own_grad, home,
    )
    return (
        energy.reshape(N), forces, grad_embed, grad_radial, grad_up, grad_charge, grad_filter,
        grad_read.reshape(N),
    )


def solution(mesh):
    fine = Mesh(mesh.devices.reshape(4, 4, 2, 2, 4), ALL)
    atoms = P(ALL)
    rows = P(None, ALL)
    return jax.shard_map(
        body,
        mesh=fine,
        in_specs=(rows, atoms, rows, rows, rows) + (P(),) * 7,
        out_specs=(atoms, rows) + (P(),) * 6,
        check_vma=False,
    )
```

```python
import functools
import math

import jax
import jax.numpy as jnp
from jax import lax
from jax.experimental import pallas as pl
from jax.experimental.pallas import tpu as pltpu
from jax.sharding import Mesh
from jax.sharding import PartitionSpec as P

CUTOFF = 5.0
SOFTEN = 0.01
WIDTH_GAUSS = 2.0
DOMAIN = 8.8
N = 128
SLOTS = 64
KINDS = 6
BASIS = 8
WAVES = 2048
ATOMS = 32768
SHARD = 256
HIGHEST = lax.Precision.HIGHEST
SCALE = 1.0 / math.sqrt(ATOMS * WAVES)

GX = ("y", "zh", "c")
GY = ("zl", "x")
ALL = GX + GY
GROUP = ("c", "x")
CROSS = ("y", "zh", "zl")
MEMBERS = 8
CROSSES = 32
DEPTH = ("zh", "zl")
PLANE = ("y", "x")

COS_POLY = None
SIN_POLY = None


def _fit():
    import numpy as np

    points = (1.0 + np.cos(np.pi * (np.arange(200) + 0.5) / 200)) / 8.0
    root = np.sqrt(points)
    found = []
    for count, value in ((7, np.cos(2 * np.pi * root)), (6, np.sin(2 * np.pi * root) / root)):
        matrix = np.vander(points * 4.0, count, increasing=True)
        terms = np.linalg.lstsq(matrix, value, rcond=None)[0] * 4.0 ** np.arange(count)
        found.append([float(term) for term in terms])
    return found


COS_POLY, SIN_POLY = _fit()


def dims(left, right):
    return (((left,), (right,)), ((), ()))


def dot(left, right, left_dim=1, right_dim=0, precision=HIGHEST):
    return lax.dot_general(
        left,
        right,
        dims(left_dim, right_dim),
        precision=precision,
        preferred_element_type=jnp.float32,
    )


def half_dot(left, right, left_dim=1, right_dim=0):
    return lax.dot_general(
        left, right, dims(left_dim, right_dim), preferred_element_type=jnp.float32
    )


def split(value):
    high = value.astype(jnp.bfloat16)
    return high, (value - high.astype(jnp.float32)).astype(jnp.bfloat16)


def dot_three(left, right, left_dim=1, right_dim=0):
    left_high, left_low = left
    right_high, right_low = right
    return (
        half_dot(left_high, right_high, left_dim, right_dim)
        + half_dot(left_high, right_low, left_dim, right_dim)
        + half_dot(left_low, right_high, left_dim, right_dim)
    )


def sigmoid(value):
    return 1.0 / (1.0 + jnp.exp(-value))


def lane(shape):
    return lax.broadcasted_iota(jnp.int32, shape, 1)


def row_of(shape):
    return lax.broadcasted_iota(jnp.int32, shape, 0)


def call(kernel, out_shape, *args, scratch=(), vmem=32, far=False, cost=None):
    more = {}
    if far:
        more["in_specs"] = [pl.BlockSpec(memory_space=pltpu.HBM)] * len(args)
        args = [pltpu.with_memory_space_constraint(value, pltpu.HBM) for value in args]
    return pl.pallas_call(
        kernel,
        out_shape=out_shape,
        scratch_shapes=list(scratch),
        cost_estimate=cost,
        **more,
        compiler_params=pltpu.CompilerParams(vmem_limit_bytes=vmem * 1024 * 1024),
    )(*args)


def f32(*shape):
    return jax.ShapeDtypeStruct(shape, jnp.float32)


def i32(*shape):
    return jax.ShapeDtypeStruct(shape, jnp.int32)


def take(row, index):
    return jnp.take_along_axis(
        jnp.broadcast_to(row, index.shape), index, axis=1, mode="promise_in_bounds"
    )


def joined(face, corner, faces, corners):
    return jnp.concatenate(
        [face[f : f + 1, :] for f in faces] + [corner[f : f + 1, :] for f in corners], axis=1
    )


def pack_kernel(pos_in, species_in, face_in, corner_in, nbr_in, embed_in, radial_in, read_in,
                near, far, own, home, pos, species, nbr, embed, radial, read, face, corner, sems):
    pairs = (
        (pos_in, pos), (species_in, species), (face_in, face), (corner_in, corner),
        (nbr_in, nbr), (embed_in, embed), (radial_in, radial), (read_in, read),
    )
    copies = [
        pltpu.make_async_copy(source, target, sems.at[number])
        for number, (source, target) in enumerate(pairs)
    ]
    for copy in copies:
        copy.start()
    for copy in copies:
        copy.wait()
    even = lax.axis_index("x") % 2 == 0
    rows = [pos[0:1, :], pos[1:2, :], pos[2:3, :], species[...].astype(jnp.float32)]
    padding = jnp.zeros((5, N), jnp.int32)
    where_from = jnp.concatenate(
        [
            joined(face, corner, (2,), (0, 2)),
            joined(face, corner, (3,), (1, 3)),
            joined(face, corner, (0, 1), ()),
            padding,
        ],
        axis=0,
    )
    home[...] = jnp.concatenate(
        [
            joined(face, corner, (0,), (0, 1)),
            joined(face, corner, (1,), (2, 3)),
            joined(face, corner, (2, 3), ()),
            padding,
        ],
        axis=0,
    )
    for number, row in enumerate(rows):
        got = take(row, where_from)
        near[number : number + 1, :] = jnp.where(even, got[1:2, :], got[0:1, :])
        far[number : number + 1, :] = jnp.where(even, got[0:1, :], got[1:2, :])
        own[number : number + 1, :] = got[2:3, :]
    zero = jnp.zeros((4, N), jnp.float32)
    near[4:8, :] = zero
    far[4:8, :] = zero
    own[4:8, :] = zero


def swapped(value, axes, odd):
    count = math.prod(lax.axis_size(axis) for axis in axes)
    places = [(at, ((((at + odd) % count) ^ 1) - odd) % count) for at in range(count)]
    return lax.ppermute(value, axes, places)


def relay_kernel(own, near, far, one, two):
    at = lane((8, N))
    even = lax.axis_index("x") % 2 == 0
    a = own[...]
    b = jnp.where(even, near[...], far[...])
    d = jnp.where(even, far[...], near[...])
    to_minus = jnp.where(at < 64, a, jnp.where(at < 96, b, pltpu.roll(d, 32, 1)))
    to_plus = jnp.where(
        at < 64, pltpu.roll(a, 64, 1), jnp.where(at < 96, pltpu.roll(b, 96, 1), d)
    )
    first = lax.axis_index("c") == 0
    one[...] = jnp.where(first, to_plus, to_minus)
    two[...] = jnp.where(first, to_minus, to_plus)


def pair_weights(embed, radial):
    scalar, vector = [], []
    for kind in range(KINDS):
        row = embed[kind : kind + 1, :]
        scalar.append(radial[0] * row * 0.25)
        vector.append(radial[1] * row * 0.05)
    return jnp.concatenate(scalar, axis=0), jnp.concatenate(vector, axis=0)


def basis_centers():
    return row_of((BASIS, N)).astype(jnp.float32) * (CUTOFF / (BASIS - 1))


def edge_kernel(
    pos, species, nbr, near_x, far_x, near_y, far_y, embed, radial,
    shared, active, invariants, vectors, sums, edges, places,
):
    at = lane((8, N))
    own = [pos[0:1, :], pos[1:2, :], pos[2:3, :], species[...].astype(jnp.float32)]
    core_zero = lax.axis_index("c") == 0
    even = lax.axis_index("x") % 2 == 0
    first = jnp.where(core_zero, near_x[...], far_x[...])
    second = jnp.where(core_zero, far_x[...], near_x[...])
    plus_y = jnp.where(even, near_y[...], far_y[...])
    minus_y = jnp.where(even, far_y[...], near_y[...])
    third = jnp.where(at < 64, plus_y, pltpu.roll(minus_y, 64, 1))
    line = lane((1, N))
    corner_y = jnp.where(line < 64, 0.0, jnp.where(line < 96, DOMAIN, -DOMAIN))
    tables = [
        own,
        [first[0:1] + DOMAIN, first[1:2] + corner_y, first[2:3], first[3:4]],
        [second[0:1] - DOMAIN, second[1:2] + corner_y, second[2:3], second[3:4]],
        [third[0:1], third[1:2] + jnp.where(line < 64, DOMAIN, -DOMAIN), third[2:3], third[3:4]],
    ]
    for group in range(SLOTS // 8):
        rows = slice(8 * group, 8 * group + 8)
        slot = nbr[rows, :]
        block = lax.shift_right_logical(slot, 6)
        table = jnp.where(
            block < 2,
            0,
            jnp.where(
                (block == 4) | (block == 5), 3, jnp.where((block & 1) == 0, 1, 2)
            ),
        )
        table = jnp.where(block == 8, 4, table)
        half = jnp.where((block == 1) | ((block >= 5) & (block < 8)), 64, 0)
        place = (slot & 63) + half
        found = []
        for number in range(4):
            value = take(tables[0][number], place)
            for other in range(1, 4):
                value = jnp.where(table == other, take(tables[other][number], place), value)
            found.append(value)
        offset = [found[d] - own[d] for d in range(3)]
        dist_sq = offset[0] * offset[0] + offset[1] * offset[1] + offset[2] * offset[2]
        valid = (table < 4).astype(jnp.float32)
        ramp = jnp.maximum(1.0 - dist_sq / (CUTOFF * CUTOFF), 0.0)
        edges[0, rows, :] = offset[0]
        edges[1, rows, :] = offset[1]
        edges[2, rows, :] = offset[2]
        edges[3, rows, :] = found[3]
        edges[4, rows, :] = jnp.sqrt(dist_sq + SOFTEN)
        edges[5, rows, :] = ramp * ramp * valid
        edges[6, rows, :] = (-2.0 / (CUTOFF * CUTOFF)) * ramp * valid
        places[0, rows, :] = table
        places[1, rows, :] = place
    centers = basis_centers()

    def step(slot, carry):
        row = pl.ds(slot, 1)
        away = edges[4, row, :] - centers
        basis = jnp.exp(-WIDTH_GAUSS * away * away) * edges[5, row, :]
        parts = [basis] + [basis * edges[d, row, :] for d in range(3)]
        kind_row = jnp.broadcast_to(edges[3, row, :], (BASIS, N))
        out = []
        for kind in range(KINDS):
            mask = kind_row == float(kind)
            for number in range(4):
                out.append(carry[4 * kind + number] + jnp.where(mask, parts[number], 0.0))
        return tuple(out)

    zero = jnp.zeros((BASIS, N), jnp.float32)
    total = lax.fori_loop(0, SLOTS, step, (zero,) * (4 * KINDS), unroll=4)
    for number in range(4):
        sums[number, :, :] = jnp.concatenate(
            [total[4 * kind + number] for kind in range(KINDS)], axis=0
        )
    scalar_w, vector_w = pair_weights(embed, radial)
    value = dot(sums[0], scalar_w, 0, 0)
    for d in range(3):
        vector = dot(sums[1 + d], vector_w, 0, 0)
        vectors[d, :, :] = vector
        value = value + vector * vector
    invariants[...] = value
    result = value * sigmoid(value)
    active[...] = result
    anchor_x = lax.convert_element_type(lax.axis_index(GX), jnp.float32) * DOMAIN
    anchor_y = lax.convert_element_type(lax.axis_index(GY), jnp.float32) * DOMAIN
    zero_row = jnp.zeros((1, N), jnp.float32)
    tail = jnp.concatenate(
        [own[0] + anchor_x, own[1] + anchor_y, own[2], own[3]] + [zero_row] * 4, axis=0
    )
    shared[0:N, :] = result
    shared[N : N + 8, :] = tail


def edge_back_kernel(
    tile_0, tile_1, tile_2, tile_3, active, invariants, vectors, sums, edges, places, embed, radial, w_up, w_charge,
    species, grad_out, read_row,
    payload, own_grad, charge_piece,
):
    total = tile_0[...] + tile_1[...] + tile_2[...] + tile_3[...]
    grad_charges = jnp.transpose(total[0:N, :])
    updated = grad_out[...] + dot(grad_charges, w_charge[...], 1, 1)
    value = invariants[...]
    logistic = sigmoid(value)
    slope = logistic * (1.0 + value * (1.0 - logistic))
    grad_inv = dot(updated, w_up[...], 1, 1) * slope
    scalar_w, vector_w = pair_weights(embed, radial)
    pulls = [dot(scalar_w, grad_inv, 1, 1)]
    grad_scalar = dot(sums[0], grad_inv)
    grad_vector = jnp.zeros((KINDS * BASIS, N), jnp.float32)
    for d in range(3):
        along = 2.0 * vectors[d] * grad_inv
        pulls.append(dot(vector_w, along, 1, 1))
        grad_vector = grad_vector + dot(sums[1 + d], along)
    onehot = (row_of((8, N)) == species[...]).astype(jnp.float32)
    grad_table = dot(onehot, updated)
    radial_zero = jnp.zeros((BASIS, N), jnp.float32)
    radial_one = jnp.zeros((BASIS, N), jnp.float32)
    table_rows = []
    for kind in range(KINDS):
        rows = slice(kind * BASIS, (kind + 1) * BASIS)
        row = embed[kind : kind + 1, :]
        part_zero, part_one = grad_scalar[rows] * 0.25, grad_vector[rows] * 0.05
        radial_zero = radial_zero + part_zero * row
        radial_one = radial_one + part_one * row
        table_rows.append(
            grad_table[kind : kind + 1]
            + jnp.sum(radial[0] * part_zero + radial[1] * part_one, axis=0, keepdims=True)
        )
    rest = jnp.concatenate(
        [radial_zero, radial_one] + table_rows + [read_row[...], jnp.zeros((1, N), jnp.float32)],
        axis=0,
    )
    up_piece = total[N + 8 : N + 24, :]
    charge_piece[...] = total[N + 24 : N + 40, :]
    centers = basis_centers()
    sub = row_of((8, N))
    sub_table = sub & 3
    high_rows = sub < 4
    lane_rows = row_of((N, N))
    pull = [
        [pulls[number][kind * BASIS : (kind + 1) * BASIS] for number in range(4)]
        for kind in range(KINDS)
    ]

    def step(slot, carry):
        row = pl.ds(slot, 1)
        kind_row = jnp.broadcast_to(edges[3, row, :], (BASIS, N))
        own_pull = list(pull[KINDS - 1])
        for kind in range(KINDS - 1):
            mask = kind_row == float(kind)
            own_pull = [jnp.where(mask, pull[kind][n], own_pull[n]) for n in range(4)]
        radius = edges[4, row, :]
        envelope = edges[5, row, :]
        away = radius - centers
        bell = jnp.exp(-WIDTH_GAUSS * away * away)
        offset = [jnp.broadcast_to(edges[d, row, :], (BASIS, N)) for d in range(3)]
        by_basis = own_pull[0]
        for d in range(3):
            by_basis = by_basis + offset[d] * own_pull[1 + d]
        by_square = by_basis * bell * (edges[6, row, :] - (2.0 * envelope / radius) * away)
        basis = bell * envelope
        table = jnp.broadcast_to(places[0, row, :], (8, N)) == sub_table
        place = lane_rows == places[1, row, :]
        onehot = jnp.where(place, 1.0, 0.0).astype(jnp.bfloat16)
        centre, pieces = [], []
        for d in range(3):
            part = basis * own_pull[1 + d] + 2.0 * offset[d] * by_square
            centre.append(carry[d] + part)
            whole = jnp.broadcast_to(jnp.sum(part, axis=0, keepdims=True), (8, N))
            high = whole.astype(jnp.bfloat16).astype(jnp.float32)
            pieces.append(jnp.where(table, jnp.where(high_rows, high, whole - high), 0.0))
        rows = jnp.concatenate(pieces, axis=0).astype(jnp.bfloat16)
        return (*centre, carry[3] + half_dot(rows, onehot, 1, 1))

    zero = jnp.zeros((8, N), jnp.float32)
    out = lax.fori_loop(
        0, SLOTS, step, (zero, zero, zero, jnp.zeros((24, N), jnp.float32)), unroll=4
    )
    scattered = out[3]
    waves = total[N : N + 8, :]
    own_rows, one_rows, two_rows, three_rows = [], [], [], []
    for d in range(3):
        both = scattered[8 * d : 8 * d + 4] + scattered[8 * d + 4 : 8 * d + 8]
        centre = jnp.sum(out[d], axis=0, keepdims=True)
        own_rows.append(both[0:1] - centre + waves[d : d + 1])
        one_rows.append(both[1:2])
        two_rows.append(both[2:3])
        three_rows.append(both[3:4])
    pad = [jnp.zeros((5, N), jnp.float32)]
    own_grad[...] = jnp.concatenate(own_rows + pad, axis=0)
    depth_of = [depth_after(step_x, step_y) for step_x, step_y in TABLE_DIRS]
    line = lane((8, N))
    ones = jnp.concatenate(one_rows + pad, axis=0)
    twos = jnp.concatenate(two_rows + pad, axis=0)
    threes = jnp.concatenate(three_rows + pad, axis=0)
    home_one = segments(line, depth_of[0:3])
    home_two = segments(line, depth_of[3:6])
    home_three = jnp.where(line < 64, depth_of[6], depth_of[7])
    for other in range(8):
        payload[other, 0:16, :] = up_piece
        payload[other, 16:40, :] = rest
        payload[other, 40:48, :] = pack_six(
            jnp.where(home_one == other, ones, 0.0), jnp.where(home_two == other, twos, 0.0)
        )
        payload[other, 48:56, :] = jnp.where(home_three == other, threes, 0.0)


TABLE_DIRS = ((1, 0), (1, 1), (1, -1), (-1, 0), (-1, 1), (-1, -1), (0, 1), (0, -1))


def segments(line, values):
    return jnp.where(line < 64, values[0], jnp.where(line < 96, values[1], values[2]))


def pack_six(one, two):
    return jnp.where(row_of((8, N)) < 4, one, pltpu.roll(two, 4, 0))


def depth_after(step_x, step_y):
    core, high = lax.axis_index("c"), lax.axis_index("zh")
    low, column = lax.axis_index("zl"), lax.axis_index("x")
    if step_x == 1:
        high = jnp.where(core == 1, (high + 1) % 4, high)
    if step_x == -1:
        high = jnp.where(core == 0, (high + 3) % 4, high)
    if step_y == 1:
        low = jnp.where(column == 3, 1 - low, low)
    if step_y == -1:
        low = jnp.where(column == 0, 1 - low, low)
    return high * 2 + low


def plane_after(step_x, step_y):
    core, high = lax.axis_index("c"), lax.axis_index("zh")
    row, column = lax.axis_index("y"), lax.axis_index("x")
    if step_x == 1:
        row = jnp.where((core == 1) & (high == 0), (row + 1) % 4, row)
    if step_x == -1:
        row = jnp.where((core == 0) & (high == 3), (row + 3) % 4, row)
    return row * 4 + (column + step_y + 4) % 4


def depth_sum_kernel(tiles, charge_piece, out):
    total = jnp.sum(tiles[...], axis=0)
    place_of = [plane_after(step_x, step_y) for step_x, step_y in TABLE_DIRS]
    line = lane((8, N))
    home = jnp.where(
        row_of((8, N)) < 4, segments(line, place_of[0:3]), segments(line, place_of[3:6])
    )
    home_three = jnp.where(line < 64, place_of[6], place_of[7])
    sixes, threes = total[40:48], total[48:56]
    row = lax.axis_index("y")
    quarter = charge_piece[0:4, :]
    for number in range(1, 4):
        quarter = jnp.where(row == number, charge_piece[4 * number : 4 * number + 4, :], quarter)
    for other in range(16):
        out[other, 0:40, :] = total[0:40]
        out[other, 40:48, :] = jnp.where(home == other, sixes, 0.0)
        out[other, 48:56, :] = jnp.where(home_three == other, threes, 0.0)
        out[other, 52:56, :] = quarter


def plane_sum_kernel(tiles, swap, threes):
    for column in range(4):
        total = tiles[column, 0:16, :]
        for row in range(1, 4):
            total = total + tiles[4 * row + column, 0:16, :]
        swap[16 * column : 16 * column + 16, :] = total
        for row in range(4):
            at = 96 + 16 * column + 4 * row
            swap[at : at + 4, :] = tiles[4 * row + column, 52:56, :]
    rest = tiles[0, 16:56, :]
    for other in range(1, 16):
        rest = rest + tiles[other, 16:56, :]
    swap[64:96, :] = rest[0:32]
    threes[...] = jnp.where(row_of((8, N)) < 4, rest[32:40], 0.0)


def finish_kernel(own, other, threes, own_grad, home, forces, grad_embed, grad_radial, grad_up,
                  grad_charge, grad_read):
    mean = 1.0 / ATOMS
    core = lax.axis_index("c")
    mine = pl.ds(pl.multiple_of(core * 64, 64), 64)
    theirs = pl.ds(pl.multiple_of((1 - core) * 64, 64), 64)
    grad_up[mine, :] = own[0:64, :] * mean
    grad_up[theirs, :] = other[0:64, :] * mean
    grad_charge[mine, :] = own[96:160, :] * mean
    grad_charge[theirs, :] = other[96:160, :] * mean
    total = (own[64:88, :] + other[64:88, :]) * mean
    grad_radial[0, :, :] = total[0:8]
    grad_radial[1, :, :] = total[8:16]
    grad_embed[...] = total[16:22]
    grad_read[...] = total[22:23]
    sixes = other[88:96, :]
    grad = own_grad[...]
    lane_rows = row_of((N, N))
    for number, piece in enumerate((sixes, pltpu.roll(sixes, 4, 0), threes[...])):
        onehot = jnp.where(lane_rows == home[number : number + 1, :], 1.0, 0.0)
        grad = grad + dot(piece, onehot, 1, 1)
    forces[...] = -grad[0:3, :]


def spread_kernel(*refs):
    out = refs[-1]
    core, column = lax.axis_index("c"), lax.axis_index("x")
    for number, shard in enumerate(refs[:-1]):
        source = (column + 4 - number % 4) % 4
        member = jnp.where(number < 4, core, 1 - core) * 4 + source
        out[pl.ds(pl.multiple_of(member * SHARD, SHARD), SHARD), :] = shard[...]


def structure_kernel(*refs):
    tiles = refs[:MEMBERS]
    kvec, embed, w_up, factor, wave_high, wave_low, feature_high, feature_low = refs[MEMBERS:]
    me = lax.axis_index(GROUP)
    at = pl.multiple_of(me * SHARD, SHARD)
    rows = jnp.concatenate(
        [kvec[:, pl.ds(at, SHARD)], jnp.zeros((5, SHARD), jnp.float32)], axis=0
    )
    turns = jnp.transpose(rows * (1.0 / (2.0 * math.pi)))
    table = jnp.concatenate([embed[...], jnp.zeros((2, N), jnp.float32)], axis=0)
    up = split(w_up[...])
    for member in range(MEMBERS):
        part = slice(member * N, (member + 1) * N)
        tile = tiles[member]
        tail = tile[N : N + 8, :]
        onehot = (row_of((8, N)).astype(jnp.float32) == tail[3:4, :]).astype(jnp.float32)
        feature = dot(onehot, table, 0, 0) + dot_three(split(tile[0:N, :]), up)
        high, low = split(feature)
        feature_high[part, :] = high
        feature_low[part, :] = low
        for chunk in range(SHARD // 64):
            waves = slice(chunk * 64, chunk * 64 + 64)
            angle = (
                turns[waves, 0:1] * tail[0:1, :]
                + turns[waves, 1:2] * tail[1:2, :]
                + turns[waves, 2:3] * tail[2:3, :]
            )
            angle = angle - jnp.round(angle)
            square = angle * angle
            cosine = jnp.full(square.shape, COS_POLY[-1], jnp.float32)
            for value in COS_POLY[-2::-1]:
                cosine = cosine * square + value
            sine = jnp.full(square.shape, SIN_POLY[-1], jnp.float32)
            for value in SIN_POLY[-2::-1]:
                sine = sine * square + value
            sine = sine * angle
            high, low = split(cosine)
            wave_high[waves, part] = high
            wave_low[waves, part] = low
            high, low = split(sine)
            waves = slice(SHARD + chunk * 64, SHARD + chunk * 64 + 64)
            wave_high[waves, part] = high
            wave_low[waves, part] = low
    project(wave_high, wave_low, feature_high[...], feature_low[...], factor)


def whole(tiles):
    return jnp.concatenate([tile[0:N, :] for tile in tiles], axis=0)


def project(wave_high, wave_low, high, low, out):
    both = jnp.concatenate([high, low], axis=1)
    wide = half_dot(wave_high[...], both)
    total = wide[:, 0:N] + wide[:, N:] + half_dot(wave_low[...], high)
    out[...] = total.reshape(CROSSES, 16, N)


def projection_kernel(*refs):
    wave_high, wave_low, out = refs[MEMBERS:]
    high, low = split(whole(refs[:MEMBERS]))
    project(wave_high, wave_low, high, low, out)


def sum_kernel(tiles, out):
    total = jnp.sum(tiles[...], axis=0)
    for other in range(out.shape[0]):
        out[other, :, :] = total


def filter_of(kfilter):
    me = lax.axis_index(GROUP)
    return kfilter[pl.ds(pl.multiple_of(me * SHARD, SHARD), SHARD), :] * SCALE


def core_sum_kernel(mine, other, *out):
    for number, ref in enumerate(out):
        ref[...] = mine[number] + other[number]


def waves_to_atoms(field, wave_high, wave_low):
    high, low = split(jnp.transpose(field))
    wide = half_dot(jnp.concatenate([high, low], axis=0), wave_high[...])
    return wide[0:N] + wide[N:] + half_dot(high, wave_low[...])


def potential_kernel(factor, w_charge, kfilter, wave_high, wave_low,
                     mine, other, weighted, charge_factor):
    scaled = filter_of(kfilter)
    charged = dot(factor[...], w_charge[...])
    charge_factor[...] = charged
    field = charged * jnp.concatenate([scaled, scaled], axis=0)
    weighted[...] = field
    total = waves_to_atoms(field, wave_high, wave_low)
    for member in range(MEMBERS):
        (mine, other)[member // 4][member % 4] = total[:, member * N : (member + 1) * N]


def energy_kernel(tile_0, tile_1, tile_2, tile_3, active, species, embed, w_up, read,
                  grad_out, energy, read_row, up_part):
    total = tile_0[...] + tile_1[...] + tile_2[...] + tile_3[...]
    table = jnp.concatenate([embed[...], jnp.zeros((2, N), jnp.float32)], axis=0)
    onehot = (row_of((8, N)) == species[...]).astype(jnp.float32)
    act = active[...]
    combined = dot(onehot, table, 0, 0) + dot(act, w_up[...]) + jnp.transpose(total)
    logistic = sigmoid(combined)
    result = combined * logistic
    weights = read[...]
    energy[...] = dot(jnp.broadcast_to(weights, (8, N)), result, 1, 1)[0:1, :]
    read_row[...] = jnp.sum(result, axis=0, keepdims=True)
    grad = weights * (logistic * (1.0 + combined * (1.0 - logistic)))
    grad_out[...] = grad
    up_part[...] = dot(act, grad, 0, 0)


def wave_trig(wave_high, wave_low):
    cosine = wave_high[0:SHARD, :].astype(jnp.float32) + wave_low[0:SHARD, :].astype(jnp.float32)
    sine = wave_high[SHARD:, :].astype(jnp.float32) + wave_low[SHARD:, :].astype(jnp.float32)
    return cosine, sine


def wave_back_kernel(*refs):
    grads, shared = refs[:MEMBERS], refs[MEMBERS : 2 * MEMBERS]
    (
        projected, factor, charge_factor, weighted, kfilter, kvec, wave_high, wave_low,
        feature_high, feature_low, w_charge, up_part,
        mine, other, grad_filter, up_grad, charge_grad,
    ) = refs[2 * MEMBERS :]
    scaled = filter_of(kfilter)
    proj = projected[...]
    mixed = charge_factor[...] * proj
    grad_filter[...] = SCALE * (mixed[0:SHARD] + mixed[SHARD:])
    field = proj * jnp.concatenate([scaled, scaled], axis=0)
    pieces = split(field)
    by_charge = waves_to_atoms(field, wave_high, wave_low)
    charge_grad[...] = dot_three(split(factor[...]), pieces, 0, 0)
    active = whole(shared)
    mix = dot_three(split(by_charge), split(active))
    weights = split(w_charge[...])
    up_grad[...] = dot_three(split(mix), weights, 0, 1) + up_part[...]
    by_feature = dot_three(pieces, weights, 1, 1)
    grad_high, grad_low = split(whole(grads))
    along = dot_three(
        split(jnp.concatenate([weighted[...], by_feature], axis=1)),
        (
            jnp.concatenate([grad_high, feature_high[...]], axis=1),
            jnp.concatenate([grad_low, feature_low[...]], axis=1),
        ),
        1, 1,
    )
    cosine, sine = wave_trig(wave_high, wave_low)
    phase = cosine * along[SHARD:] - sine * along[0:SHARD]
    me = lax.axis_index(GROUP)
    rows = jnp.concatenate(
        [
            kvec[:, pl.ds(pl.multiple_of(me * SHARD, SHARD), SHARD)],
            jnp.zeros((5, SHARD), jnp.float32),
        ],
        axis=0,
    )
    by_pos = dot_three(split(rows), split(phase))
    core, column = lax.axis_index("c"), lax.axis_index("x")
    for member in range(MEMBERS):
        part = slice(member * N, (member + 1) * N)
        out = (mine, other)[member // 4].at[member % 4]
        place = jnp.where(core == member // 4, 0, 4) + (column + 4 - member % 4) % 4
        place = place * 16
        piece = pl.ds(pl.multiple_of(place, 16), 16)
        out[0:N, :] = by_charge[:, part]
        out[N : N + 8, :] = by_pos[:, part]
        out[N + 8 : N + 24, :] = up_grad[piece, :]
        out[N + 24 : N + 40, :] = charge_grad[piece, :]


def body(
    positions, species, neighbours, face_sends, corner_sends,
    embed, radial, w_up, w_charge, kvec, kfilter, read,
):
    near, far, own_x, home, positions, species, neighbours, embed, radial, read = call(
        pack_kernel,
        (f32(8, N),) * 3
        + (
            i32(8, N), f32(3, N), i32(1, N), i32(SLOTS, N), f32(KINDS, N), f32(2, BASIS, N),
            f32(1, N),
        ),
        positions, species.reshape(1, N), face_sends, corner_sends, neighbours, embed, radial,
        read.reshape(1, N),
        scratch=(
            pltpu.VMEM((4, N // 2), jnp.int32),
            pltpu.VMEM((4, N // 4), jnp.int32),
            pltpu.SemaphoreType.DMA((8,)),
        ),
        far=True,
    )
    near_y, far_y = swapped(near, GY, 0), swapped(far, GY, 1)
    near, far = call(relay_kernel, (f32(8, N),) * 2, own_x, near_y, far_y)
    near_x, far_x = swapped(near, GX, 0), swapped(far, GX, 1)
    shared, active, invariants, vectors, sums, edges, places = call(
        edge_kernel,
        (
            f32(N + 8, N), f32(N, N), f32(N, N), f32(3, N, N), f32(4, KINDS * BASIS, N),
            f32(7, SLOTS, N), i32(2, SLOTS, N),
        ),
        positions, species, neighbours, near_x, far_x, near_y, far_y, embed, radial,
    )
    swap = [(0, 1), (1, 0)]

    def other_core(value):
        return lax.ppermute(value, "c", swap)

    def step_x(value, step):
        return lax.ppermute(value, "x", [(at, (at + step) % 4) for at in range(4)])

    def gather(value):
        values = [value] + [step_x(value, step) for step in (1, 2, 3)]
        return values + [other_core(item) for item in values]

    def scatter(mine, other):
        tiles = call(core_sum_kernel, (f32(*mine.shape[1:]),) * 4, mine, other_core(other))
        return [tiles[0]] + [step_x(tiles[step], -step) for step in (1, 2, 3)]

    shared = gather(shared)
    half = jax.ShapeDtypeStruct((2 * SHARD, MEMBERS * N), jnp.bfloat16)
    feature = jax.ShapeDtypeStruct((MEMBERS * N, N), jnp.bfloat16)
    factor, wave_high, wave_low, feature_high, feature_low = call(
        structure_kernel,
        (f32(CROSSES, 16, N), half, half, feature, feature),
        *shared, kvec, embed, w_up,
    )

    def cross_sum(tiles):
        tiles = lax.all_to_all(tiles, CROSS, 0, 0)
        tiles = call(sum_kernel, f32(CROSSES, 16, N), tiles)
        return lax.all_to_all(tiles, CROSS, 0, 0).reshape(2 * SHARD, N)

    factor = cross_sum(factor)
    mine, other, weighted, charge_factor = call(
        potential_kernel,
        (f32(4, N, N), f32(4, N, N), f32(2 * SHARD, N), f32(2 * SHARD, N)),
        factor, w_charge, kfilter, wave_high, wave_low,
    )
    grad_out, energy, read_row, up_part = call(
        energy_kernel,
        (f32(N, N), f32(1, N), f32(1, N), f32(N, N)),
        *scatter(mine, other), active, species, embed, w_up, read,
    )
    grads = gather(grad_out)
    projected = cross_sum(
        call(projection_kernel, f32(CROSSES, 16, N), *grads, wave_high, wave_low)
    )
    square = pltpu.VMEM((N, N), jnp.float32)
    mine, other, shard = call(
        wave_back_kernel,
        (f32(4, N + 40, N), f32(4, N + 40, N), f32(SHARD, N)),
        *grads, *shared, projected, factor, charge_factor, weighted, kfilter, kvec,
        wave_high, wave_low, feature_high, feature_low, w_charge, up_part,
        scratch=(square, square),
    )
    tiles = scatter(mine, other)
    shard, *tiles = lax.optimization_barrier((shard, *tiles))
    shards = [shard] + [step_x(shard, step) for step in (1, 2, 3)]
    payload, own_grad, charge_piece = call(
        edge_back_kernel,
        (f32(8, 56, N), f32(8, N), f32(16, N)),
        *tiles, active, invariants, vectors, sums, edges, places, embed, radial, w_up,
        w_charge, species, grad_out, read_row,
        cost=pl.CostEstimate(flops=10**9, bytes_accessed=10**7, transcendentals=10**5),
    )
    payload, *shards = lax.optimization_barrier((payload, *shards))
    payload = lax.all_to_all(payload, DEPTH, 0, 0)
    payload = call(depth_sum_kernel, f32(16, 56, N), payload, charge_piece)
    payload = lax.all_to_all(payload, PLANE, 0, 0)
    payload, threes = call(plane_sum_kernel, (f32(160, N), f32(8, N)), payload)
    shards += [other_core(value) for value in shards]
    payload_other = other_core(payload)
    grad_filter = call(spread_kernel, f32(WAVES, N), *shards)
    forces, grad_embed, grad_radial, grad_up, grad_charge, grad_read = call(
        finish_kernel,
        (f32(3, N), f32(KINDS, N), f32(2, BASIS, N), f32(N, N), f32(N, N), f32(1, N)),
        payload, payload_other, threes, own_grad, home,
    )
    return (
        energy.reshape(N), forces, grad_embed, grad_radial, grad_up, grad_charge, grad_filter,
        grad_read.reshape(N),
    )


def solution(mesh):
    fine = Mesh(mesh.devices.reshape(4, 4, 2, 2, 4), ALL)
    atoms = P(ALL)
    rows = P(None, ALL)
    return jax.shard_map(
        body,
        mesh=fine,
        in_specs=(rows, atoms, rows, rows, rows) + (P(),) * 7,
        out_specs=(atoms, rows) + (P(),) * 6,
        check_vma=False,
    )
```

```python
import functools
import math

import jax
import jax.numpy as jnp
from jax import lax
from jax.experimental import pallas as pl
from jax.experimental.pallas import tpu as pltpu
from jax.sharding import Mesh
from jax.sharding import PartitionSpec as P

CUTOFF = 5.0
SOFTEN = 0.01
WIDTH_GAUSS = 2.0
DOMAIN = 8.8
N = 128
SLOTS = 64
KINDS = 6
BASIS = 8
WAVES = 2048
ATOMS = 32768
SHARD = 256
HIGHEST = lax.Precision.HIGHEST
SCALE = 1.0 / math.sqrt(ATOMS * WAVES)

GX = ("y", "zh", "c")
GY = ("zl", "x")
ALL = GX + GY
GROUP = ("c", "x")
CROSS = ("y", "zh", "zl")
MEMBERS = 8
CROSSES = 32
DEPTH = ("zh", "zl")
PLANE = ("y", "x")

COS_POLY = None
SIN_POLY = None


def _fit():
    import numpy as np

    points = (1.0 + np.cos(np.pi * (np.arange(200) + 0.5) / 200)) / 8.0
    root = np.sqrt(points)
    found = []
    for count, value in ((7, np.cos(2 * np.pi * root)), (6, np.sin(2 * np.pi * root) / root)):
        matrix = np.vander(points * 4.0, count, increasing=True)
        terms = np.linalg.lstsq(matrix, value, rcond=None)[0] * 4.0 ** np.arange(count)
        found.append([float(term) for term in terms])
    return found


COS_POLY, SIN_POLY = _fit()


def dims(left, right):
    return (((left,), (right,)), ((), ()))


def exact_dot(left, right, left_dim=1, right_dim=0):
    return lax.dot_general(
        left,
        right,
        dims(left_dim, right_dim),
        precision=HIGHEST,
        preferred_element_type=jnp.float32,
    )


def half_dot(left, right, left_dim=1, right_dim=0):
    return lax.dot_general(
        left, right, dims(left_dim, right_dim), preferred_element_type=jnp.float32
    )


def split(value):
    high = value.astype(jnp.bfloat16)
    return high, (value - high.astype(jnp.float32)).astype(jnp.bfloat16)


def dot_three(left, right, left_dim=1, right_dim=0):
    left_high, left_low = left
    right_high, right_low = right
    return (
        half_dot(left_high, right_high, left_dim, right_dim)
        + half_dot(left_high, right_low, left_dim, right_dim)
        + half_dot(left_low, right_high, left_dim, right_dim)
    )


def dot(left, right, left_dim=1, right_dim=0):
    return dot_three(split(left), split(right), left_dim, right_dim)


def sigmoid(value):
    return 1.0 / (1.0 + jnp.exp(-value))


def lane(shape):
    return lax.broadcasted_iota(jnp.int32, shape, 1)


def row_of(shape):
    return lax.broadcasted_iota(jnp.int32, shape, 0)


def call(kernel, out_shape, *args, scratch=(), vmem=32, far=False, cost=None):
    more = {}
    if far:
        more["in_specs"] = [pl.BlockSpec(memory_space=pltpu.HBM)] * len(args)
        args = [pltpu.with_memory_space_constraint(value, pltpu.HBM) for value in args]
    return pl.pallas_call(
        kernel,
        out_shape=out_shape,
        scratch_shapes=list(scratch),
        cost_estimate=cost,
        **more,
        compiler_params=pltpu.CompilerParams(vmem_limit_bytes=vmem * 1024 * 1024),
    )(*args)


def f32(*shape):
    return jax.ShapeDtypeStruct(shape, jnp.float32)


def i32(*shape):
    return jax.ShapeDtypeStruct(shape, jnp.int32)


def take(row, index):
    return jnp.take_along_axis(
        jnp.broadcast_to(row, index.shape), index, axis=1, mode="promise_in_bounds"
    )


def joined(face, corner, faces, corners):
    return jnp.concatenate(
        [face[f : f + 1, :] for f in faces] + [corner[f : f + 1, :] for f in corners], axis=1
    )


def pack_kernel(pos_in, species_in, face_in, corner_in, nbr_in, embed_in, radial_in, read_in,
                near, far, own, home, pos, species, nbr, embed, radial, read, face, corner, sems):
    pairs = (
        (pos_in, pos), (species_in, species), (face_in, face), (corner_in, corner),
        (nbr_in, nbr), (embed_in, embed), (radial_in, radial), (read_in, read),
    )
    copies = [
        pltpu.make_async_copy(source, target, sems.at[number])
        for number, (source, target) in enumerate(pairs)
    ]
    for copy in copies:
        copy.start()
    for copy in copies:
        copy.wait()
    even = lax.axis_index("x") % 2 == 0
    rows = [pos[0:1, :], pos[1:2, :], pos[2:3, :], species[...].astype(jnp.float32)]
    padding = jnp.zeros((5, N), jnp.int32)
    where_from = jnp.concatenate(
        [
            joined(face, corner, (2,), (0, 2)),
            joined(face, corner, (3,), (1, 3)),
            joined(face, corner, (0, 1), ()),
            padding,
        ],
        axis=0,
    )
    home[...] = jnp.concatenate(
        [
            joined(face, corner, (0,), (0, 1)),
            joined(face, corner, (1,), (2, 3)),
            joined(face, corner, (2, 3), ()),
            padding,
        ],
        axis=0,
    )
    for number, row in enumerate(rows):
        got = take(row, where_from)
        near[number : number + 1, :] = jnp.where(even, got[1:2, :], got[0:1, :])
        far[number : number + 1, :] = jnp.where(even, got[0:1, :], got[1:2, :])
        own[number : number + 1, :] = got[2:3, :]
    zero = jnp.zeros((4, N), jnp.float32)
    near[4:8, :] = zero
    far[4:8, :] = zero
    own[4:8, :] = zero


def swapped(value, axes, odd):
    count = math.prod(lax.axis_size(axis) for axis in axes)
    places = [(at, ((((at + odd) % count) ^ 1) - odd) % count) for at in range(count)]
    return lax.ppermute(value, axes, places)


def relay_kernel(own, near, far, one, two):
    at = lane((8, N))
    even = lax.axis_index("x") % 2 == 0
    a = own[...]
    b = jnp.where(even, near[...], far[...])
    d = jnp.where(even, far[...], near[...])
    to_minus = jnp.where(at < 64, a, jnp.where(at < 96, b, pltpu.roll(d, 32, 1)))
    to_plus = jnp.where(
        at < 64, pltpu.roll(a, 64, 1), jnp.where(at < 96, pltpu.roll(b, 96, 1), d)
    )
    first = lax.axis_index("c") == 0
    one[...] = jnp.where(first, to_plus, to_minus)
    two[...] = jnp.where(first, to_minus, to_plus)


def pair_weights(embed, radial):
    scalar, vector = [], []
    for kind in range(KINDS):
        row = embed[kind : kind + 1, :]
        scalar.append(radial[0] * row * 0.25)
        vector.append(radial[1] * row * 0.05)
    return jnp.concatenate(scalar, axis=0), jnp.concatenate(vector, axis=0)


def basis_centers():
    return row_of((BASIS, N)).astype(jnp.float32) * (CUTOFF / (BASIS - 1))


def edge_kernel(
    pos, species, nbr, near_x, far_x, near_y, far_y, embed, radial,
    shared, active, invariants, vectors, sums, edges, places,
):
    at = lane((8, N))
    own = [pos[0:1, :], pos[1:2, :], pos[2:3, :], species[...].astype(jnp.float32)]
    core_zero = lax.axis_index("c") == 0
    even = lax.axis_index("x") % 2 == 0
    first = jnp.where(core_zero, near_x[...], far_x[...])
    second = jnp.where(core_zero, far_x[...], near_x[...])
    plus_y = jnp.where(even, near_y[...], far_y[...])
    minus_y = jnp.where(even, far_y[...], near_y[...])
    third = jnp.where(at < 64, plus_y, pltpu.roll(minus_y, 64, 1))
    line = lane((1, N))
    corner_y = jnp.where(line < 64, 0.0, jnp.where(line < 96, DOMAIN, -DOMAIN))
    tables = [
        own,
        [first[0:1] + DOMAIN, first[1:2] + corner_y, first[2:3], first[3:4]],
        [second[0:1] - DOMAIN, second[1:2] + corner_y, second[2:3], second[3:4]],
        [third[0:1], third[1:2] + jnp.where(line < 64, DOMAIN, -DOMAIN), third[2:3], third[3:4]],
    ]
    for group in range(SLOTS // 8):
        rows = slice(8 * group, 8 * group + 8)
        slot = nbr[rows, :]
        block = lax.shift_right_logical(slot, 6)
        table = jnp.where(
            block < 2,
            0,
            jnp.where(
                (block == 4) | (block == 5), 3, jnp.where((block & 1) == 0, 1, 2)
            ),
        )
        table = jnp.where(block == 8, 4, table)
        half = jnp.where((block == 1) | ((block >= 5) & (block < 8)), 64, 0)
        place = (slot & 63) + half
        found = []
        for number in range(4):
            value = take(tables[0][number], place)
            for other in range(1, 4):
                value = jnp.where(table == other, take(tables[other][number], place), value)
            found.append(value)
        offset = [found[d] - own[d] for d in range(3)]
        dist_sq = offset[0] * offset[0] + offset[1] * offset[1] + offset[2] * offset[2]
        valid = (table < 4).astype(jnp.float32)
        ramp = jnp.maximum(1.0 - dist_sq / (CUTOFF * CUTOFF), 0.0)
        edges[0, rows, :] = offset[0]
        edges[1, rows, :] = offset[1]
        edges[2, rows, :] = offset[2]
        edges[3, rows, :] = found[3]
        edges[4, rows, :] = jnp.sqrt(dist_sq + SOFTEN)
        edges[5, rows, :] = ramp * ramp * valid
        edges[6, rows, :] = (-2.0 / (CUTOFF * CUTOFF)) * ramp * valid
        places[0, rows, :] = table
        places[1, rows, :] = place
    centers = basis_centers()

    def step(slot, carry):
        row = pl.ds(slot, 1)
        away = edges[4, row, :] - centers
        basis = jnp.exp(-WIDTH_GAUSS * away * away) * edges[5, row, :]
        parts = [basis] + [basis * edges[d, row, :] for d in range(3)]
        kind_row = jnp.broadcast_to(edges[3, row, :], (BASIS, N))
        out = []
        for kind in range(KINDS):
            mask = kind_row == float(kind)
            for number in range(4):
                out.append(carry[4 * kind + number] + jnp.where(mask, parts[number], 0.0))
        return tuple(out)

    zero = jnp.zeros((BASIS, N), jnp.float32)
    total = lax.fori_loop(0, SLOTS, step, (zero,) * (4 * KINDS), unroll=16)
    for number in range(4):
        sums[number, :, :] = jnp.concatenate(
            [total[4 * kind + number] for kind in range(KINDS)], axis=0
        )
    scalar_w, vector_w = pair_weights(embed, radial)
    value = dot(sums[0], scalar_w, 0, 0)
    for d in range(3):
        vector = dot(sums[1 + d], vector_w, 0, 0)
        vectors[d, :, :] = vector
        value = value + vector * vector
    invariants[...] = value
    result = value * sigmoid(value)
    active[...] = result
    anchor_x = lax.convert_element_type(lax.axis_index(GX), jnp.float32) * DOMAIN
    anchor_y = lax.convert_element_type(lax.axis_index(GY), jnp.float32) * DOMAIN
    zero_row = jnp.zeros((1, N), jnp.float32)
    tail = jnp.concatenate(
        [own[0] + anchor_x, own[1] + anchor_y, own[2], own[3]] + [zero_row] * 4, axis=0
    )
    shared[0:N, :] = result
    shared[N : N + 8, :] = tail


def edge_back_kernel(
    tile_0, tile_1, tile_2, tile_3, active, invariants, vectors, sums, edges, places, embed, radial, w_up, w_charge,
    species, grad_out, read_row,
    payload, own_grad, charge_piece,
):
    total = tile_0[...] + tile_1[...] + tile_2[...] + tile_3[...]
    grad_charges = jnp.transpose(total[0:N, :])
    updated = grad_out[...] + dot(grad_charges, w_charge[...], 1, 1)
    value = invariants[...]
    logistic = sigmoid(value)
    slope = logistic * (1.0 + value * (1.0 - logistic))
    grad_inv = dot(updated, w_up[...], 1, 1) * slope
    scalar_w, vector_w = pair_weights(embed, radial)
    pulls = [dot(scalar_w, grad_inv, 1, 1)]
    grad_scalar = dot(sums[0], grad_inv)
    grad_vector = jnp.zeros((KINDS * BASIS, N), jnp.float32)
    for d in range(3):
        along = 2.0 * vectors[d] * grad_inv
        pulls.append(dot(vector_w, along, 1, 1))
        grad_vector = grad_vector + dot(sums[1 + d], along)
    onehot = (row_of((8, N)) == species[...]).astype(jnp.float32)
    grad_table = dot(onehot, updated)
    radial_zero = jnp.zeros((BASIS, N), jnp.float32)
    radial_one = jnp.zeros((BASIS, N), jnp.float32)
    table_rows = []
    for kind in range(KINDS):
        rows = slice(kind * BASIS, (kind + 1) * BASIS)
        row = embed[kind : kind + 1, :]
        part_zero, part_one = grad_scalar[rows] * 0.25, grad_vector[rows] * 0.05
        radial_zero = radial_zero + part_zero * row
        radial_one = radial_one + part_one * row
        table_rows.append(
            grad_table[kind : kind + 1]
            + jnp.sum(radial[0] * part_zero + radial[1] * part_one, axis=0, keepdims=True)
        )
    rest = jnp.concatenate(
        [radial_zero, radial_one] + table_rows + [read_row[...], jnp.zeros((1, N), jnp.float32)],
        axis=0,
    )
    up_piece = total[N + 8 : N + 24, :]
    charge_piece[...] = total[N + 24 : N + 40, :]
    centers = basis_centers()
    sub = row_of((8, N))
    sub_table = sub & 3
    high_rows = sub < 4
    lane_rows = row_of((N, N))
    pull = [
        [pulls[number][kind * BASIS : (kind + 1) * BASIS] for number in range(4)]
        for kind in range(KINDS)
    ]

    def step(slot, carry):
        row = pl.ds(slot, 1)
        kind_row = jnp.broadcast_to(edges[3, row, :], (BASIS, N))
        own_pull = list(pull[KINDS - 1])
        for kind in range(KINDS - 1):
            mask = kind_row == float(kind)
            own_pull = [jnp.where(mask, pull[kind][n], own_pull[n]) for n in range(4)]
        radius = edges[4, row, :]
        envelope = edges[5, row, :]
        away = radius - centers
        bell = jnp.exp(-WIDTH_GAUSS * away * away)
        offset = [jnp.broadcast_to(edges[d, row, :], (BASIS, N)) for d in range(3)]
        by_basis = own_pull[0]
        for d in range(3):
            by_basis = by_basis + offset[d] * own_pull[1 + d]
        by_square = by_basis * bell * (edges[6, row, :] - (2.0 * envelope / radius) * away)
        basis = bell * envelope
        table = jnp.broadcast_to(places[0, row, :], (8, N)) == sub_table
        place = lane_rows == places[1, row, :]
        onehot = jnp.where(place, 1.0, 0.0).astype(jnp.bfloat16)
        centre, pieces = [], []
        for d in range(3):
            part = basis * own_pull[1 + d] + 2.0 * offset[d] * by_square
            centre.append(carry[d] + part)
            whole = jnp.broadcast_to(jnp.sum(part, axis=0, keepdims=True), (8, N))
            high = whole.astype(jnp.bfloat16).astype(jnp.float32)
            pieces.append(jnp.where(table, jnp.where(high_rows, high, whole - high), 0.0))
        rows = jnp.concatenate(pieces, axis=0).astype(jnp.bfloat16)
        return (*centre, carry[3] + half_dot(rows, onehot, 1, 1))

    zero = jnp.zeros((8, N), jnp.float32)
    out = lax.fori_loop(
        0, SLOTS, step, (zero, zero, zero, jnp.zeros((24, N), jnp.float32)), unroll=16
    )
    scattered = out[3]
    waves = total[N : N + 8, :]
    own_rows, one_rows, two_rows, three_rows = [], [], [], []
    for d in range(3):
        both = scattered[8 * d : 8 * d + 4] + scattered[8 * d + 4 : 8 * d + 8]
        centre = jnp.sum(out[d], axis=0, keepdims=True)
        own_rows.append(both[0:1] - centre + waves[d : d + 1])
        one_rows.append(both[1:2])
        two_rows.append(both[2:3])
        three_rows.append(both[3:4])
    pad = [jnp.zeros((5, N), jnp.float32)]
    own_grad[...] = jnp.concatenate(own_rows + pad, axis=0)
    depth_of = [depth_after(step_x, step_y) for step_x, step_y in TABLE_DIRS]
    line = lane((8, N))
    ones = jnp.concatenate(one_rows + pad, axis=0)
    twos = jnp.concatenate(two_rows + pad, axis=0)
    threes = jnp.concatenate(three_rows + pad, axis=0)
    home_one = segments(line, depth_of[0:3])
    home_two = segments(line, depth_of[3:6])
    home_three = jnp.where(line < 64, depth_of[6], depth_of[7])
    for other in range(8):
        payload[other, 0:16, :] = up_piece
        payload[other, 16:40, :] = rest
        payload[other, 40:48, :] = pack_six(
            jnp.where(home_one == other, ones, 0.0), jnp.where(home_two == other, twos, 0.0)
        )
        payload[other, 48:56, :] = jnp.where(home_three == other, threes, 0.0)


TABLE_DIRS = ((1, 0), (1, 1), (1, -1), (-1, 0), (-1, 1), (-1, -1), (0, 1), (0, -1))


def segments(line, values):
    return jnp.where(line < 64, values[0], jnp.where(line < 96, values[1], values[2]))


def pack_six(one, two):
    return jnp.where(row_of((8, N)) < 4, one, pltpu.roll(two, 4, 0))


def depth_after(step_x, step_y):
    core, high = lax.axis_index("c"), lax.axis_index("zh")
    low, column = lax.axis_index("zl"), lax.axis_index("x")
    if step_x == 1:
        high = jnp.where(core == 1, (high + 1) % 4, high)
    if step_x == -1:
        high = jnp.where(core == 0, (high + 3) % 4, high)
    if step_y == 1:
        low = jnp.where(column == 3, 1 - low, low)
    if step_y == -1:
        low = jnp.where(column == 0, 1 - low, low)
    return high * 2 + low


def plane_after(step_x, step_y):
    core, high = lax.axis_index("c"), lax.axis_index("zh")
    row, column = lax.axis_index("y"), lax.axis_index("x")
    if step_x == 1:
        row = jnp.where((core == 1) & (high == 0), (row + 1) % 4, row)
    if step_x == -1:
        row = jnp.where((core == 0) & (high == 3), (row + 3) % 4, row)
    return row * 4 + (column + step_y + 4) % 4


def depth_sum_kernel(tiles, charge_piece, out):
    total = jnp.sum(tiles[...], axis=0)
    place_of = [plane_after(step_x, step_y) for step_x, step_y in TABLE_DIRS]
    line = lane((8, N))
    home = jnp.where(
        row_of((8, N)) < 4, segments(line, place_of[0:3]), segments(line, place_of[3:6])
    )
    home_three = jnp.where(line < 64, place_of[6], place_of[7])
    sixes, threes = total[40:48], total[48:56]
    row = lax.axis_index("y")
    quarter = charge_piece[0:4, :]
    for number in range(1, 4):
        quarter = jnp.where(row == number, charge_piece[4 * number : 4 * number + 4, :], quarter)
    for other in range(16):
        out[other, 0:40, :] = total[0:40]
        out[other, 40:48, :] = jnp.where(home == other, sixes, 0.0)
        out[other, 48:56, :] = jnp.where(home_three == other, threes, 0.0)
        out[other, 52:56, :] = quarter


def plane_sum_kernel(tiles, swap, threes):
    for column in range(4):
        total = tiles[column, 0:16, :]
        for row in range(1, 4):
            total = total + tiles[4 * row + column, 0:16, :]
        swap[16 * column : 16 * column + 16, :] = total
        for row in range(4):
            at = 96 + 16 * column + 4 * row
            swap[at : at + 4, :] = tiles[4 * row + column, 52:56, :]
    rest = tiles[0, 16:56, :]
    for other in range(1, 16):
        rest = rest + tiles[other, 16:56, :]
    swap[64:96, :] = rest[0:32]
    threes[...] = jnp.where(row_of((8, N)) < 4, rest[32:40], 0.0)


def finish_kernel(own, other, threes, own_grad, home, forces, grad_embed, grad_radial, grad_up,
                  grad_charge, grad_read):
    mean = 1.0 / ATOMS
    core = lax.axis_index("c")
    mine = pl.ds(pl.multiple_of(core * 64, 64), 64)
    theirs = pl.ds(pl.multiple_of((1 - core) * 64, 64), 64)
    grad_up[mine, :] = own[0:64, :] * mean
    grad_up[theirs, :] = other[0:64, :] * mean
    grad_charge[mine, :] = own[96:160, :] * mean
    grad_charge[theirs, :] = other[96:160, :] * mean
    total = (own[64:88, :] + other[64:88, :]) * mean
    grad_radial[0, :, :] = total[0:8]
    grad_radial[1, :, :] = total[8:16]
    grad_embed[...] = total[16:22]
    grad_read[...] = total[22:23]
    sixes = other[88:96, :]
    grad = own_grad[...]
    lane_rows = row_of((N, N))
    for number, piece in enumerate((sixes, pltpu.roll(sixes, 4, 0), threes[...])):
        onehot = jnp.where(lane_rows == home[number : number + 1, :], 1.0, 0.0)
        grad = grad + dot(piece, onehot, 1, 1)
    forces[...] = -grad[0:3, :]


def spread_kernel(*refs):
    out = refs[-1]
    core, column = lax.axis_index("c"), lax.axis_index("x")
    for number, pair in enumerate(refs[:-1]):
        for half in range(2):
            source = column ^ (2 * (number % 2) + half)
            member = jnp.where(number < 2, core, 1 - core) * 4 + source
            place = pl.ds(pl.multiple_of(member * SHARD, SHARD), SHARD)
            out[place, :] = pair[half * SHARD : (half + 1) * SHARD, :]


def structure_kernel(*refs):
    tiles = refs[:MEMBERS]
    kvec, embed, w_up, factor, wave_high, wave_low, feature_high, feature_low = refs[MEMBERS:]
    me = lax.axis_index(GROUP)
    at = pl.multiple_of(me * SHARD, SHARD)
    rows = jnp.concatenate(
        [kvec[:, pl.ds(at, SHARD)], jnp.zeros((5, SHARD), jnp.float32)], axis=0
    )
    turns = jnp.transpose(rows * (1.0 / (2.0 * math.pi)))
    table = jnp.concatenate([embed[...], jnp.zeros((2, N), jnp.float32)], axis=0)
    up = split(w_up[...])
    for member in range(MEMBERS):
        part = slice(member * N, (member + 1) * N)
        tile = tiles[member]
        tail = tile[N : N + 8, :]
        onehot = (row_of((8, N)).astype(jnp.float32) == tail[3:4, :]).astype(jnp.float32)
        feature = exact_dot(onehot, table, 0, 0) + dot_three(split(tile[0:N, :]), up)
        high, low = split(feature)
        feature_high[part, :] = high
        feature_low[part, :] = low
        for chunk in range(SHARD // 64):
            waves = slice(chunk * 64, chunk * 64 + 64)
            angle = (
                turns[waves, 0:1] * tail[0:1, :]
                + turns[waves, 1:2] * tail[1:2, :]
                + turns[waves, 2:3] * tail[2:3, :]
            )
            angle = angle - jnp.round(angle)
            square = angle * angle
            cosine = jnp.full(square.shape, COS_POLY[-1], jnp.float32)
            for value in COS_POLY[-2::-1]:
                cosine = cosine * square + value
            sine = jnp.full(square.shape, SIN_POLY[-1], jnp.float32)
            for value in SIN_POLY[-2::-1]:
                sine = sine * square + value
            sine = sine * angle
            high, low = split(cosine)
            wave_high[waves, part] = high
            wave_low[waves, part] = low
            high, low = split(sine)
            waves = slice(SHARD + chunk * 64, SHARD + chunk * 64 + 64)
            wave_high[waves, part] = high
            wave_low[waves, part] = low
    project(wave_high, wave_low, feature_high[...], feature_low[...], factor)


def whole(tiles):
    return jnp.concatenate([tile[0:N, :] for tile in tiles], axis=0)


def project(wave_high, wave_low, high, low, out):
    both = jnp.concatenate([high, low], axis=1)
    wide = half_dot(wave_high[...], both)
    total = wide[:, 0:N] + wide[:, N:] + half_dot(wave_low[...], high)
    out[...] = total.reshape(CROSSES, 16, N)


def projection_kernel(*refs):
    wave_high, wave_low, out = refs[MEMBERS:]
    high, low = split(whole(refs[:MEMBERS]))
    project(wave_high, wave_low, high, low, out)


def sum_kernel(tiles, out):
    total = jnp.sum(tiles[...], axis=0)
    for other in range(out.shape[0]):
        out[other, :, :] = total


def filter_of(kfilter):
    me = lax.axis_index(GROUP)
    return kfilter[pl.ds(pl.multiple_of(me * SHARD, SHARD), SHARD), :] * SCALE


def core_sum_kernel(mine, other, *out):
    for number, ref in enumerate(out):
        ref[...] = mine[number] + other[number]


def waves_to_atoms(field, wave_high, wave_low):
    high, low = split(jnp.transpose(field))
    wide = half_dot(jnp.concatenate([high, low], axis=0), wave_high[...])
    return wide[0:N] + wide[N:] + half_dot(high, wave_low[...])


def potential_kernel(factor, w_charge, kfilter, wave_high, wave_low,
                     mine, other, weighted, charge_factor):
    scaled = filter_of(kfilter)
    charged = dot(factor[...], w_charge[...])
    charge_factor[...] = charged
    field = charged * jnp.concatenate([scaled, scaled], axis=0)
    weighted[...] = field
    total = waves_to_atoms(field, wave_high, wave_low)
    for member in range(MEMBERS):
        (mine, other)[member // 4][member % 4] = total[:, member * N : (member + 1) * N]


def energy_kernel(tile_0, tile_1, tile_2, tile_3, feature_high, feature_low, read,
                  grad_out, result_out):
    total = tile_0[...] + tile_1[...] + tile_2[...] + tile_3[...]
    feature = feature_high[0:N, :].astype(jnp.float32) + feature_low[0:N, :].astype(jnp.float32)
    combined = feature + jnp.transpose(total)
    logistic = sigmoid(combined)
    result_out[...] = combined * logistic
    grad_out[...] = read[...] * (logistic * (1.0 + combined * (1.0 - logistic)))


def read_kernel(result, grad, active, read, energy, read_row, up_part):
    value = result[...]
    energy[...] = dot(jnp.broadcast_to(read[...], (8, N)), value, 1, 1)[0:1, :]
    read_row[...] = jnp.sum(value, axis=0, keepdims=True)
    up_part[...] = dot(active[...], grad[...], 0, 0)


def wave_trig(wave_high, wave_low):
    cosine = wave_high[0:SHARD, :].astype(jnp.float32) + wave_low[0:SHARD, :].astype(jnp.float32)
    sine = wave_high[SHARD:, :].astype(jnp.float32) + wave_low[SHARD:, :].astype(jnp.float32)
    return cosine, sine


def wave_back_kernel(*refs):
    grads, shared = refs[:MEMBERS], refs[MEMBERS : 2 * MEMBERS]
    (
        projected, factor, charge_factor, weighted, kfilter, kvec, wave_high, wave_low,
        feature_high, feature_low, w_charge, up_part,
        mine, other, grad_filter, up_grad, charge_grad,
    ) = refs[2 * MEMBERS :]
    scaled = filter_of(kfilter)
    proj = projected[...]
    mixed = charge_factor[...] * proj
    grad_filter[...] = SCALE * (mixed[0:SHARD] + mixed[SHARD:])
    field = proj * jnp.concatenate([scaled, scaled], axis=0)
    pieces = split(field)
    by_charge = waves_to_atoms(field, wave_high, wave_low)
    charge_grad[...] = dot_three(split(factor[...]), pieces, 0, 0)
    active = whole(shared)
    mix = dot_three(split(by_charge), split(active))
    weights = split(w_charge[...])
    up_grad[...] = dot_three(split(mix), weights, 0, 1) + up_part[...]
    by_feature = dot_three(pieces, weights, 1, 1)
    grad_high, grad_low = split(whole(grads))
    along = dot_three(
        split(jnp.concatenate([weighted[...], by_feature], axis=1)),
        (
            jnp.concatenate([grad_high, feature_high[...]], axis=1),
            jnp.concatenate([grad_low, feature_low[...]], axis=1),
        ),
        1, 1,
    )
    cosine, sine = wave_trig(wave_high, wave_low)
    phase = cosine * along[SHARD:] - sine * along[0:SHARD]
    me = lax.axis_index(GROUP)
    rows = jnp.concatenate(
        [
            kvec[:, pl.ds(pl.multiple_of(me * SHARD, SHARD), SHARD)],
            jnp.zeros((5, SHARD), jnp.float32),
        ],
        axis=0,
    )
    by_pos = dot_three(split(rows), split(phase))
    core, column = lax.axis_index("c"), lax.axis_index("x")
    for member in range(MEMBERS):
        part = slice(member * N, (member + 1) * N)
        out = (mine, other)[member // 4].at[member % 4]
        place = jnp.where(core == member // 4, 0, 4) + (column + 4 - member % 4) % 4
        place = place * 16
        piece = pl.ds(pl.multiple_of(place, 16), 16)
        out[0:N, :] = by_charge[:, part]
        out[N : N + 8, :] = by_pos[:, part]
        out[N + 8 : N + 24, :] = up_grad[piece, :]
        out[N + 24 : N + 40, :] = charge_grad[piece, :]


def body(
    positions, species, neighbours, face_sends, corner_sends,
    embed, radial, w_up, w_charge, kvec, kfilter, read,
):
    near, far, own_x, home, positions, species, neighbours, embed, radial, read = call(
        pack_kernel,
        (f32(8, N),) * 3
        + (
            i32(8, N), f32(3, N), i32(1, N), i32(SLOTS, N), f32(KINDS, N), f32(2, BASIS, N),
            f32(1, N),
        ),
        positions, species.reshape(1, N), face_sends, corner_sends, neighbours, embed, radial,
        read.reshape(1, N),
        scratch=(
            pltpu.VMEM((4, N // 2), jnp.int32),
            pltpu.VMEM((4, N // 4), jnp.int32),
            pltpu.SemaphoreType.DMA((8,)),
        ),
        far=True,
    )
    near_y, far_y = swapped(near, GY, 0), swapped(far, GY, 1)
    near, far = call(relay_kernel, (f32(8, N),) * 2, own_x, near_y, far_y)
    near_x, far_x = swapped(near, GX, 0), swapped(far, GX, 1)
    shared, active, invariants, vectors, sums, edges, places = call(
        edge_kernel,
        (
            f32(N + 8, N), f32(N, N), f32(N, N), f32(3, N, N), f32(4, KINDS * BASIS, N),
            f32(7, SLOTS, N), i32(2, SLOTS, N),
        ),
        positions, species, neighbours, near_x, far_x, near_y, far_y, embed, radial,
    )
    swap = [(0, 1), (1, 0)]

    def other_core(value):
        return lax.ppermute(value, "c", swap)

    def step_x(value, step):
        return lax.ppermute(value, "x", [(at, (at + step) % 4) for at in range(4)])

    def gather(value):
        values = [value] + [step_x(value, step) for step in (1, 2, 3)]
        return values + [other_core(item) for item in values]

    def scatter(mine, other):
        tiles = call(core_sum_kernel, (f32(*mine.shape[1:]),) * 4, mine, other_core(other))
        return [tiles[0]] + [step_x(tiles[step], -step) for step in (1, 2, 3)]

    shared = gather(shared)
    half = jax.ShapeDtypeStruct((2 * SHARD, MEMBERS * N), jnp.bfloat16)
    feature = jax.ShapeDtypeStruct((MEMBERS * N, N), jnp.bfloat16)
    factor, wave_high, wave_low, feature_high, feature_low = call(
        structure_kernel,
        (f32(CROSSES, 16, N), half, half, feature, feature),
        *shared, kvec, embed, w_up,
    )

    def cross_sum(tiles):
        tiles = lax.all_to_all(tiles, CROSS, 0, 0)
        tiles = call(sum_kernel, f32(CROSSES, 16, N), tiles)
        return lax.all_to_all(tiles, CROSS, 0, 0).reshape(2 * SHARD, N)

    factor = cross_sum(factor)
    mine, other, weighted, charge_factor = call(
        potential_kernel,
        (f32(4, N, N), f32(4, N, N), f32(2 * SHARD, N), f32(2 * SHARD, N)),
        factor, w_charge, kfilter, wave_high, wave_low,
    )
    grad_out, result = call(
        energy_kernel, (f32(N, N),) * 2, *scatter(mine, other), feature_high, feature_low, read
    )
    grads = gather(grad_out)
    energy, read_row, up_part = call(
        read_kernel, (f32(1, N), f32(1, N), f32(N, N)), result, grad_out, active, read
    )
    *grads, energy, read_row, up_part = lax.optimization_barrier(
        (*grads, energy, read_row, up_part)
    )
    projected = cross_sum(
        call(projection_kernel, f32(CROSSES, 16, N), *grads, wave_high, wave_low)
    )
    square = pltpu.VMEM((N, N), jnp.float32)
    mine, other, shard = call(
        wave_back_kernel,
        (f32(4, N + 40, N), f32(4, N + 40, N), f32(SHARD, N)),
        *grads, *shared, projected, factor, charge_factor, weighted, kfilter, kvec,
        wave_high, wave_low, feature_high, feature_low, w_charge, up_part,
        scratch=(square, square),
    )
    tiles = scatter(mine, other)
    shard, *tiles = lax.optimization_barrier((shard, *tiles))
    next_shard = lax.ppermute(shard, "x", [(at, at ^ 1) for at in range(4)])
    payload, own_grad, charge_piece = call(
        edge_back_kernel,
        (f32(8, 56, N), f32(8, N), f32(16, N)),
        *tiles, active, invariants, vectors, sums, edges, places, embed, radial, w_up,
        w_charge, species, grad_out, read_row,
        cost=pl.CostEstimate(flops=10**9, bytes_accessed=10**7, transcendentals=10**5),
    )
    payload, next_shard = lax.optimization_barrier((payload, next_shard))
    near_shards = jnp.concatenate([shard, next_shard], axis=0)
    far_shards = lax.ppermute(near_shards, "x", [(at, at ^ 2) for at in range(4)])
    payload = lax.all_to_all(payload, DEPTH, 0, 0)
    payload = call(depth_sum_kernel, f32(16, 56, N), payload, charge_piece)
    payload = lax.all_to_all(payload, PLANE, 0, 0)
    payload, threes = call(plane_sum_kernel, (f32(160, N), f32(8, N)), payload)
    shards = [near_shards, far_shards, other_core(near_shards), other_core(far_shards)]
    payload_other = other_core(payload)
    grad_filter = call(spread_kernel, f32(WAVES, N), *shards)
    forces, grad_embed, grad_radial, grad_up, grad_charge, grad_read = call(
        finish_kernel,
        (f32(3, N), f32(KINDS, N), f32(2, BASIS, N), f32(N, N), f32(N, N), f32(1, N)),
        payload, payload_other, threes, own_grad, home,
    )
    return (
        energy.reshape(N), forces, grad_embed, grad_radial, grad_up, grad_charge, grad_filter,
        grad_read.reshape(N),
    )


def solution(mesh):
    fine = Mesh(mesh.devices.reshape(4, 4, 2, 2, 4), ALL)
    atoms = P(ALL)
    rows = P(None, ALL)
    return jax.shard_map(
        body,
        mesh=fine,
        in_specs=(rows, atoms, rows, rows, rows) + (P(),) * 7,
        out_specs=(atoms, rows) + (P(),) * 6,
        check_vma=False,
    )
```

```python
import functools
import math

import jax
import jax.numpy as jnp
from jax import lax
from jax.experimental import pallas as pl
from jax.experimental.pallas import tpu as pltpu
from jax.sharding import Mesh
from jax.sharding import PartitionSpec as P

CUTOFF = 5.0
SOFTEN = 0.01
WIDTH_GAUSS = 2.0
DOMAIN = 8.8
N = 128
SLOTS = 64
KINDS = 6
BASIS = 8
WAVES = 2048
ATOMS = 32768
SHARD = 256
HIGHEST = lax.Precision.HIGHEST
SCALE = 1.0 / math.sqrt(ATOMS * WAVES)

GX = ("y", "zh", "c")
GY = ("zl", "x")
ALL = GX + GY
GROUP = ("c", "x")
CROSS = ("y", "zh", "zl")
MEMBERS = 8
CROSSES = 32
DEPTH = ("zh", "zl")
PLANE = ("y", "x")

COS_POLY = None
SIN_POLY = None


def _fit():
    import numpy as np

    points = (1.0 + np.cos(np.pi * (np.arange(200) + 0.5) / 200)) / 8.0
    root = np.sqrt(points)
    found = []
    for count, value in ((7, np.cos(2 * np.pi * root)), (6, np.sin(2 * np.pi * root) / root)):
        matrix = np.vander(points * 4.0, count, increasing=True)
        terms = np.linalg.lstsq(matrix, value, rcond=None)[0] * 4.0 ** np.arange(count)
        found.append([float(term) for term in terms])
    return found


COS_POLY, SIN_POLY = _fit()


def dims(left, right):
    return (((left,), (right,)), ((), ()))


def exact_dot(left, right, left_dim=1, right_dim=0):
    return lax.dot_general(
        left,
        right,
        dims(left_dim, right_dim),
        precision=HIGHEST,
        preferred_element_type=jnp.float32,
    )


def half_dot(left, right, left_dim=1, right_dim=0):
    return lax.dot_general(
        left, right, dims(left_dim, right_dim), preferred_element_type=jnp.float32
    )


def split(value):
    high = value.astype(jnp.bfloat16)
    return high, (value - high.astype(jnp.float32)).astype(jnp.bfloat16)


def dot_three(left, right, left_dim=1, right_dim=0):
    left_high, left_low = left
    right_high, right_low = right
    return (
        half_dot(left_high, right_high, left_dim, right_dim)
        + half_dot(left_high, right_low, left_dim, right_dim)
        + half_dot(left_low, right_high, left_dim, right_dim)
    )


def dot(left, right, left_dim=1, right_dim=0):
    return dot_three(split(left), split(right), left_dim, right_dim)


def sigmoid(value):
    return 1.0 / (1.0 + jnp.exp(-value))


def lane(shape):
    return lax.broadcasted_iota(jnp.int32, shape, 1)


def row_of(shape):
    return lax.broadcasted_iota(jnp.int32, shape, 0)


def call(kernel, out_shape, *args, scratch=(), vmem=32, far=False, cost=None):
    more = {}
    if far:
        more["in_specs"] = [pl.BlockSpec(memory_space=pltpu.HBM)] * len(args)
        args = [pltpu.with_memory_space_constraint(value, pltpu.HBM) for value in args]
    return pl.pallas_call(
        kernel,
        out_shape=out_shape,
        scratch_shapes=list(scratch),
        cost_estimate=cost,
        **more,
        compiler_params=pltpu.CompilerParams(vmem_limit_bytes=vmem * 1024 * 1024),
    )(*args)


def f32(*shape):
    return jax.ShapeDtypeStruct(shape, jnp.float32)


def i32(*shape):
    return jax.ShapeDtypeStruct(shape, jnp.int32)


def take(row, index):
    return jnp.take_along_axis(
        jnp.broadcast_to(row, index.shape), index, axis=1, mode="promise_in_bounds"
    )


def joined(face, corner, faces, corners):
    return jnp.concatenate(
        [face[f : f + 1, :] for f in faces] + [corner[f : f + 1, :] for f in corners], axis=1
    )


def pack_kernel(pos_in, species_in, face_in, corner_in, nbr_in, embed_in, radial_in, read_in,
                near, far, own, home, pos, species, nbr, embed, radial, read, face, corner, sems):
    pairs = (
        (pos_in, pos), (species_in, species), (face_in, face), (corner_in, corner),
        (nbr_in, nbr), (embed_in, embed), (radial_in, radial), (read_in, read),
    )
    copies = [
        pltpu.make_async_copy(source, target, sems.at[number])
        for number, (source, target) in enumerate(pairs)
    ]
    for copy in copies:
        copy.start()
    for copy in copies:
        copy.wait()
    even = lax.axis_index("x") % 2 == 0
    rows = [pos[0:1, :], pos[1:2, :], pos[2:3, :], species[...].astype(jnp.float32)]
    padding = jnp.zeros((5, N), jnp.int32)
    where_from = jnp.concatenate(
        [
            joined(face, corner, (2,), (0, 2)),
            joined(face, corner, (3,), (1, 3)),
            joined(face, corner, (0, 1), ()),
            padding,
        ],
        axis=0,
    )
    home[...] = jnp.concatenate(
        [
            joined(face, corner, (0,), (0, 1)),
            joined(face, corner, (1,), (2, 3)),
            joined(face, corner, (2, 3), ()),
            padding,
        ],
        axis=0,
    )
    for number, row in enumerate(rows):
        got = take(row, where_from)
        near[number : number + 1, :] = jnp.where(even, got[1:2, :], got[0:1, :])
        far[number : number + 1, :] = jnp.where(even, got[0:1, :], got[1:2, :])
        own[number : number + 1, :] = got[2:3, :]
    zero = jnp.zeros((4, N), jnp.float32)
    near[4:8, :] = zero
    far[4:8, :] = zero
    own[4:8, :] = zero


def swapped(value, axes, odd):
    count = math.prod(lax.axis_size(axis) for axis in axes)
    places = [(at, ((((at + odd) % count) ^ 1) - odd) % count) for at in range(count)]
    return lax.ppermute(value, axes, places)


def relay_kernel(own, near, far, one, two):
    at = lane((8, N))
    even = lax.axis_index("x") % 2 == 0
    a = own[...]
    b = jnp.where(even, near[...], far[...])
    d = jnp.where(even, far[...], near[...])
    to_minus = jnp.where(at < 64, a, jnp.where(at < 96, b, pltpu.roll(d, 32, 1)))
    to_plus = jnp.where(
        at < 64, pltpu.roll(a, 64, 1), jnp.where(at < 96, pltpu.roll(b, 96, 1), d)
    )
    first = lax.axis_index("c") == 0
    one[...] = jnp.where(first, to_plus, to_minus)
    two[...] = jnp.where(first, to_minus, to_plus)


def pair_weights(embed, radial):
    scalar, vector = [], []
    for kind in range(KINDS):
        row = embed[kind : kind + 1, :]
        scalar.append(radial[0] * row * 0.25)
        vector.append(radial[1] * row * 0.05)
    return jnp.concatenate(scalar, axis=0), jnp.concatenate(vector, axis=0)


def basis_centers():
    return row_of((BASIS, N)).astype(jnp.float32) * (CUTOFF / (BASIS - 1))


def edge_kernel(
    pos, species, nbr, near_x, far_x, near_y, far_y, embed, radial,
    shared, active, invariants, vectors, sums, edges, places,
):
    at = lane((8, N))
    own = [pos[0:1, :], pos[1:2, :], pos[2:3, :], species[...].astype(jnp.float32)]
    core_zero = lax.axis_index("c") == 0
    even = lax.axis_index("x") % 2 == 0
    first = jnp.where(core_zero, near_x[...], far_x[...])
    second = jnp.where(core_zero, far_x[...], near_x[...])
    plus_y = jnp.where(even, near_y[...], far_y[...])
    minus_y = jnp.where(even, far_y[...], near_y[...])
    third = jnp.where(at < 64, plus_y, pltpu.roll(minus_y, 64, 1))
    line = lane((1, N))
    corner_y = jnp.where(line < 64, 0.0, jnp.where(line < 96, DOMAIN, -DOMAIN))
    tables = [
        own,
        [first[0:1] + DOMAIN, first[1:2] + corner_y, first[2:3], first[3:4]],
        [second[0:1] - DOMAIN, second[1:2] + corner_y, second[2:3], second[3:4]],
        [third[0:1], third[1:2] + jnp.where(line < 64, DOMAIN, -DOMAIN), third[2:3], third[3:4]],
    ]
    for group in range(SLOTS // 8):
        rows = slice(8 * group, 8 * group + 8)
        slot = nbr[rows, :]
        block = lax.shift_right_logical(slot, 6)
        table = jnp.where(
            block < 2,
            0,
            jnp.where(
                (block == 4) | (block == 5), 3, jnp.where((block & 1) == 0, 1, 2)
            ),
        )
        table = jnp.where(block == 8, 4, table)
        half = jnp.where((block == 1) | ((block >= 5) & (block < 8)), 64, 0)
        place = (slot & 63) + half
        found = []
        for number in range(4):
            value = take(tables[0][number], place)
            for other in range(1, 4):
                value = jnp.where(table == other, take(tables[other][number], place), value)
            found.append(value)
        offset = [found[d] - own[d] for d in range(3)]
        dist_sq = offset[0] * offset[0] + offset[1] * offset[1] + offset[2] * offset[2]
        valid = (table < 4).astype(jnp.float32)
        ramp = jnp.maximum(1.0 - dist_sq / (CUTOFF * CUTOFF), 0.0)
        edges[0, rows, :] = offset[0]
        edges[1, rows, :] = offset[1]
        edges[2, rows, :] = offset[2]
        edges[3, rows, :] = found[3]
        edges[4, rows, :] = jnp.sqrt(dist_sq + SOFTEN)
        edges[5, rows, :] = ramp * ramp * valid
        edges[6, rows, :] = (-2.0 / (CUTOFF * CUTOFF)) * ramp * valid
        places[0, rows, :] = table
        places[1, rows, :] = place
    centers = basis_centers()

    def step(slot, carry):
        row = pl.ds(slot, 1)
        away = edges[4, row, :] - centers
        basis = jnp.exp(-WIDTH_GAUSS * away * away) * edges[5, row, :]
        parts = [basis] + [basis * edges[d, row, :] for d in range(3)]
        kind_row = jnp.broadcast_to(edges[3, row, :], (BASIS, N))
        out = []
        for kind in range(KINDS):
            mask = kind_row == float(kind)
            for number in range(4):
                out.append(carry[4 * kind + number] + jnp.where(mask, parts[number], 0.0))
        return tuple(out)

    zero = jnp.zeros((BASIS, N), jnp.float32)
    total = lax.fori_loop(0, SLOTS, step, (zero,) * (4 * KINDS), unroll=16)
    for number in range(4):
        sums[number, :, :] = jnp.concatenate(
            [total[4 * kind + number] for kind in range(KINDS)], axis=0
        )
    scalar_w, vector_w = pair_weights(embed, radial)
    value = dot(sums[0], scalar_w, 0, 0)
    for d in range(3):
        vector = dot(sums[1 + d], vector_w, 0, 0)
        vectors[d, :, :] = vector
        value = value + vector * vector
    invariants[...] = value
    result = value * sigmoid(value)
    active[...] = result
    anchor_x = lax.convert_element_type(lax.axis_index(GX), jnp.float32) * DOMAIN
    anchor_y = lax.convert_element_type(lax.axis_index(GY), jnp.float32) * DOMAIN
    zero_row = jnp.zeros((1, N), jnp.float32)
    tail = jnp.concatenate(
        [own[0] + anchor_x, own[1] + anchor_y, own[2], own[3]] + [zero_row] * 4, axis=0
    )
    shared[0:N, :] = result
    shared[N : N + 8, :] = tail


def edge_back_kernel(
    tile_0, tile_1, tile_2, tile_3, active, invariants, vectors, sums, edges, places, embed, radial, w_up, w_charge,
    species, grad_out, read_row,
    payload, own_grad, charge_piece,
):
    total = tile_0[...] + tile_1[...] + tile_2[...] + tile_3[...]
    grad_charges = jnp.transpose(total[0:N, :])
    updated = grad_out[...] + dot(grad_charges, w_charge[...], 1, 1)
    value = invariants[...]
    logistic = sigmoid(value)
    slope = logistic * (1.0 + value * (1.0 - logistic))
    grad_inv = dot(updated, w_up[...], 1, 1) * slope
    scalar_w, vector_w = pair_weights(embed, radial)
    pulls = [dot(scalar_w, grad_inv, 1, 1)]
    grad_scalar = dot(sums[0], grad_inv)
    grad_vector = jnp.zeros((KINDS * BASIS, N), jnp.float32)
    for d in range(3):
        along = 2.0 * vectors[d] * grad_inv
        pulls.append(dot(vector_w, along, 1, 1))
        grad_vector = grad_vector + dot(sums[1 + d], along)
    onehot = (row_of((8, N)) == species[...]).astype(jnp.float32)
    grad_table = dot(onehot, updated)
    radial_zero = jnp.zeros((BASIS, N), jnp.float32)
    radial_one = jnp.zeros((BASIS, N), jnp.float32)
    table_rows = []
    for kind in range(KINDS):
        rows = slice(kind * BASIS, (kind + 1) * BASIS)
        row = embed[kind : kind + 1, :]
        part_zero, part_one = grad_scalar[rows] * 0.25, grad_vector[rows] * 0.05
        radial_zero = radial_zero + part_zero * row
        radial_one = radial_one + part_one * row
        table_rows.append(
            grad_table[kind : kind + 1]
            + jnp.sum(radial[0] * part_zero + radial[1] * part_one, axis=0, keepdims=True)
        )
    rest = jnp.concatenate(
        [radial_zero, radial_one] + table_rows + [read_row[...], jnp.zeros((1, N), jnp.float32)],
        axis=0,
    )
    up_piece = total[N + 8 : N + 24, :]
    charge_piece[...] = total[N + 24 : N + 40, :]
    centers = basis_centers()
    sub = row_of((8, N))
    sub_table = sub & 3
    high_rows = sub < 4
    lane_rows = row_of((N, N))
    pull = [
        [pulls[number][kind * BASIS : (kind + 1) * BASIS] for number in range(4)]
        for kind in range(KINDS)
    ]

    def one(slot):
        row = pl.ds(slot, 1)
        kind_row = jnp.broadcast_to(edges[3, row, :], (BASIS, N))
        own_pull = list(pull[KINDS - 1])
        for kind in range(KINDS - 1):
            mask = kind_row == float(kind)
            own_pull = [jnp.where(mask, pull[kind][n], own_pull[n]) for n in range(4)]
        radius = edges[4, row, :]
        envelope = edges[5, row, :]
        away = radius - centers
        bell = jnp.exp(-WIDTH_GAUSS * away * away)
        offset = [jnp.broadcast_to(edges[d, row, :], (BASIS, N)) for d in range(3)]
        by_basis = own_pull[0]
        for d in range(3):
            by_basis = by_basis + offset[d] * own_pull[1 + d]
        by_square = by_basis * bell * (edges[6, row, :] - (2.0 * envelope / radius) * away)
        basis = bell * envelope
        table = jnp.broadcast_to(places[0, row, :], (8, N)) == sub_table
        place = lane_rows == places[1, row, :]
        onehot = jnp.where(place, 1.0, 0.0).astype(jnp.bfloat16)
        parts, pieces = [], []
        for d in range(3):
            part = basis * own_pull[1 + d] + 2.0 * offset[d] * by_square
            parts.append(part)
            whole = jnp.broadcast_to(jnp.sum(part, axis=0, keepdims=True), (8, N))
            high = whole.astype(jnp.bfloat16).astype(jnp.float32)
            pieces.append(jnp.where(table, jnp.where(high_rows, high, whole - high), 0.0))
        return parts, jnp.concatenate(pieces, axis=0).astype(jnp.bfloat16), onehot

    def step(group, carry):
        found = [one(group * 8 + number) for number in range(8)]
        centre = list(carry[:3])
        for parts, _, _ in found:
            centre = [centre[d] + parts[d] for d in range(3)]
        rows = jnp.concatenate([item[1] for item in found], axis=1)
        onehot = jnp.concatenate([item[2] for item in found], axis=1)
        return (*centre, carry[3] + half_dot(rows, onehot, 1, 1))

    zero = jnp.zeros((8, N), jnp.float32)
    out = (zero, zero, zero, jnp.zeros((24, N), jnp.float32))
    for group in range(SLOTS // 8):
        out = step(group, out)
    scattered = out[3]
    waves = total[N : N + 8, :]
    own_rows, one_rows, two_rows, three_rows = [], [], [], []
    for d in range(3):
        both = scattered[8 * d : 8 * d + 4] + scattered[8 * d + 4 : 8 * d + 8]
        centre = jnp.sum(out[d], axis=0, keepdims=True)
        own_rows.append(both[0:1] - centre + waves[d : d + 1])
        one_rows.append(both[1:2])
        two_rows.append(both[2:3])
        three_rows.append(both[3:4])
    pad = [jnp.zeros((5, N), jnp.float32)]
    own_grad[...] = jnp.concatenate(own_rows + pad, axis=0)
    depth_of = [depth_after(step_x, step_y) for step_x, step_y in TABLE_DIRS]
    line = lane((8, N))
    ones = jnp.concatenate(one_rows + pad, axis=0)
    twos = jnp.concatenate(two_rows + pad, axis=0)
    threes = jnp.concatenate(three_rows + pad, axis=0)
    home_one = segments(line, depth_of[0:3])
    home_two = segments(line, depth_of[3:6])
    home_three = jnp.where(line < 64, depth_of[6], depth_of[7])
    for other in range(8):
        payload[other, 0:16, :] = up_piece
        payload[other, 16:40, :] = rest
        payload[other, 40:48, :] = pack_six(
            jnp.where(home_one == other, ones, 0.0), jnp.where(home_two == other, twos, 0.0)
        )
        payload[other, 48:56, :] = jnp.where(home_three == other, threes, 0.0)


TABLE_DIRS = ((1, 0), (1, 1), (1, -1), (-1, 0), (-1, 1), (-1, -1), (0, 1), (0, -1))


def segments(line, values):
    return jnp.where(line < 64, values[0], jnp.where(line < 96, values[1], values[2]))


def pack_six(one, two):
    return jnp.where(row_of((8, N)) < 4, one, pltpu.roll(two, 4, 0))


def depth_after(step_x, step_y):
    core, high = lax.axis_index("c"), lax.axis_index("zh")
    low, column = lax.axis_index("zl"), lax.axis_index("x")
    if step_x == 1:
        high = jnp.where(core == 1, (high + 1) % 4, high)
    if step_x == -1:
        high = jnp.where(core == 0, (high + 3) % 4, high)
    if step_y == 1:
        low = jnp.where(column == 3, 1 - low, low)
    if step_y == -1:
        low = jnp.where(column == 0, 1 - low, low)
    return high * 2 + low


def plane_after(step_x, step_y):
    core, high = lax.axis_index("c"), lax.axis_index("zh")
    row, column = lax.axis_index("y"), lax.axis_index("x")
    if step_x == 1:
        row = jnp.where((core == 1) & (high == 0), (row + 1) % 4, row)
    if step_x == -1:
        row = jnp.where((core == 0) & (high == 3), (row + 3) % 4, row)
    return row * 4 + (column + step_y + 4) % 4


def depth_sum_kernel(tiles, charge_piece, out):
    total = jnp.sum(tiles[...], axis=0)
    place_of = [plane_after(step_x, step_y) for step_x, step_y in TABLE_DIRS]
    line = lane((8, N))
    home = jnp.where(
        row_of((8, N)) < 4, segments(line, place_of[0:3]), segments(line, place_of[3:6])
    )
    home_three = jnp.where(line < 64, place_of[6], place_of[7])
    sixes, threes = total[40:48], total[48:56]
    row = lax.axis_index("y")
    quarter = charge_piece[0:4, :]
    for number in range(1, 4):
        quarter = jnp.where(row == number, charge_piece[4 * number : 4 * number + 4, :], quarter)
    for other in range(16):
        out[other, 0:40, :] = total[0:40]
        out[other, 40:48, :] = jnp.where(home == other, sixes, 0.0)
        out[other, 48:56, :] = jnp.where(home_three == other, threes, 0.0)
        out[other, 52:56, :] = quarter


def plane_sum_kernel(tiles, swap, threes):
    for column in range(4):
        total = tiles[column, 0:16, :]
        for row in range(1, 4):
            total = total + tiles[4 * row + column, 0:16, :]
        swap[16 * column : 16 * column + 16, :] = total
        for row in range(4):
            at = 96 + 16 * column + 4 * row
            swap[at : at + 4, :] = tiles[4 * row + column, 52:56, :]
    rest = tiles[0, 16:56, :]
    for other in range(1, 16):
        rest = rest + tiles[other, 16:56, :]
    swap[64:96, :] = rest[0:32]
    threes[...] = jnp.where(row_of((8, N)) < 4, rest[32:40], 0.0)


def finish_kernel(own, other, threes, own_grad, home, forces, grad_embed, grad_radial, grad_up,
                  grad_charge, grad_read):
    mean = 1.0 / ATOMS
    core = lax.axis_index("c")
    mine = pl.ds(pl.multiple_of(core * 64, 64), 64)
    theirs = pl.ds(pl.multiple_of((1 - core) * 64, 64), 64)
    grad_up[mine, :] = own[0:64, :] * mean
    grad_up[theirs, :] = other[0:64, :] * mean
    grad_charge[mine, :] = own[96:160, :] * mean
    grad_charge[theirs, :] = other[96:160, :] * mean
    total = (own[64:88, :] + other[64:88, :]) * mean
    grad_radial[0, :, :] = total[0:8]
    grad_radial[1, :, :] = total[8:16]
    grad_embed[...] = total[16:22]
    grad_read[...] = total[22:23]
    sixes = other[88:96, :]
    grad = own_grad[...]
    lane_rows = row_of((N, N))
    for number, piece in enumerate((sixes, pltpu.roll(sixes, 4, 0), threes[...])):
        onehot = jnp.where(lane_rows == home[number : number + 1, :], 1.0, 0.0)
        grad = grad + dot(piece, onehot, 1, 1)
    forces[...] = -grad[0:3, :]


def spread_kernel(*refs):
    out = refs[-1]
    core, column = lax.axis_index("c"), lax.axis_index("x")
    for number, pair in enumerate(refs[:-1]):
        for half in range(2):
            source = column ^ (2 * (number % 2) + half)
            member = jnp.where(number < 2, core, 1 - core) * 4 + source
            place = pl.ds(pl.multiple_of(member * SHARD, SHARD), SHARD)
            out[place, :] = pair[half * SHARD : (half + 1) * SHARD, :]


def structure_part(tiles, kvec, embed, w_up, wave_high, wave_low, feature_high, feature_low):
    me = lax.axis_index(GROUP)
    at = pl.multiple_of(me * SHARD, SHARD)
    rows = jnp.concatenate(
        [kvec[:, pl.ds(at, SHARD)], jnp.zeros((5, SHARD), jnp.float32)], axis=0
    )
    turns = jnp.transpose(rows * (1.0 / (2.0 * math.pi)))
    table = jnp.concatenate([embed[...], jnp.zeros((2, N), jnp.float32)], axis=0)
    up = split(w_up[...])
    for member, tile in enumerate(tiles):
        part = slice(member * N, (member + 1) * N)
        tail = tile[N : N + 8, :]
        onehot = (row_of((8, N)).astype(jnp.float32) == tail[3:4, :]).astype(jnp.float32)
        feature = exact_dot(onehot, table, 0, 0) + dot_three(split(tile[0:N, :]), up)
        high, low = split(feature)
        feature_high[part, :] = high
        feature_low[part, :] = low
        for chunk in range(SHARD // 64):
            waves = slice(chunk * 64, chunk * 64 + 64)
            angle = (
                turns[waves, 0:1] * tail[0:1, :]
                + turns[waves, 1:2] * tail[1:2, :]
                + turns[waves, 2:3] * tail[2:3, :]
            )
            angle = angle - jnp.round(angle)
            square = angle * angle
            cosine = jnp.full(square.shape, COS_POLY[-1], jnp.float32)
            for value in COS_POLY[-2::-1]:
                cosine = cosine * square + value
            sine = jnp.full(square.shape, SIN_POLY[-1], jnp.float32)
            for value in SIN_POLY[-2::-1]:
                sine = sine * square + value
            sine = sine * angle
            high, low = split(cosine)
            wave_high[waves, part] = high
            wave_low[waves, part] = low
            high, low = split(sine)
            waves = slice(SHARD + chunk * 64, SHARD + chunk * 64 + 64)
            wave_high[waves, part] = high
            wave_low[waves, part] = low
    return project(wave_high, wave_low, feature_high[...], feature_low[...])


def structure_mine_kernel(*refs):
    kvec, embed, w_up, factor, *part = refs[4:]
    factor[...] = structure_part(refs[:4], kvec, embed, w_up, *part)


def structure_other_kernel(*refs):
    kvec, embed, w_up, mine, factor, *part = refs[4:]
    total = mine[...] + structure_part(refs[:4], kvec, embed, w_up, *part)
    factor[...] = total.reshape(CROSSES, 16, N)


def whole(tiles):
    return jnp.concatenate([tile[0:N, :] for tile in tiles], axis=0)


def project(wave_high, wave_low, high, low):
    wide = half_dot(wave_high[...], jnp.concatenate([high, low], axis=1))
    return wide[:, 0:N] + wide[:, N:] + half_dot(wave_low[...], high)


def projection_mine_kernel(*refs):
    wave_high, wave_low, out = refs[4:]
    out[...] = project(wave_high, wave_low, *split(whole(refs[:4])))


def projection_other_kernel(*refs):
    wave_high, wave_low, mine, out = refs[4:]
    total = mine[...] + project(wave_high, wave_low, *split(whole(refs[:4])))
    out[...] = total.reshape(CROSSES, 16, N)


def sum_kernel(tiles, out):
    total = jnp.sum(tiles[...], axis=0)
    for other in range(out.shape[0]):
        out[other, :, :] = total


def filter_of(kfilter):
    me = lax.axis_index(GROUP)
    return kfilter[pl.ds(pl.multiple_of(me * SHARD, SHARD), SHARD), :] * SCALE


def core_sum_kernel(mine, other, *out):
    for number, ref in enumerate(out):
        ref[...] = mine[number] + other[number]


def core_sum_late_kernel(mine, late, other, *out):
    for number, ref in enumerate(out):
        ref[...] = mine[number] + other[number]
        ref[N : N + 8, :] = mine[number, N : N + 8, :] + (
            late[number] + other[number, N : N + 8, :]
        )


def field_rows(field):
    return jnp.concatenate(split(jnp.transpose(field)), axis=0)


def waves_to_atoms(rows, wave_high, wave_low):
    wide = half_dot(rows, wave_high[...])
    return wide[0:N] + wide[N:] + half_dot(rows[0:N], wave_low[...])


def to_tiles(total, out):
    for member in range(4):
        out[member, 0:N, :] = total[:, member * N : (member + 1) * N]


def potential_other_kernel(factor, w_charge, kfilter, wave_high, wave_low,
                           other, weighted, charge_factor, rows_out):
    scaled = filter_of(kfilter)
    charged = dot(factor[...], w_charge[...])
    charge_factor[...] = charged
    field = charged * jnp.concatenate([scaled, scaled], axis=0)
    weighted[...] = field
    rows = field_rows(field)
    rows_out[...] = rows
    to_tiles(waves_to_atoms(rows, wave_high, wave_low), other)


def potential_mine_kernel(rows, wave_high, wave_low, mine):
    to_tiles(waves_to_atoms(rows[...], wave_high, wave_low), mine)


def energy_kernel(tile_0, tile_1, tile_2, tile_3, feature_high, feature_low, read,
                  grad_out, result_out):
    total = tile_0[...] + tile_1[...] + tile_2[...] + tile_3[...]
    feature = feature_high[0:N, :].astype(jnp.float32) + feature_low[0:N, :].astype(jnp.float32)
    combined = feature + jnp.transpose(total)
    logistic = sigmoid(combined)
    result_out[...] = combined * logistic
    grad_out[...] = read[...] * (logistic * (1.0 + combined * (1.0 - logistic)))


def read_kernel(result, grad, active, read, energy, read_row, up_part):
    value = result[...]
    energy[...] = dot(jnp.broadcast_to(read[...], (8, N)), value, 1, 1)[0:1, :]
    read_row[...] = jnp.sum(value, axis=0, keepdims=True)
    up_part[...] = dot(active[...], grad[...], 0, 0)


def wave_trig(wave_high, wave_low):
    cosine = wave_high[0:SHARD, :].astype(jnp.float32) + wave_low[0:SHARD, :].astype(jnp.float32)
    sine = wave_high[SHARD:, :].astype(jnp.float32) + wave_low[SHARD:, :].astype(jnp.float32)
    return cosine, sine


def by_position(left, grads, feature_high, feature_low, kvec, wave_high, wave_low):
    grad_high, grad_low = split(whole(grads))
    along = dot_three(
        left,
        (
            jnp.concatenate([grad_high, feature_high[...]], axis=1),
            jnp.concatenate([grad_low, feature_low[...]], axis=1),
        ),
        1, 1,
    )
    cosine, sine = wave_trig(wave_high, wave_low)
    phase = cosine * along[SHARD:] - sine * along[0:SHARD]
    me = lax.axis_index(GROUP)
    rows = jnp.concatenate(
        [
            kvec[:, pl.ds(pl.multiple_of(me * SHARD, SHARD), SHARD)],
            jnp.zeros((5, SHARD), jnp.float32),
        ],
        axis=0,
    )
    return dot_three(split(rows), split(phase))


def wave_back_kernel(*refs):
    grads, shared = refs[:4], refs[4:12]
    (
        projected, factor, weighted, kfilter, kvec, mine_high, mine_low, wave_high, wave_low,
        feature_high, feature_low, w_charge, up_part,
        mine, other, left_high, left_low, up_grad, charge_grad,
    ) = refs[12:]
    scaled = filter_of(kfilter)
    field = projected[...] * jnp.concatenate([scaled, scaled], axis=0)
    pieces = split(field)
    rows = field_rows(field)
    mine_charge = waves_to_atoms(rows, mine_high, mine_low)
    other_charge = waves_to_atoms(rows, wave_high, wave_low)
    charge_grad[...] = dot_three(split(factor[...]), pieces, 0, 0)
    mix = dot(mine_charge, whole(shared[:4])) + dot(other_charge, whole(shared[4:]))
    weights = split(w_charge[...])
    up_grad[...] = dot_three(split(mix), weights, 0, 1) + up_part[...]
    left = split(
        jnp.concatenate([weighted[...], dot_three(pieces, weights, 1, 1)], axis=1)
    )
    left_high[...], left_low[...] = left
    by_pos = by_position(left, grads, feature_high, feature_low, kvec, wave_high, wave_low)
    to_tiles(mine_charge, mine)
    to_tiles(other_charge, other)
    core, column = lax.axis_index("c"), lax.axis_index("x")
    for member in range(MEMBERS):
        number = member % 4
        out = (mine, other)[member // 4].at[number]
        place = jnp.where(core == member // 4, 0, 4) + (column + 4 - number) % 4
        piece = pl.ds(pl.multiple_of(place * 16, 16), 16)
        if member < 4:
            out[N : N + 8, :] = jnp.zeros((8, N), jnp.float32)
        else:
            out[N : N + 8, :] = by_pos[:, number * N : (number + 1) * N]
        out[N + 8 : N + 24, :] = up_grad[piece, :]
        out[N + 24 : N + 40, :] = charge_grad[piece, :]


def wave_back_late_kernel(*refs):
    (
        left_high, left_low, projected, charge_factor, kvec, wave_high, wave_low,
        feature_high, feature_low, late, grad_filter,
    ) = refs[4:]
    mixed = charge_factor[...] * projected[...]
    grad_filter[...] = SCALE * (mixed[0:SHARD] + mixed[SHARD:])
    left = (left_high[...], left_low[...])
    by_pos = by_position(left, refs[:4], feature_high, feature_low, kvec, wave_high, wave_low)
    for member in range(4):
        late[member, :, :] = by_pos[:, member * N : (member + 1) * N]


def body(
    positions, species, neighbours, face_sends, corner_sends,
    embed, radial, w_up, w_charge, kvec, kfilter, read,
):
    near, far, own_x, home, positions, species, neighbours, embed, radial, read = call(
        pack_kernel,
        (f32(8, N),) * 3
        + (
            i32(8, N), f32(3, N), i32(1, N), i32(SLOTS, N), f32(KINDS, N), f32(2, BASIS, N),
            f32(1, N),
        ),
        positions, species.reshape(1, N), face_sends, corner_sends, neighbours, embed, radial,
        read.reshape(1, N),
        scratch=(
            pltpu.VMEM((4, N // 2), jnp.int32),
            pltpu.VMEM((4, N // 4), jnp.int32),
            pltpu.SemaphoreType.DMA((8,)),
        ),
        far=True,
    )
    near_y, far_y = swapped(near, GY, 0), swapped(far, GY, 1)
    near, far = call(relay_kernel, (f32(8, N),) * 2, own_x, near_y, far_y)
    near_x, far_x = swapped(near, GX, 0), swapped(far, GX, 1)
    shared, active, invariants, vectors, sums, edges, places = call(
        edge_kernel,
        (
            f32(N + 8, N), f32(N, N), f32(N, N), f32(3, N, N), f32(4, KINDS * BASIS, N),
            f32(7, SLOTS, N), i32(2, SLOTS, N),
        ),
        positions, species, neighbours, near_x, far_x, near_y, far_y, embed, radial,
    )
    swap = [(0, 1), (1, 0)]

    def other_core(value):
        return lax.ppermute(value, "c", swap)

    def step_x(value, step):
        return lax.ppermute(value, "x", [(at, (at + step) % 4) for at in range(4)])

    def gather(value):
        values = [value] + [step_x(value, step) for step in (1, 2, 3)]
        return values + [other_core(item) for item in values]

    def scatter(kernel, parts, other):
        shape = f32(*other.shape[1:])
        tiles = call(kernel, (shape,) * 4, *parts, other_core(other))
        return [tiles[0]] + [step_x(tiles[step], -step) for step in (1, 2, 3)]

    shared = gather(shared)
    half = jax.ShapeDtypeStruct((2 * SHARD, 4 * N), jnp.bfloat16)
    feature = jax.ShapeDtypeStruct((4 * N, N), jnp.bfloat16)
    part = (half, half, feature, feature)
    both = f32(2 * SHARD, N)
    factor, *mine_part = call(
        structure_mine_kernel, (both,) + part, *shared[:4], kvec, embed, w_up
    )
    factor, *other_part = call(
        structure_other_kernel, (f32(CROSSES, 16, N),) + part, *shared[4:], kvec, embed, w_up,
        factor,
    )
    mine_waves, mine_features = mine_part[:2], mine_part[2:]
    other_waves, other_features = other_part[:2], other_part[2:]

    def cross_sum(tiles):
        tiles = lax.all_to_all(tiles, CROSS, 0, 0)
        tiles = call(sum_kernel, f32(CROSSES, 16, N), tiles)
        return lax.all_to_all(tiles, CROSS, 0, 0).reshape(2 * SHARD, N)

    factor = cross_sum(factor)
    rows = jax.ShapeDtypeStruct((2 * N, 2 * SHARD), jnp.bfloat16)
    other, weighted, charge_factor, rows = call(
        potential_other_kernel, (f32(4, N, N), both, both, rows),
        factor, w_charge, kfilter, *other_waves,
    )
    mine = call(potential_mine_kernel, f32(4, N, N), rows, *mine_waves)
    grad_out, result = call(
        energy_kernel, (f32(N, N),) * 2,
        *scatter(core_sum_kernel, (mine,), other), *mine_features, read,
    )
    grads = gather(grad_out)
    energy, read_row, up_part = call(
        read_kernel, (f32(1, N), f32(1, N), f32(N, N)), result, grad_out, active, read
    )
    projected = call(projection_mine_kernel, both, *grads[:4], *mine_waves)
    *others, energy, read_row, up_part = lax.optimization_barrier(
        (*grads[4:], energy, read_row, up_part)
    )
    projected = cross_sum(
        call(projection_other_kernel, f32(CROSSES, 16, N), *others, *other_waves, projected)
    )
    square = pltpu.VMEM((N, N), jnp.float32)
    left = jax.ShapeDtypeStruct((2 * SHARD, 2 * N), jnp.bfloat16)
    mine, other, *left = call(
        wave_back_kernel,
        (f32(4, N + 40, N), f32(4, N + 40, N), left, left),
        *others, *shared, projected, factor, weighted, kfilter, kvec, *mine_waves,
        *other_waves, *other_features, w_charge, up_part,
        scratch=(square, square),
    )
    late, shard = call(
        wave_back_late_kernel, (f32(4, 8, N), f32(SHARD, N)),
        *grads[:4], *left, projected, charge_factor, kvec, *mine_waves, *mine_features,
    )
    tiles = scatter(core_sum_late_kernel, (mine, late), other)
    shard, *tiles = lax.optimization_barrier((shard, *tiles))
    next_shard = lax.ppermute(shard, "x", [(at, at ^ 1) for at in range(4)])
    payload, own_grad, charge_piece = call(
        edge_back_kernel,
        (f32(8, 56, N), f32(8, N), f32(16, N)),
        *tiles, active, invariants, vectors, sums, edges, places, embed, radial, w_up,
        w_charge, species, grad_out, read_row,
        cost=pl.CostEstimate(flops=10**9, bytes_accessed=10**7, transcendentals=10**5),
    )
    payload, next_shard = lax.optimization_barrier((payload, next_shard))
    near_shards = jnp.concatenate([shard, next_shard], axis=0)
    far_shards = lax.ppermute(near_shards, "x", [(at, at ^ 2) for at in range(4)])
    payload = lax.all_to_all(payload, DEPTH, 0, 0)
    payload = call(depth_sum_kernel, f32(16, 56, N), payload, charge_piece)
    payload = lax.all_to_all(payload, PLANE, 0, 0)
    payload, threes = call(plane_sum_kernel, (f32(160, N), f32(8, N)), payload)
    shards = [near_shards, far_shards, other_core(near_shards), other_core(far_shards)]
    payload_other = other_core(payload)
    grad_filter = call(spread_kernel, f32(WAVES, N), *shards)
    forces, grad_embed, grad_radial, grad_up, grad_charge, grad_read = call(
        finish_kernel,
        (f32(3, N), f32(KINDS, N), f32(2, BASIS, N), f32(N, N), f32(N, N), f32(1, N)),
        payload, payload_other, threes, own_grad, home,
    )
    return (
        energy.reshape(N), forces, grad_embed, grad_radial, grad_up, grad_charge, grad_filter,
        grad_read.reshape(N),
    )


def solution(mesh):
    fine = Mesh(mesh.devices.reshape(4, 4, 2, 2, 4), ALL)
    atoms = P(ALL)
    rows = P(None, ALL)
    return jax.shard_map(
        body,
        mesh=fine,
        in_specs=(rows, atoms, rows, rows, rows) + (P(),) * 7,
        out_specs=(atoms, rows) + (P(),) * 6,
        check_vma=False,
    )
```

```python
import functools
import math

import jax
import jax.numpy as jnp
from jax import lax
from jax.experimental import pallas as pl
from jax.experimental.pallas import tpu as pltpu
from jax.sharding import Mesh
from jax.sharding import PartitionSpec as P

CUTOFF = 5.0
SOFTEN = 0.01
WIDTH_GAUSS = 2.0
DOMAIN = 8.8
N = 128
SLOTS = 64
KINDS = 6
BASIS = 8
WAVES = 2048
ATOMS = 32768
SHARD = 256
HIGHEST = lax.Precision.HIGHEST
SCALE = 1.0 / math.sqrt(ATOMS * WAVES)

GX = ("y", "zh", "c")
GY = ("zl", "x")
ALL = GX + GY
GROUP = ("c", "x")
CROSS = ("y", "zh", "zl")
MEMBERS = 8
CROSSES = 32
DEPTH = ("zh", "zl")
PLANE = ("y", "x")

COS_POLY = (
    0.999999989059021,
    -19.73920449945393,
    64.93911745989678,
    -85.45013953089901,
    60.16763095102345,
    -25.96759924855853,
    6.528658161204758,
)
SIN_POLY = (
    6.283184916495438,
    -41.34158923268875,
    81.59994332978647,
    -76.61447253128671,
    41.34288235472546,
    -12.471243535272281,
)


def dims(left, right):
    return (((left,), (right,)), ((), ()))


def exact_dot(left, right, left_dim=1, right_dim=0):
    return lax.dot_general(
        left,
        right,
        dims(left_dim, right_dim),
        precision=HIGHEST,
        preferred_element_type=jnp.float32,
    )


def half_dot(left, right, left_dim=1, right_dim=0):
    return lax.dot_general(
        left, right, dims(left_dim, right_dim), preferred_element_type=jnp.float32
    )


def split(value):
    high = value.astype(jnp.bfloat16)
    return high, (value - high.astype(jnp.float32)).astype(jnp.bfloat16)


def dot_three(left, right, left_dim=1, right_dim=0):
    left_high, left_low = left
    right_high, right_low = right
    return (
        half_dot(left_high, right_high, left_dim, right_dim)
        + half_dot(left_high, right_low, left_dim, right_dim)
        + half_dot(left_low, right_high, left_dim, right_dim)
    )


def dot(left, right, left_dim=1, right_dim=0):
    return dot_three(split(left), split(right), left_dim, right_dim)


def sigmoid(value):
    return 1.0 / (1.0 + jnp.exp(-value))


def lane(shape):
    return lax.broadcasted_iota(jnp.int32, shape, 1)


def row_of(shape):
    return lax.broadcasted_iota(jnp.int32, shape, 0)


def call(kernel, out_shape, *args, scratch=(), vmem=32, far=False, cost=None):
    more = {}
    if far:
        more["in_specs"] = [pl.BlockSpec(memory_space=pltpu.HBM)] * len(args)
        args = [pltpu.with_memory_space_constraint(value, pltpu.HBM) for value in args]
    return pl.pallas_call(
        kernel,
        out_shape=out_shape,
        scratch_shapes=list(scratch),
        cost_estimate=cost,
        **more,
        compiler_params=pltpu.CompilerParams(vmem_limit_bytes=vmem * 1024 * 1024),
    )(*args)


def f32(*shape):
    return jax.ShapeDtypeStruct(shape, jnp.float32)


def i32(*shape):
    return jax.ShapeDtypeStruct(shape, jnp.int32)


def take(row, index):
    return jnp.take_along_axis(
        jnp.broadcast_to(row, index.shape), index, axis=1, mode="promise_in_bounds"
    )


def joined(face, corner, faces, corners):
    return jnp.concatenate(
        [face[f : f + 1, :] for f in faces] + [corner[f : f + 1, :] for f in corners], axis=1
    )


def pack_kernel(pos_in, species_in, face_in, corner_in, nbr_in, embed_in, radial_in, read_in,
                near, far, own, home, pos, species, nbr, embed, radial, read, face, corner, sems):
    pairs = (
        (pos_in, pos), (species_in, species), (face_in, face), (corner_in, corner),
        (nbr_in, nbr), (embed_in, embed), (radial_in, radial), (read_in, read),
    )
    copies = [
        pltpu.make_async_copy(source, target, sems.at[number])
        for number, (source, target) in enumerate(pairs)
    ]
    for copy in copies:
        copy.start()
    for copy in copies:
        copy.wait()
    even = lax.axis_index("x") % 2 == 0
    rows = [pos[0:1, :], pos[1:2, :], pos[2:3, :], species[...].astype(jnp.float32)]
    padding = jnp.zeros((5, N), jnp.int32)
    where_from = jnp.concatenate(
        [
            joined(face, corner, (2,), (0, 2)),
            joined(face, corner, (3,), (1, 3)),
            joined(face, corner, (0, 1), ()),
            padding,
        ],
        axis=0,
    )
    home[...] = jnp.concatenate(
        [
            joined(face, corner, (0,), (0, 1)),
            joined(face, corner, (1,), (2, 3)),
            joined(face, corner, (2, 3), ()),
            padding,
        ],
        axis=0,
    )
    for number, row in enumerate(rows):
        got = take(row, where_from)
        near[number : number + 1, :] = jnp.where(even, got[1:2, :], got[0:1, :])
        far[number : number + 1, :] = jnp.where(even, got[0:1, :], got[1:2, :])
        own[number : number + 1, :] = got[2:3, :]
    zero = jnp.zeros((4, N), jnp.float32)
    near[4:8, :] = zero
    far[4:8, :] = zero
    own[4:8, :] = zero


def swapped(value, axes, odd):
    count = math.prod(lax.axis_size(axis) for axis in axes)
    places = [(at, ((((at + odd) % count) ^ 1) - odd) % count) for at in range(count)]
    return lax.ppermute(value, axes, places)


def relay_kernel(own, near, far, one, two):
    at = lane((8, N))
    even = lax.axis_index("x") % 2 == 0
    a = own[...]
    b = jnp.where(even, near[...], far[...])
    d = jnp.where(even, far[...], near[...])
    to_minus = jnp.where(at < 64, a, jnp.where(at < 96, b, pltpu.roll(d, 32, 1)))
    to_plus = jnp.where(
        at < 64, pltpu.roll(a, 64, 1), jnp.where(at < 96, pltpu.roll(b, 96, 1), d)
    )
    first = lax.axis_index("c") == 0
    one[...] = jnp.where(first, to_plus, to_minus)
    two[...] = jnp.where(first, to_minus, to_plus)


def pair_weights(embed, radial):
    scalar, vector = [], []
    for kind in range(KINDS):
        row = embed[kind : kind + 1, :]
        scalar.append(radial[0] * row * 0.25)
        vector.append(radial[1] * row * 0.05)
    return jnp.concatenate(scalar, axis=0), jnp.concatenate(vector, axis=0)


def basis_centers():
    return row_of((BASIS, N)).astype(jnp.float32) * (CUTOFF / (BASIS - 1))


def edge_kernel(
    pos, species, nbr, near_x, far_x, near_y, far_y, embed, radial,
    shared, active, invariants, vectors, sums, edges, places,
):
    at = lane((8, N))
    own = [pos[0:1, :], pos[1:2, :], pos[2:3, :], species[...].astype(jnp.float32)]
    core_zero = lax.axis_index("c") == 0
    even = lax.axis_index("x") % 2 == 0
    first = jnp.where(core_zero, near_x[...], far_x[...])
    second = jnp.where(core_zero, far_x[...], near_x[...])
    plus_y = jnp.where(even, near_y[...], far_y[...])
    minus_y = jnp.where(even, far_y[...], near_y[...])
    third = jnp.where(at < 64, plus_y, pltpu.roll(minus_y, 64, 1))
    line = lane((1, N))
    corner_y = jnp.where(line < 64, 0.0, jnp.where(line < 96, DOMAIN, -DOMAIN))
    tables = [
        own,
        [first[0:1] + DOMAIN, first[1:2] + corner_y, first[2:3], first[3:4]],
        [second[0:1] - DOMAIN, second[1:2] + corner_y, second[2:3], second[3:4]],
        [third[0:1], third[1:2] + jnp.where(line < 64, DOMAIN, -DOMAIN), third[2:3], third[3:4]],
    ]
    for group in range(SLOTS // 8):
        rows = slice(8 * group, 8 * group + 8)
        slot = nbr[rows, :]
        block = lax.shift_right_logical(slot, 6)
        table = jnp.where(
            block < 2,
            0,
            jnp.where(
                (block == 4) | (block == 5), 3, jnp.where((block & 1) == 0, 1, 2)
            ),
        )
        table = jnp.where(block == 8, 4, table)
        half = jnp.where((block == 1) | ((block >= 5) & (block < 8)), 64, 0)
        place = (slot & 63) + half
        found = []
        for number in range(4):
            value = take(tables[0][number], place)
            for other in range(1, 4):
                value = jnp.where(table == other, take(tables[other][number], place), value)
            found.append(value)
        offset = [found[d] - own[d] for d in range(3)]
        dist_sq = offset[0] * offset[0] + offset[1] * offset[1] + offset[2] * offset[2]
        valid = (table < 4).astype(jnp.float32)
        ramp = jnp.maximum(1.0 - dist_sq / (CUTOFF * CUTOFF), 0.0)
        edges[0, rows, :] = offset[0]
        edges[1, rows, :] = offset[1]
        edges[2, rows, :] = offset[2]
        edges[3, rows, :] = found[3]
        edges[4, rows, :] = jnp.sqrt(dist_sq + SOFTEN)
        edges[5, rows, :] = ramp * ramp * valid
        edges[6, rows, :] = (-2.0 / (CUTOFF * CUTOFF)) * ramp * valid
        places[0, rows, :] = table
        places[1, rows, :] = place
    centers = basis_centers()

    def step(slot, carry):
        row = pl.ds(slot, 1)
        away = edges[4, row, :] - centers
        basis = jnp.exp(-WIDTH_GAUSS * away * away) * edges[5, row, :]
        parts = [basis] + [basis * edges[d, row, :] for d in range(3)]
        kind_row = jnp.broadcast_to(edges[3, row, :], (BASIS, N))
        out = []
        for kind in range(KINDS):
            mask = kind_row == float(kind)
            for number in range(4):
                out.append(carry[4 * kind + number] + jnp.where(mask, parts[number], 0.0))
        return tuple(out)

    zero = jnp.zeros((BASIS, N), jnp.float32)
    total = lax.fori_loop(0, SLOTS, step, (zero,) * (4 * KINDS), unroll=16)
    for number in range(4):
        sums[number, :, :] = jnp.concatenate(
            [total[4 * kind + number] for kind in range(KINDS)], axis=0
        )
    scalar_w, vector_w = pair_weights(embed, radial)
    value = dot(sums[0], scalar_w, 0, 0)
    for d in range(3):
        vector = dot(sums[1 + d], vector_w, 0, 0)
        vectors[d, :, :] = vector
        value = value + vector * vector
    invariants[...] = value
    result = value * sigmoid(value)
    active[...] = result
    anchor_x = lax.convert_element_type(lax.axis_index(GX), jnp.float32) * DOMAIN
    anchor_y = lax.convert_element_type(lax.axis_index(GY), jnp.float32) * DOMAIN
    zero_row = jnp.zeros((1, N), jnp.float32)
    tail = jnp.concatenate(
        [own[0] + anchor_x, own[1] + anchor_y, own[2], own[3]] + [zero_row] * 4, axis=0
    )
    shared[0:N, :] = result
    shared[N : N + 8, :] = tail


def edge_back_kernel(
    tile_0, tile_1, tile_2, tile_3, active, invariants, vectors, sums, edges, places, embed, radial, w_up, w_charge,
    species, grad_out, read_row,
    payload, own_grad, charge_piece,
):
    total = tile_0[...] + tile_1[...] + tile_2[...] + tile_3[...]
    grad_charges = jnp.transpose(total[0:N, :])
    updated = grad_out[...] + dot(grad_charges, w_charge[...], 1, 1)
    value = invariants[...]
    logistic = sigmoid(value)
    slope = logistic * (1.0 + value * (1.0 - logistic))
    grad_inv = dot(updated, w_up[...], 1, 1) * slope
    scalar_w, vector_w = pair_weights(embed, radial)
    pulls = [dot(scalar_w, grad_inv, 1, 1)]
    grad_scalar = dot(sums[0], grad_inv)
    grad_vector = jnp.zeros((KINDS * BASIS, N), jnp.float32)
    for d in range(3):
        along = 2.0 * vectors[d] * grad_inv
        pulls.append(dot(vector_w, along, 1, 1))
        grad_vector = grad_vector + dot(sums[1 + d], along)
    onehot = (row_of((8, N)) == species[...]).astype(jnp.float32)
    grad_table = dot(onehot, updated)
    radial_zero = jnp.zeros((BASIS, N), jnp.float32)
    radial_one = jnp.zeros((BASIS, N), jnp.float32)
    table_rows = []
    for kind in range(KINDS):
        rows = slice(kind * BASIS, (kind + 1) * BASIS)
        row = embed[kind : kind + 1, :]
        part_zero, part_one = grad_scalar[rows] * 0.25, grad_vector[rows] * 0.05
        radial_zero = radial_zero + part_zero * row
        radial_one = radial_one + part_one * row
        table_rows.append(
            grad_table[kind : kind + 1]
            + jnp.sum(radial[0] * part_zero + radial[1] * part_one, axis=0, keepdims=True)
        )
    rest = jnp.concatenate(
        [radial_zero, radial_one] + table_rows + [read_row[...], jnp.zeros((1, N), jnp.float32)],
        axis=0,
    )
    up_piece = total[N + 8 : N + 24, :]
    charge_piece[...] = total[N + 24 : N + 40, :]
    centers = basis_centers()
    sub = row_of((8, N))
    sub_table = sub & 3
    high_rows = sub < 4
    lane_rows = row_of((N, N))
    pull = [
        [pulls[number][kind * BASIS : (kind + 1) * BASIS] for number in range(4)]
        for kind in range(KINDS)
    ]

    def one(slot):
        row = pl.ds(slot, 1)
        kind_row = jnp.broadcast_to(edges[3, row, :], (BASIS, N))
        own_pull = list(pull[KINDS - 1])
        for kind in range(KINDS - 1):
            mask = kind_row == float(kind)
            own_pull = [jnp.where(mask, pull[kind][n], own_pull[n]) for n in range(4)]
        radius = edges[4, row, :]
        envelope = edges[5, row, :]
        away = radius - centers
        bell = jnp.exp(-WIDTH_GAUSS * away * away)
        offset = [jnp.broadcast_to(edges[d, row, :], (BASIS, N)) for d in range(3)]
        by_basis = own_pull[0]
        for d in range(3):
            by_basis = by_basis + offset[d] * own_pull[1 + d]
        by_square = by_basis * bell * (edges[6, row, :] - (2.0 * envelope / radius) * away)
        basis = bell * envelope
        table = jnp.broadcast_to(places[0, row, :], (8, N)) == sub_table
        place = lane_rows == places[1, row, :]
        onehot = jnp.where(place, 1.0, 0.0).astype(jnp.bfloat16)
        parts, pieces = [], []
        for d in range(3):
            part = basis * own_pull[1 + d] + 2.0 * offset[d] * by_square
            parts.append(part)
            whole = jnp.broadcast_to(jnp.sum(part, axis=0, keepdims=True), (8, N))
            high = whole.astype(jnp.bfloat16).astype(jnp.float32)
            pieces.append(jnp.where(table, jnp.where(high_rows, high, whole - high), 0.0))
        return parts, jnp.concatenate(pieces, axis=0).astype(jnp.bfloat16), onehot

    def step(group, carry):
        found = [one(group * 8 + number) for number in range(8)]
        centre = list(carry[:3])
        for parts, _, _ in found:
            centre = [centre[d] + parts[d] for d in range(3)]
        rows = jnp.concatenate([item[1] for item in found], axis=1)
        onehot = jnp.concatenate([item[2] for item in found], axis=1)
        return (*centre, carry[3] + half_dot(rows, onehot, 1, 1))

    zero = jnp.zeros((8, N), jnp.float32)
    out = (zero, zero, zero, jnp.zeros((24, N), jnp.float32))
    for group in range(SLOTS // 8):
        out = step(group, out)
    scattered = out[3]
    waves = total[N : N + 8, :]
    own_rows, one_rows, two_rows, three_rows = [], [], [], []
    for d in range(3):
        both = scattered[8 * d : 8 * d + 4] + scattered[8 * d + 4 : 8 * d + 8]
        centre = jnp.sum(out[d], axis=0, keepdims=True)
        own_rows.append(both[0:1] - centre + waves[d : d + 1])
        one_rows.append(both[1:2])
        two_rows.append(both[2:3])
        three_rows.append(both[3:4])
    pad = [jnp.zeros((5, N), jnp.float32)]
    own_grad[...] = jnp.concatenate(own_rows + pad, axis=0)
    depth_of = [depth_after(step_x, step_y) for step_x, step_y in TABLE_DIRS]
    line = lane((8, N))
    ones = jnp.concatenate(one_rows + pad, axis=0)
    twos = jnp.concatenate(two_rows + pad, axis=0)
    threes = jnp.concatenate(three_rows + pad, axis=0)
    home_one = segments(line, depth_of[0:3])
    home_two = segments(line, depth_of[3:6])
    home_three = jnp.where(line < 64, depth_of[6], depth_of[7])
    for other in range(8):
        payload[other, 0:16, :] = up_piece
        payload[other, 16:40, :] = rest
        payload[other, 40:48, :] = pack_six(
            jnp.where(home_one == other, ones, 0.0), jnp.where(home_two == other, twos, 0.0)
        )
        payload[other, 48:56, :] = jnp.where(home_three == other, threes, 0.0)


TABLE_DIRS = ((1, 0), (1, 1), (1, -1), (-1, 0), (-1, 1), (-1, -1), (0, 1), (0, -1))


def segments(line, values):
    return jnp.where(line < 64, values[0], jnp.where(line < 96, values[1], values[2]))


def pack_six(one, two):
    return jnp.where(row_of((8, N)) < 4, one, pltpu.roll(two, 4, 0))


def depth_after(step_x, step_y):
    core, high = lax.axis_index("c"), lax.axis_index("zh")
    low, column = lax.axis_index("zl"), lax.axis_index("x")
    if step_x == 1:
        high = jnp.where(core == 1, (high + 1) % 4, high)
    if step_x == -1:
        high = jnp.where(core == 0, (high + 3) % 4, high)
    if step_y == 1:
        low = jnp.where(column == 3, 1 - low, low)
    if step_y == -1:
        low = jnp.where(column == 0, 1 - low, low)
    return high * 2 + low


def plane_after(step_x, step_y):
    core, high = lax.axis_index("c"), lax.axis_index("zh")
    row, column = lax.axis_index("y"), lax.axis_index("x")
    if step_x == 1:
        row = jnp.where((core == 1) & (high == 0), (row + 1) % 4, row)
    if step_x == -1:
        row = jnp.where((core == 0) & (high == 3), (row + 3) % 4, row)
    return row * 4 + (column + step_y + 4) % 4


def depth_sum_kernel(tiles, charge_piece, out):
    total = jnp.sum(tiles[...], axis=0)
    place_of = [plane_after(step_x, step_y) for step_x, step_y in TABLE_DIRS]
    line = lane((8, N))
    home = jnp.where(
        row_of((8, N)) < 4, segments(line, place_of[0:3]), segments(line, place_of[3:6])
    )
    home_three = jnp.where(line < 64, place_of[6], place_of[7])
    sixes, threes = total[40:48], total[48:56]
    row = lax.axis_index("y")
    quarter = charge_piece[0:4, :]
    for number in range(1, 4):
        quarter = jnp.where(row == number, charge_piece[4 * number : 4 * number + 4, :], quarter)
    for other in range(16):
        out[other, 0:40, :] = total[0:40]
        out[other, 40:48, :] = jnp.where(home == other, sixes, 0.0)
        out[other, 48:56, :] = jnp.where(home_three == other, threes, 0.0)
        out[other, 52:56, :] = quarter


def plane_sum_kernel(tiles, swap, threes):
    for column in range(4):
        total = tiles[column, 0:16, :]
        for row in range(1, 4):
            total = total + tiles[4 * row + column, 0:16, :]
        swap[16 * column : 16 * column + 16, :] = total
        for row in range(4):
            at = 96 + 16 * column + 4 * row
            swap[at : at + 4, :] = tiles[4 * row + column, 52:56, :]
    rest = tiles[0, 16:56, :]
    for other in range(1, 16):
        rest = rest + tiles[other, 16:56, :]
    swap[64:96, :] = rest[0:32]
    threes[...] = jnp.where(row_of((8, N)) < 4, rest[32:40], 0.0)


def finish_kernel(own, other, threes, own_grad, home, forces, grad_embed, grad_radial, grad_up,
                  grad_charge, grad_read):
    mean = 1.0 / ATOMS
    core = lax.axis_index("c")
    mine = pl.ds(pl.multiple_of(core * 64, 64), 64)
    theirs = pl.ds(pl.multiple_of((1 - core) * 64, 64), 64)
    grad_up[mine, :] = own[0:64, :] * mean
    grad_up[theirs, :] = other[0:64, :] * mean
    grad_charge[mine, :] = own[96:160, :] * mean
    grad_charge[theirs, :] = other[96:160, :] * mean
    total = (own[64:88, :] + other[64:88, :]) * mean
    grad_radial[0, :, :] = total[0:8]
    grad_radial[1, :, :] = total[8:16]
    grad_embed[...] = total[16:22]
    grad_read[...] = total[22:23]
    sixes = other[88:96, :]
    grad = own_grad[...]
    lane_rows = row_of((N, N))
    for number, piece in enumerate((sixes, pltpu.roll(sixes, 4, 0), threes[...])):
        onehot = jnp.where(lane_rows == home[number : number + 1, :], 1.0, 0.0)
        grad = grad + dot(piece, onehot, 1, 1)
    forces[...] = -grad[0:3, :]


def spread_kernel(*refs):
    out = refs[-1]
    core, column = lax.axis_index("c"), lax.axis_index("x")
    for number, pair in enumerate(refs[:-1]):
        for half in range(2):
            source = column ^ (2 * (number % 2) + half)
            member = jnp.where(number < 2, core, 1 - core) * 4 + source
            place = pl.ds(pl.multiple_of(member * SHARD, SHARD), SHARD)
            out[place, :] = pair[half * SHARD : (half + 1) * SHARD, :]


def structure_part(tiles, kvec, embed, w_up, wave_high, wave_low, feature_high, feature_low):
    me = lax.axis_index(GROUP)
    at = pl.multiple_of(me * SHARD, SHARD)
    rows = jnp.concatenate(
        [kvec[:, pl.ds(at, SHARD)], jnp.zeros((5, SHARD), jnp.float32)], axis=0
    )
    turns = jnp.transpose(rows * (1.0 / (2.0 * math.pi)))
    table = jnp.concatenate([embed[...], jnp.zeros((2, N), jnp.float32)], axis=0)
    up = split(w_up[...])
    for member, tile in enumerate(tiles):
        part = slice(member * N, (member + 1) * N)
        tail = tile[N : N + 8, :]
        onehot = (row_of((8, N)).astype(jnp.float32) == tail[3:4, :]).astype(jnp.float32)
        feature = exact_dot(onehot, table, 0, 0) + dot_three(split(tile[0:N, :]), up)
        high, low = split(feature)
        feature_high[part, :] = high
        feature_low[part, :] = low
        for chunk in range(SHARD // 64):
            waves = slice(chunk * 64, chunk * 64 + 64)
            angle = (
                turns[waves, 0:1] * tail[0:1, :]
                + turns[waves, 1:2] * tail[1:2, :]
                + turns[waves, 2:3] * tail[2:3, :]
            )
            angle = angle - jnp.round(angle)
            square = angle * angle
            cosine = jnp.full(square.shape, COS_POLY[-1], jnp.float32)
            for value in COS_POLY[-2::-1]:
                cosine = cosine * square + value
            sine = jnp.full(square.shape, SIN_POLY[-1], jnp.float32)
            for value in SIN_POLY[-2::-1]:
                sine = sine * square + value
            sine = sine * angle
            high, low = split(cosine)
            wave_high[waves, part] = high
            wave_low[waves, part] = low
            high, low = split(sine)
            waves = slice(SHARD + chunk * 64, SHARD + chunk * 64 + 64)
            wave_high[waves, part] = high
            wave_low[waves, part] = low
    return project(wave_high, wave_low, feature_high[...], feature_low[...])


def structure_mine_kernel(*refs):
    kvec, embed, w_up, factor, *part = refs[4:]
    factor[...] = structure_part(refs[:4], kvec, embed, w_up, *part)


def structure_other_kernel(*refs):
    kvec, embed, w_up, mine, factor, *part = refs[4:]
    total = mine[...] + structure_part(refs[:4], kvec, embed, w_up, *part)
    factor[...] = total.reshape(CROSSES, 16, N)


def whole(tiles):
    return jnp.concatenate([tile[0:N, :] for tile in tiles], axis=0)


def project(wave_high, wave_low, high, low):
    wide = half_dot(wave_high[...], jnp.concatenate([high, low], axis=1))
    return wide[:, 0:N] + wide[:, N:] + half_dot(wave_low[...], high)


def projection_mine_kernel(*refs):
    wave_high, wave_low, out = refs[4:]
    out[...] = project(wave_high, wave_low, *split(whole(refs[:4])))


def projection_other_kernel(*refs):
    wave_high, wave_low, mine, out = refs[4:]
    total = mine[...] + project(wave_high, wave_low, *split(whole(refs[:4])))
    out[...] = total.reshape(CROSSES, 16, N)


def sum_kernel(tiles, out):
    total = jnp.sum(tiles[...], axis=0)
    for other in range(out.shape[0]):
        out[other, :, :] = total


def filter_of(kfilter):
    me = lax.axis_index(GROUP)
    return kfilter[pl.ds(pl.multiple_of(me * SHARD, SHARD), SHARD), :] * SCALE


def core_sum_kernel(mine, other, *out):
    for number, ref in enumerate(out):
        ref[...] = mine[number] + other[number]


def core_sum_late_kernel(mine, late, other, *out):
    for number, ref in enumerate(out):
        ref[...] = mine[number] + other[number]
        ref[N : N + 8, :] = mine[number, N : N + 8, :] + (
            late[number] + other[number, N : N + 8, :]
        )


def field_rows(field):
    return jnp.concatenate(split(jnp.transpose(field)), axis=0)


def waves_to_atoms(rows, wave_high, wave_low):
    wide = half_dot(rows, wave_high[...])
    return wide[0:N] + wide[N:] + half_dot(rows[0:N], wave_low[...])


def to_tiles(total, out):
    for member in range(4):
        out[member, 0:N, :] = total[:, member * N : (member + 1) * N]


def potential_other_kernel(factor, w_charge, kfilter, wave_high, wave_low,
                           other, weighted, charge_factor, rows_out):
    scaled = filter_of(kfilter)
    charged = dot(factor[...], w_charge[...])
    charge_factor[...] = charged
    field = charged * jnp.concatenate([scaled, scaled], axis=0)
    weighted[...] = field
    rows = field_rows(field)
    rows_out[...] = rows
    to_tiles(waves_to_atoms(rows, wave_high, wave_low), other)


def potential_mine_kernel(rows, wave_high, wave_low, mine):
    to_tiles(waves_to_atoms(rows[...], wave_high, wave_low), mine)


def energy_kernel(tile_0, tile_1, tile_2, tile_3, feature_high, feature_low, read,
                  grad_out, result_out):
    total = tile_0[...] + tile_1[...] + tile_2[...] + tile_3[...]
    feature = feature_high[0:N, :].astype(jnp.float32) + feature_low[0:N, :].astype(jnp.float32)
    combined = feature + jnp.transpose(total)
    logistic = sigmoid(combined)
    result_out[...] = combined * logistic
    grad_out[...] = read[...] * (logistic * (1.0 + combined * (1.0 - logistic)))


def read_kernel(result, grad, active, read, energy, read_row, up_part):
    value = result[...]
    energy[...] = dot(jnp.broadcast_to(read[...], (8, N)), value, 1, 1)[0:1, :]
    read_row[...] = jnp.sum(value, axis=0, keepdims=True)
    up_part[...] = dot(active[...], grad[...], 0, 0)


def wave_trig(wave_high, wave_low):
    cosine = wave_high[0:SHARD, :].astype(jnp.float32) + wave_low[0:SHARD, :].astype(jnp.float32)
    sine = wave_high[SHARD:, :].astype(jnp.float32) + wave_low[SHARD:, :].astype(jnp.float32)
    return cosine, sine


def by_position(left, grads, feature_high, feature_low, kvec, wave_high, wave_low):
    grad_high, grad_low = split(whole(grads))
    along = dot_three(
        left,
        (
            jnp.concatenate([grad_high, feature_high[...]], axis=1),
            jnp.concatenate([grad_low, feature_low[...]], axis=1),
        ),
        1, 1,
    )
    cosine, sine = wave_trig(wave_high, wave_low)
    phase = cosine * along[SHARD:] - sine * along[0:SHARD]
    me = lax.axis_index(GROUP)
    rows = jnp.concatenate(
        [
            kvec[:, pl.ds(pl.multiple_of(me * SHARD, SHARD), SHARD)],
            jnp.zeros((5, SHARD), jnp.float32),
        ],
        axis=0,
    )
    return dot_three(split(rows), split(phase))


def wave_back_kernel(*refs):
    grads, shared = refs[:4], refs[4:12]
    (
        projected, factor, weighted, kfilter, kvec, mine_high, mine_low, wave_high, wave_low,
        feature_high, feature_low, w_charge, up_part,
        mine, other, left_high, left_low, up_grad, charge_grad,
    ) = refs[12:]
    scaled = filter_of(kfilter)
    field = projected[...] * jnp.concatenate([scaled, scaled], axis=0)
    pieces = split(field)
    rows = field_rows(field)
    mine_charge = waves_to_atoms(rows, mine_high, mine_low)
    other_charge = waves_to_atoms(rows, wave_high, wave_low)
    charge_grad[...] = dot_three(split(factor[...]), pieces, 0, 0)
    mix = dot(mine_charge, whole(shared[:4])) + dot(other_charge, whole(shared[4:]))
    weights = split(w_charge[...])
    up_grad[...] = dot_three(split(mix), weights, 0, 1) + up_part[...]
    left = split(
        jnp.concatenate([weighted[...], dot_three(pieces, weights, 1, 1)], axis=1)
    )
    left_high[...], left_low[...] = left
    by_pos = by_position(left, grads, feature_high, feature_low, kvec, wave_high, wave_low)
    to_tiles(mine_charge, mine)
    to_tiles(other_charge, other)
    core, column = lax.axis_index("c"), lax.axis_index("x")
    for member in range(MEMBERS):
        number = member % 4
        out = (mine, other)[member // 4].at[number]
        place = jnp.where(core == member // 4, 0, 4) + (column + 4 - number) % 4
        piece = pl.ds(pl.multiple_of(place * 16, 16), 16)
        if member < 4:
            out[N : N + 8, :] = jnp.zeros((8, N), jnp.float32)
        else:
            out[N : N + 8, :] = by_pos[:, number * N : (number + 1) * N]
        out[N + 8 : N + 24, :] = up_grad[piece, :]
        out[N + 24 : N + 40, :] = charge_grad[piece, :]


def wave_back_late_kernel(*refs):
    (
        left_high, left_low, projected, charge_factor, kvec, wave_high, wave_low,
        feature_high, feature_low, late, grad_filter,
    ) = refs[4:]
    mixed = charge_factor[...] * projected[...]
    grad_filter[...] = SCALE * (mixed[0:SHARD] + mixed[SHARD:])
    left = (left_high[...], left_low[...])
    by_pos = by_position(left, refs[:4], feature_high, feature_low, kvec, wave_high, wave_low)
    for member in range(4):
        late[member, :, :] = by_pos[:, member * N : (member + 1) * N]


def body(
    positions, species, neighbours, face_sends, corner_sends,
    embed, radial, w_up, w_charge, kvec, kfilter, read,
):
    near, far, own_x, home, positions, species, neighbours, embed, radial, read = call(
        pack_kernel,
        (f32(8, N),) * 3
        + (
            i32(8, N), f32(3, N), i32(1, N), i32(SLOTS, N), f32(KINDS, N), f32(2, BASIS, N),
            f32(1, N),
        ),
        positions, species.reshape(1, N), face_sends, corner_sends, neighbours, embed, radial,
        read.reshape(1, N),
        scratch=(
            pltpu.VMEM((4, N // 2), jnp.int32),
            pltpu.VMEM((4, N // 4), jnp.int32),
            pltpu.SemaphoreType.DMA((8,)),
        ),
        far=True,
    )
    near_y, far_y = swapped(near, GY, 0), swapped(far, GY, 1)
    near, far = call(relay_kernel, (f32(8, N),) * 2, own_x, near_y, far_y)
    near_x, far_x = swapped(near, GX, 0), swapped(far, GX, 1)
    shared, active, invariants, vectors, sums, edges, places = call(
        edge_kernel,
        (
            f32(N + 8, N), f32(N, N), f32(N, N), f32(3, N, N), f32(4, KINDS * BASIS, N),
            f32(7, SLOTS, N), i32(2, SLOTS, N),
        ),
        positions, species, neighbours, near_x, far_x, near_y, far_y, embed, radial,
    )
    swap = [(0, 1), (1, 0)]

    def other_core(value):
        return lax.ppermute(value, "c", swap)

    def step_x(value, step):
        return lax.ppermute(value, "x", [(at, (at + step) % 4) for at in range(4)])

    def gather(value, beside=()):
        one, two, three = (step_x(value, step) for step in (1, 2, 3))
        two, *beside = lax.optimization_barrier((two, *beside))
        values = [value, one, two, three]
        return values + [other_core(item) for item in values], beside

    def scatter(kernel, parts, other):
        shape = f32(*other.shape[1:])
        tiles = call(kernel, (shape,) * 4, *parts, other_core(other))
        return [tiles[0]] + [step_x(tiles[step], -step) for step in (1, 2, 3)]

    shared, _ = gather(shared)
    half = jax.ShapeDtypeStruct((2 * SHARD, 4 * N), jnp.bfloat16)
    feature = jax.ShapeDtypeStruct((4 * N, N), jnp.bfloat16)
    part = (half, half, feature, feature)
    both = f32(2 * SHARD, N)
    factor, *mine_part = call(
        structure_mine_kernel, (both,) + part, *shared[:4], kvec, embed, w_up
    )
    factor, *other_part = call(
        structure_other_kernel, (f32(CROSSES, 16, N),) + part, *shared[4:], kvec, embed, w_up,
        factor,
    )
    mine_waves, mine_features = mine_part[:2], mine_part[2:]
    other_waves, other_features = other_part[:2], other_part[2:]

    def cross_sum(tiles):
        tiles = lax.all_to_all(tiles, CROSS, 0, 0)
        tiles = call(sum_kernel, f32(CROSSES, 16, N), tiles)
        return lax.all_to_all(tiles, CROSS, 0, 0).reshape(2 * SHARD, N)

    factor = cross_sum(factor)
    rows = jax.ShapeDtypeStruct((2 * N, 2 * SHARD), jnp.bfloat16)
    other, weighted, charge_factor, rows = call(
        potential_other_kernel, (f32(4, N, N), both, both, rows),
        factor, w_charge, kfilter, *other_waves,
    )
    mine = call(potential_mine_kernel, f32(4, N, N), rows, *mine_waves)
    grad_out, result = call(
        energy_kernel, (f32(N, N),) * 2,
        *scatter(core_sum_kernel, (mine,), other), *mine_features, read,
    )
    beside = call(read_kernel, (f32(1, N), f32(1, N), f32(N, N)), result, grad_out, active, read)
    grads, (energy, read_row, up_part) = gather(grad_out, beside)
    projected = call(projection_mine_kernel, both, *grads[:4], *mine_waves)
    others = grads[4:]
    projected = cross_sum(
        call(projection_other_kernel, f32(CROSSES, 16, N), *others, *other_waves, projected)
    )
    square = pltpu.VMEM((N, N), jnp.float32)
    left = jax.ShapeDtypeStruct((2 * SHARD, 2 * N), jnp.bfloat16)
    mine, other, *left = call(
        wave_back_kernel,
        (f32(4, N + 40, N), f32(4, N + 40, N), left, left),
        *others, *shared, projected, factor, weighted, kfilter, kvec, *mine_waves,
        *other_waves, *other_features, w_charge, up_part,
        scratch=(square, square),
    )
    late, shard = call(
        wave_back_late_kernel, (f32(4, 8, N), f32(SHARD, N)),
        *grads[:4], *left, projected, charge_factor, kvec, *mine_waves, *mine_features,
    )
    tiles = scatter(core_sum_late_kernel, (mine, late), other)
    next_shard = lax.ppermute(shard, "x", [(at, at ^ 1) for at in range(4)])
    payload, own_grad, charge_piece = call(
        edge_back_kernel,
        (f32(8, 56, N), f32(8, N), f32(16, N)),
        *tiles, active, invariants, vectors, sums, edges, places, embed, radial, w_up,
        w_charge, species, grad_out, read_row,
        cost=pl.CostEstimate(flops=10**9, bytes_accessed=10**7, transcendentals=10**5),
    )
    near_shards = jnp.concatenate([shard, next_shard], axis=0)
    far_shards = lax.ppermute(near_shards, "x", [(at, at ^ 2) for at in range(4)])
    payload = lax.all_to_all(payload, DEPTH, 0, 0)
    payload = call(depth_sum_kernel, f32(16, 56, N), payload, charge_piece)
    payload = lax.all_to_all(payload, PLANE, 0, 0)
    payload, threes = call(plane_sum_kernel, (f32(160, N), f32(8, N)), payload)
    shards = [near_shards, far_shards, other_core(near_shards), other_core(far_shards)]
    payload_other = other_core(payload)
    grad_filter = call(spread_kernel, f32(WAVES, N), *shards)
    forces, grad_embed, grad_radial, grad_up, grad_charge, grad_read = call(
        finish_kernel,
        (f32(3, N), f32(KINDS, N), f32(2, BASIS, N), f32(N, N), f32(N, N), f32(1, N)),
        payload, payload_other, threes, own_grad, home,
    )
    return (
        energy.reshape(N), forces, grad_embed, grad_radial, grad_up, grad_charge, grad_filter,
        grad_read.reshape(N),
    )


def solution(mesh):
    fine = Mesh(mesh.devices.reshape(4, 4, 2, 2, 4), ALL)
    atoms = P(ALL)
    rows = P(None, ALL)
    return jax.shard_map(
        body,
        mesh=fine,
        in_specs=(rows, atoms, rows, rows, rows) + (P(),) * 7,
        out_specs=(atoms, rows) + (P(),) * 6,
        check_vma=False,
    )
```

```python
import functools
import math

import jax
import jax.numpy as jnp
from jax import lax
from jax.experimental import pallas as pl
from jax.experimental.pallas import tpu as pltpu
from jax.sharding import Mesh
from jax.sharding import PartitionSpec as P

CUTOFF = 5.0
SOFTEN = 0.01
WIDTH_GAUSS = 2.0
DOMAIN = 8.8
N = 128
SLOTS = 64
KINDS = 6
BASIS = 8
WAVES = 2048
ATOMS = 32768
SHARD = 256
HIGHEST = lax.Precision.HIGHEST
SCALE = 1.0 / math.sqrt(ATOMS * WAVES)

GX = ("y", "zh", "c")
GY = ("zl", "x")
ALL = GX + GY
GROUP = ("c", "x")
CROSS = ("y", "zh", "zl")
MEMBERS = 8
CROSSES = 32
DEPTH = ("zh", "zl")
PLANE = ("y", "x")

COS_POLY = (
    0.999999989059021,
    -19.73920449945393,
    64.93911745989678,
    -85.45013953089901,
    60.16763095102345,
    -25.96759924855853,
    6.528658161204758,
)
SIN_POLY = (
    6.283184916495438,
    -41.34158923268875,
    81.59994332978647,
    -76.61447253128671,
    41.34288235472546,
    -12.471243535272281,
)


def dims(left, right):
    return (((left,), (right,)), ((), ()))


def exact_dot(left, right, left_dim=1, right_dim=0):
    return lax.dot_general(
        left,
        right,
        dims(left_dim, right_dim),
        precision=HIGHEST,
        preferred_element_type=jnp.float32,
    )


def half_dot(left, right, left_dim=1, right_dim=0):
    return lax.dot_general(
        left, right, dims(left_dim, right_dim), preferred_element_type=jnp.float32
    )


def split(value):
    high = value.astype(jnp.bfloat16)
    return high, (value - high.astype(jnp.float32)).astype(jnp.bfloat16)


def dot_three(left, right, left_dim=1, right_dim=0):
    left_high, left_low = left
    right_high, right_low = right
    return (
        half_dot(left_high, right_high, left_dim, right_dim)
        + half_dot(left_high, right_low, left_dim, right_dim)
        + half_dot(left_low, right_high, left_dim, right_dim)
    )


def dot(left, right, left_dim=1, right_dim=0):
    return dot_three(split(left), split(right), left_dim, right_dim)


def sigmoid(value):
    return 1.0 / (1.0 + jnp.exp(-value))


def lane(shape):
    return lax.broadcasted_iota(jnp.int32, shape, 1)


def row_of(shape):
    return lax.broadcasted_iota(jnp.int32, shape, 0)


def call(kernel, out_shape, *args, scratch=(), vmem=32, far=False, cost=None):
    more = {}
    if far:
        more["in_specs"] = [pl.BlockSpec(memory_space=pltpu.HBM)] * len(args)
        args = [pltpu.with_memory_space_constraint(value, pltpu.HBM) for value in args]
    return pl.pallas_call(
        kernel,
        out_shape=out_shape,
        scratch_shapes=list(scratch),
        cost_estimate=cost,
        **more,
        compiler_params=pltpu.CompilerParams(vmem_limit_bytes=vmem * 1024 * 1024),
    )(*args)


def f32(*shape):
    return jax.ShapeDtypeStruct(shape, jnp.float32)


def i32(*shape):
    return jax.ShapeDtypeStruct(shape, jnp.int32)


def take(row, index):
    return jnp.take_along_axis(
        jnp.broadcast_to(row, index.shape), index, axis=1, mode="promise_in_bounds"
    )


def joined(face, corner, faces, corners):
    return jnp.concatenate(
        [face[f : f + 1, :] for f in faces] + [corner[f : f + 1, :] for f in corners], axis=1
    )


def pack_kernel(pos_in, species_in, face_in, corner_in, nbr_in, embed_in, radial_in, read_in,
                near, far, own, home, pos, species, nbr, embed, radial, read, face, corner, sems):
    pairs = (
        (pos_in, pos), (species_in, species), (face_in, face), (corner_in, corner),
        (nbr_in, nbr), (embed_in, embed), (radial_in, radial), (read_in, read),
    )
    copies = [
        pltpu.make_async_copy(source, target, sems.at[number])
        for number, (source, target) in enumerate(pairs)
    ]
    for copy in copies:
        copy.start()
    for copy in copies[:4]:
        copy.wait()
    even = lax.axis_index("x") % 2 == 0
    rows = [pos[0:1, :], pos[1:2, :], pos[2:3, :], species[...].astype(jnp.float32)]
    padding = jnp.zeros((5, N), jnp.int32)
    where_from = jnp.concatenate(
        [
            joined(face, corner, (2,), (0, 2)),
            joined(face, corner, (3,), (1, 3)),
            joined(face, corner, (0, 1), ()),
            padding,
        ],
        axis=0,
    )
    home[...] = jnp.concatenate(
        [
            joined(face, corner, (0,), (0, 1)),
            joined(face, corner, (1,), (2, 3)),
            joined(face, corner, (2, 3), ()),
            padding,
        ],
        axis=0,
    )
    for number, row in enumerate(rows):
        got = take(row, where_from)
        near[number : number + 1, :] = jnp.where(even, got[1:2, :], got[0:1, :])
        far[number : number + 1, :] = jnp.where(even, got[0:1, :], got[1:2, :])
        own[number : number + 1, :] = got[2:3, :]
    zero = jnp.zeros((4, N), jnp.float32)
    near[4:8, :] = zero
    far[4:8, :] = zero
    own[4:8, :] = zero
    for copy in copies[4:]:
        copy.wait()


def swapped(value, axes, odd):
    count = math.prod(lax.axis_size(axis) for axis in axes)
    places = [(at, ((((at + odd) % count) ^ 1) - odd) % count) for at in range(count)]
    return lax.ppermute(value, axes, places)


def relay_kernel(own, near, far, one, two):
    at = lane((8, N))
    even = lax.axis_index("x") % 2 == 0
    a = own[...]
    b = jnp.where(even, near[...], far[...])
    d = jnp.where(even, far[...], near[...])
    to_minus = jnp.where(at < 64, a, jnp.where(at < 96, b, pltpu.roll(d, 32, 1)))
    to_plus = jnp.where(
        at < 64, pltpu.roll(a, 64, 1), jnp.where(at < 96, pltpu.roll(b, 96, 1), d)
    )
    first = lax.axis_index("c") == 0
    one[...] = jnp.where(first, to_plus, to_minus)
    two[...] = jnp.where(first, to_minus, to_plus)


def pair_weights(embed, radial):
    scalar, vector = [], []
    for kind in range(KINDS):
        row = embed[kind : kind + 1, :]
        scalar.append(radial[0] * row * 0.25)
        vector.append(radial[1] * row * 0.05)
    return jnp.concatenate(scalar, axis=0), jnp.concatenate(vector, axis=0)


def basis_centers():
    return row_of((BASIS, N)).astype(jnp.float32) * (CUTOFF / (BASIS - 1))


def edge_kernel(
    pos, species, nbr, near_x, far_x, near_y, far_y, embed, radial,
    shared, active, invariants, vectors, sums, edges, places,
):
    at = lane((8, N))
    own = [pos[0:1, :], pos[1:2, :], pos[2:3, :], species[...].astype(jnp.float32)]
    core_zero = lax.axis_index("c") == 0
    even = lax.axis_index("x") % 2 == 0
    first = jnp.where(core_zero, near_x[...], far_x[...])
    second = jnp.where(core_zero, far_x[...], near_x[...])
    plus_y = jnp.where(even, near_y[...], far_y[...])
    minus_y = jnp.where(even, far_y[...], near_y[...])
    third = jnp.where(at < 64, plus_y, pltpu.roll(minus_y, 64, 1))
    line = lane((1, N))
    corner_y = jnp.where(line < 64, 0.0, jnp.where(line < 96, DOMAIN, -DOMAIN))
    tables = [
        own,
        [first[0:1] + DOMAIN, first[1:2] + corner_y, first[2:3], first[3:4]],
        [second[0:1] - DOMAIN, second[1:2] + corner_y, second[2:3], second[3:4]],
        [third[0:1], third[1:2] + jnp.where(line < 64, DOMAIN, -DOMAIN), third[2:3], third[3:4]],
    ]
    for group in range(SLOTS // 8):
        rows = slice(8 * group, 8 * group + 8)
        slot = nbr[rows, :]
        block = lax.shift_right_logical(slot, 6)
        table = jnp.where(
            block < 2,
            0,
            jnp.where(
                (block == 4) | (block == 5), 3, jnp.where((block & 1) == 0, 1, 2)
            ),
        )
        table = jnp.where(block == 8, 4, table)
        half = jnp.where((block == 1) | ((block >= 5) & (block < 8)), 64, 0)
        place = (slot & 63) + half
        found = []
        for number in range(4):
            value = take(tables[0][number], place)
            for other in range(1, 4):
                value = jnp.where(table == other, take(tables[other][number], place), value)
            found.append(value)
        offset = [found[d] - own[d] for d in range(3)]
        dist_sq = offset[0] * offset[0] + offset[1] * offset[1] + offset[2] * offset[2]
        valid = (table < 4).astype(jnp.float32)
        ramp = jnp.maximum(1.0 - dist_sq / (CUTOFF * CUTOFF), 0.0)
        edges[0, rows, :] = offset[0]
        edges[1, rows, :] = offset[1]
        edges[2, rows, :] = offset[2]
        edges[3, rows, :] = found[3]
        edges[4, rows, :] = jnp.sqrt(dist_sq + SOFTEN)
        edges[5, rows, :] = ramp * ramp * valid
        edges[6, rows, :] = (-2.0 / (CUTOFF * CUTOFF)) * ramp * valid
        places[0, rows, :] = table
        places[1, rows, :] = place
    centers = basis_centers()

    def step(slot, carry):
        row = pl.ds(slot, 1)
        away = edges[4, row, :] - centers
        basis = jnp.exp(-WIDTH_GAUSS * away * away) * edges[5, row, :]
        parts = [basis] + [basis * edges[d, row, :] for d in range(3)]
        kind_row = jnp.broadcast_to(edges[3, row, :], (BASIS, N))
        out = []
        for kind in range(KINDS):
            mask = kind_row == float(kind)
            for number in range(4):
                out.append(carry[4 * kind + number] + jnp.where(mask, parts[number], 0.0))
        return tuple(out)

    zero = jnp.zeros((BASIS, N), jnp.float32)
    total = lax.fori_loop(0, SLOTS, step, (zero,) * (4 * KINDS), unroll=16)
    for number in range(4):
        sums[number, :, :] = jnp.concatenate(
            [total[4 * kind + number] for kind in range(KINDS)], axis=0
        )
    scalar_w, vector_w = pair_weights(embed, radial)
    value = dot(sums[0], scalar_w, 0, 0)
    for d in range(3):
        vector = dot(sums[1 + d], vector_w, 0, 0)
        vectors[d, :, :] = vector
        value = value + vector * vector
    invariants[...] = value
    result = value * sigmoid(value)
    active[...] = result
    anchor_x = lax.convert_element_type(lax.axis_index(GX), jnp.float32) * DOMAIN
    anchor_y = lax.convert_element_type(lax.axis_index(GY), jnp.float32) * DOMAIN
    zero_row = jnp.zeros((1, N), jnp.float32)
    tail = jnp.concatenate(
        [own[0] + anchor_x, own[1] + anchor_y, own[2], own[3]] + [zero_row] * 4, axis=0
    )
    shared[0:N, :] = result
    shared[N : N + 8, :] = tail


def edge_back_kernel(
    tile_0, tile_1, tile_2, tile_3, active, invariants, vectors, sums, edges, places, embed, radial, w_up, w_charge,
    species, grad_out, read_row,
    payload, own_grad, charge_piece,
):
    total = tile_0[...] + tile_1[...] + tile_2[...] + tile_3[...]
    grad_charges = jnp.transpose(total[0:N, :])
    updated = grad_out[...] + dot(grad_charges, w_charge[...], 1, 1)
    value = invariants[...]
    logistic = sigmoid(value)
    slope = logistic * (1.0 + value * (1.0 - logistic))
    grad_inv = dot(updated, w_up[...], 1, 1) * slope
    scalar_w, vector_w = pair_weights(embed, radial)
    pulls = [dot(scalar_w, grad_inv, 1, 1)]
    grad_scalar = dot(sums[0], grad_inv)
    grad_vector = jnp.zeros((KINDS * BASIS, N), jnp.float32)
    for d in range(3):
        along = 2.0 * vectors[d] * grad_inv
        pulls.append(dot(vector_w, along, 1, 1))
        grad_vector = grad_vector + dot(sums[1 + d], along)
    onehot = (row_of((8, N)) == species[...]).astype(jnp.float32)
    grad_table = dot(onehot, updated)
    radial_zero = jnp.zeros((BASIS, N), jnp.float32)
    radial_one = jnp.zeros((BASIS, N), jnp.float32)
    table_rows = []
    for kind in range(KINDS):
        rows = slice(kind * BASIS, (kind + 1) * BASIS)
        row = embed[kind : kind + 1, :]
        part_zero, part_one = grad_scalar[rows] * 0.25, grad_vector[rows] * 0.05
        radial_zero = radial_zero + part_zero * row
        radial_one = radial_one + part_one * row
        table_rows.append(
            grad_table[kind : kind + 1]
            + jnp.sum(radial[0] * part_zero + radial[1] * part_one, axis=0, keepdims=True)
        )
    rest = jnp.concatenate(
        [radial_zero, radial_one] + table_rows + [read_row[...], jnp.zeros((1, N), jnp.float32)],
        axis=0,
    )
    up_piece = total[N + 8 : N + 24, :]
    charge_piece[...] = total[N + 24 : N + 40, :]
    centers = basis_centers()
    sub = row_of((8, N))
    sub_table = sub & 3
    high_rows = sub < 4
    lane_rows = row_of((N, N))
    pull = [
        [pulls[number][kind * BASIS : (kind + 1) * BASIS] for number in range(4)]
        for kind in range(KINDS)
    ]

    def one(slot):
        row = pl.ds(slot, 1)
        kind_row = jnp.broadcast_to(edges[3, row, :], (BASIS, N))
        own_pull = list(pull[KINDS - 1])
        for kind in range(KINDS - 1):
            mask = kind_row == float(kind)
            own_pull = [jnp.where(mask, pull[kind][n], own_pull[n]) for n in range(4)]
        radius = edges[4, row, :]
        envelope = edges[5, row, :]
        away = radius - centers
        bell = jnp.exp(-WIDTH_GAUSS * away * away)
        offset = [jnp.broadcast_to(edges[d, row, :], (BASIS, N)) for d in range(3)]
        by_basis = own_pull[0]
        for d in range(3):
            by_basis = by_basis + offset[d] * own_pull[1 + d]
        by_square = by_basis * bell * (edges[6, row, :] - (2.0 * envelope / radius) * away)
        basis = bell * envelope
        table = jnp.broadcast_to(places[0, row, :], (8, N)) == sub_table
        place = lane_rows == places[1, row, :]
        onehot = jnp.where(place, 1.0, 0.0).astype(jnp.bfloat16)
        parts, pieces = [], []
        for d in range(3):
            part = basis * own_pull[1 + d] + 2.0 * offset[d] * by_square
            parts.append(part)
            whole = jnp.broadcast_to(jnp.sum(part, axis=0, keepdims=True), (8, N))
            high = whole.astype(jnp.bfloat16).astype(jnp.float32)
            pieces.append(jnp.where(table, jnp.where(high_rows, high, whole - high), 0.0))
        return parts, jnp.concatenate(pieces, axis=0).astype(jnp.bfloat16), onehot

    def step(group, carry):
        found = [one(group * 8 + number) for number in range(8)]
        centre = list(carry[:3])
        for parts, _, _ in found:
            centre = [centre[d] + parts[d] for d in range(3)]
        rows = jnp.concatenate([item[1] for item in found], axis=1)
        onehot = jnp.concatenate([item[2] for item in found], axis=1)
        return (*centre, carry[3] + half_dot(rows, onehot, 1, 1))

    zero = jnp.zeros((8, N), jnp.float32)
    out = (zero, zero, zero, jnp.zeros((24, N), jnp.float32))
    for group in range(SLOTS // 8):
        out = step(group, out)
    scattered = out[3]
    waves = total[N : N + 8, :]
    own_rows, one_rows, two_rows, three_rows = [], [], [], []
    for d in range(3):
        both = scattered[8 * d : 8 * d + 4] + scattered[8 * d + 4 : 8 * d + 8]
        centre = jnp.sum(out[d], axis=0, keepdims=True)
        own_rows.append(both[0:1] - centre + waves[d : d + 1])
        one_rows.append(both[1:2])
        two_rows.append(both[2:3])
        three_rows.append(both[3:4])
    pad = [jnp.zeros((5, N), jnp.float32)]
    own_grad[...] = jnp.concatenate(own_rows + pad, axis=0)
    depth_of = [depth_after(step_x, step_y) for step_x, step_y in TABLE_DIRS]
    line = lane((8, N))
    ones = jnp.concatenate(one_rows + pad, axis=0)
    twos = jnp.concatenate(two_rows + pad, axis=0)
    threes = jnp.concatenate(three_rows + pad, axis=0)
    home_one = segments(line, depth_of[0:3])
    home_two = segments(line, depth_of[3:6])
    home_three = jnp.where(line < 64, depth_of[6], depth_of[7])
    for other in range(8):
        payload[other, 0:16, :] = up_piece
        payload[other, 16:40, :] = rest
        payload[other, 40:48, :] = pack_six(
            jnp.where(home_one == other, ones, 0.0), jnp.where(home_two == other, twos, 0.0)
        )
        payload[other, 48:56, :] = jnp.where(home_three == other, threes, 0.0)


TABLE_DIRS = ((1, 0), (1, 1), (1, -1), (-1, 0), (-1, 1), (-1, -1), (0, 1), (0, -1))


def segments(line, values):
    return jnp.where(line < 64, values[0], jnp.where(line < 96, values[1], values[2]))


def pack_six(one, two):
    return jnp.where(row_of((8, N)) < 4, one, pltpu.roll(two, 4, 0))


def depth_after(step_x, step_y):
    core, high = lax.axis_index("c"), lax.axis_index("zh")
    low, column = lax.axis_index("zl"), lax.axis_index("x")
    if step_x == 1:
        high = jnp.where(core == 1, (high + 1) % 4, high)
    if step_x == -1:
        high = jnp.where(core == 0, (high + 3) % 4, high)
    if step_y == 1:
        low = jnp.where(column == 3, 1 - low, low)
    if step_y == -1:
        low = jnp.where(column == 0, 1 - low, low)
    return high * 2 + low


def plane_after(step_x, step_y):
    core, high = lax.axis_index("c"), lax.axis_index("zh")
    row, column = lax.axis_index("y"), lax.axis_index("x")
    if step_x == 1:
        row = jnp.where((core == 1) & (high == 0), (row + 1) % 4, row)
    if step_x == -1:
        row = jnp.where((core == 0) & (high == 3), (row + 3) % 4, row)
    return row * 4 + (column + step_y + 4) % 4


def depth_sum_kernel(tiles, charge_piece, out):
    total = jnp.sum(tiles[...], axis=0)
    place_of = [plane_after(step_x, step_y) for step_x, step_y in TABLE_DIRS]
    line = lane((8, N))
    home = jnp.where(
        row_of((8, N)) < 4, segments(line, place_of[0:3]), segments(line, place_of[3:6])
    )
    home_three = jnp.where(line < 64, place_of[6], place_of[7])
    sixes, threes = total[40:48], total[48:56]
    row = lax.axis_index("y")
    quarter = charge_piece[0:4, :]
    for number in range(1, 4):
        quarter = jnp.where(row == number, charge_piece[4 * number : 4 * number + 4, :], quarter)
    for other in range(16):
        out[other, 0:40, :] = total[0:40]
        out[other, 40:48, :] = jnp.where(home == other, sixes, 0.0)
        out[other, 48:56, :] = jnp.where(home_three == other, threes, 0.0)
        out[other, 52:56, :] = quarter


def plane_sum_kernel(tiles, swap, threes):
    for column in range(4):
        total = tiles[column, 0:16, :]
        for row in range(1, 4):
            total = total + tiles[4 * row + column, 0:16, :]
        swap[16 * column : 16 * column + 16, :] = total
        for row in range(4):
            at = 96 + 16 * column + 4 * row
            swap[at : at + 4, :] = tiles[4 * row + column, 52:56, :]
    rest = tiles[0, 16:56, :]
    for other in range(1, 16):
        rest = rest + tiles[other, 16:56, :]
    swap[64:96, :] = rest[0:32]
    threes[...] = jnp.where(row_of((8, N)) < 4, rest[32:40], 0.0)


def finish_kernel(own, other, threes, own_grad, home, forces, grad_embed, grad_radial, grad_up,
                  grad_charge, grad_read):
    mean = 1.0 / ATOMS
    core = lax.axis_index("c")
    mine = pl.ds(pl.multiple_of(core * 64, 64), 64)
    theirs = pl.ds(pl.multiple_of((1 - core) * 64, 64), 64)
    grad_up[mine, :] = own[0:64, :] * mean
    grad_up[theirs, :] = other[0:64, :] * mean
    grad_charge[mine, :] = own[96:160, :] * mean
    grad_charge[theirs, :] = other[96:160, :] * mean
    total = (own[64:88, :] + other[64:88, :]) * mean
    grad_radial[0, :, :] = total[0:8]
    grad_radial[1, :, :] = total[8:16]
    grad_embed[...] = total[16:22]
    grad_read[...] = total[22:23]
    sixes = other[88:96, :]
    grad = own_grad[...]
    lane_rows = row_of((N, N))
    for number, piece in enumerate((sixes, pltpu.roll(sixes, 4, 0), threes[...])):
        onehot = jnp.where(lane_rows == home[number : number + 1, :], 1.0, 0.0)
        grad = grad + dot(piece, onehot, 1, 1)
    forces[...] = -grad[0:3, :]


def spread_kernel(*refs):
    out = refs[-1]
    core, column = lax.axis_index("c"), lax.axis_index("x")
    for number, pair in enumerate(refs[:-1]):
        for half in range(2):
            source = column ^ (2 * (number % 2) + half)
            member = jnp.where(number < 2, core, 1 - core) * 4 + source
            place = pl.ds(pl.multiple_of(member * SHARD, SHARD), SHARD)
            out[place, :] = pair[half * SHARD : (half + 1) * SHARD, :]


def structure_part(tiles, kvec, embed, w_up, wave_high, wave_low, feature_high, feature_low):
    me = lax.axis_index(GROUP)
    at = pl.multiple_of(me * SHARD, SHARD)
    rows = jnp.concatenate(
        [kvec[:, pl.ds(at, SHARD)], jnp.zeros((5, SHARD), jnp.float32)], axis=0
    )
    turns = jnp.transpose(rows * (1.0 / (2.0 * math.pi)))
    table = jnp.concatenate([embed[...], jnp.zeros((2, N), jnp.float32)], axis=0)
    up = split(w_up[...])
    for member, tile in enumerate(tiles):
        part = slice(member * N, (member + 1) * N)
        tail = tile[N : N + 8, :]
        onehot = (row_of((8, N)).astype(jnp.float32) == tail[3:4, :]).astype(jnp.float32)
        feature = exact_dot(onehot, table, 0, 0) + dot_three(split(tile[0:N, :]), up)
        high, low = split(feature)
        feature_high[part, :] = high
        feature_low[part, :] = low
        for chunk in range(SHARD // 64):
            waves = slice(chunk * 64, chunk * 64 + 64)
            angle = (
                turns[waves, 0:1] * tail[0:1, :]
                + turns[waves, 1:2] * tail[1:2, :]
                + turns[waves, 2:3] * tail[2:3, :]
            )
            angle = angle - jnp.round(angle)
            square = angle * angle
            cosine = jnp.full(square.shape, COS_POLY[-1], jnp.float32)
            for value in COS_POLY[-2::-1]:
                cosine = cosine * square + value
            sine = jnp.full(square.shape, SIN_POLY[-1], jnp.float32)
            for value in SIN_POLY[-2::-1]:
                sine = sine * square + value
            sine = sine * angle
            high, low = split(cosine)
            wave_high[waves, part] = high
            wave_low[waves, part] = low
            high, low = split(sine)
            waves = slice(SHARD + chunk * 64, SHARD + chunk * 64 + 64)
            wave_high[waves, part] = high
            wave_low[waves, part] = low
    return project(wave_high, wave_low, feature_high[...], feature_low[...])


def structure_mine_kernel(*refs):
    kvec, embed, w_up, factor, *part = refs[4:]
    factor[...] = structure_part(refs[:4], kvec, embed, w_up, *part)


def structure_other_kernel(*refs):
    kvec, embed, w_up, mine, factor, *part = refs[4:]
    total = mine[...] + structure_part(refs[:4], kvec, embed, w_up, *part)
    factor[...] = total.reshape(CROSSES, 16, N)


def whole(tiles):
    return jnp.concatenate([tile[0:N, :] for tile in tiles], axis=0)


def project(wave_high, wave_low, high, low):
    wide = half_dot(wave_high[...], jnp.concatenate([high, low], axis=1))
    return wide[:, 0:N] + wide[:, N:] + half_dot(wave_low[...], high)


def projection_mine_kernel(*refs):
    wave_high, wave_low, out = refs[4:]
    out[...] = project(wave_high, wave_low, *split(whole(refs[:4])))


def projection_other_kernel(*refs):
    wave_high, wave_low, mine, out = refs[4:]
    total = mine[...] + project(wave_high, wave_low, *split(whole(refs[:4])))
    out[...] = total.reshape(CROSSES, 16, N)


def sum_kernel(tiles, out):
    total = jnp.sum(tiles[...], axis=0)
    for other in range(out.shape[0]):
        out[other, :, :] = total


def filter_of(kfilter):
    me = lax.axis_index(GROUP)
    return kfilter[pl.ds(pl.multiple_of(me * SHARD, SHARD), SHARD), :] * SCALE


def core_sum_kernel(mine, other, *out):
    for number, ref in enumerate(out):
        ref[...] = mine[number] + other[number]


def core_sum_late_kernel(mine, late, other, *out):
    for number, ref in enumerate(out):
        ref[...] = mine[number] + other[number]
        ref[N : N + 8, :] = mine[number, N : N + 8, :] + (
            late[number] + other[number, N : N + 8, :]
        )


def field_rows(field):
    return jnp.concatenate(split(jnp.transpose(field)), axis=0)


def waves_to_atoms(rows, wave_high, wave_low):
    wide = half_dot(rows, wave_high[...])
    return wide[0:N] + wide[N:] + half_dot(rows[0:N], wave_low[...])


def to_tiles(total, out):
    for member in range(4):
        out[member, 0:N, :] = total[:, member * N : (member + 1) * N]


def potential_other_kernel(factor, w_charge, kfilter, wave_high, wave_low,
                           other, weighted, charge_factor, rows_out):
    scaled = filter_of(kfilter)
    charged = dot(factor[...], w_charge[...])
    charge_factor[...] = charged
    field = charged * jnp.concatenate([scaled, scaled], axis=0)
    weighted[...] = field
    rows = field_rows(field)
    rows_out[...] = rows
    to_tiles(waves_to_atoms(rows, wave_high, wave_low), other)


def potential_mine_kernel(rows, wave_high, wave_low, mine):
    to_tiles(waves_to_atoms(rows[...], wave_high, wave_low), mine)


def energy_kernel(tile_0, tile_1, tile_2, tile_3, feature_high, feature_low, read,
                  grad_out, result_out):
    total = tile_0[...] + tile_1[...] + tile_2[...] + tile_3[...]
    feature = feature_high[0:N, :].astype(jnp.float32) + feature_low[0:N, :].astype(jnp.float32)
    combined = feature + jnp.transpose(total)
    logistic = sigmoid(combined)
    result_out[...] = combined * logistic
    grad_out[...] = read[...] * (logistic * (1.0 + combined * (1.0 - logistic)))


def read_kernel(result, grad, active, read, energy, read_row, up_part):
    value = result[...]
    energy[...] = dot(jnp.broadcast_to(read[...], (8, N)), value, 1, 1)[0:1, :]
    read_row[...] = jnp.sum(value, axis=0, keepdims=True)
    up_part[...] = dot(active[...], grad[...], 0, 0)


def wave_trig(wave_high, wave_low):
    cosine = wave_high[0:SHARD, :].astype(jnp.float32) + wave_low[0:SHARD, :].astype(jnp.float32)
    sine = wave_high[SHARD:, :].astype(jnp.float32) + wave_low[SHARD:, :].astype(jnp.float32)
    return cosine, sine


def by_position(left, grads, feature_high, feature_low, kvec, wave_high, wave_low):
    grad_high, grad_low = split(whole(grads))
    along = dot_three(
        left,
        (
            jnp.concatenate([grad_high, feature_high[...]], axis=1),
            jnp.concatenate([grad_low, feature_low[...]], axis=1),
        ),
        1, 1,
    )
    cosine, sine = wave_trig(wave_high, wave_low)
    phase = cosine * along[SHARD:] - sine * along[0:SHARD]
    me = lax.axis_index(GROUP)
    rows = jnp.concatenate(
        [
            kvec[:, pl.ds(pl.multiple_of(me * SHARD, SHARD), SHARD)],
            jnp.zeros((5, SHARD), jnp.float32),
        ],
        axis=0,
    )
    return dot_three(split(rows), split(phase))


def wave_back_kernel(*refs):
    grads, shared = refs[:4], refs[4:12]
    (
        projected, factor, weighted, kfilter, kvec, mine_high, mine_low, wave_high, wave_low,
        feature_high, feature_low, w_charge, up_part,
        mine, other, left_high, left_low, up_grad, charge_grad,
    ) = refs[12:]
    scaled = filter_of(kfilter)
    field = projected[...] * jnp.concatenate([scaled, scaled], axis=0)
    pieces = split(field)
    rows = field_rows(field)
    mine_charge = waves_to_atoms(rows, mine_high, mine_low)
    other_charge = waves_to_atoms(rows, wave_high, wave_low)
    charge_grad[...] = dot_three(split(factor[...]), pieces, 0, 0)
    mix = dot(mine_charge, whole(shared[:4])) + dot(other_charge, whole(shared[4:]))
    weights = split(w_charge[...])
    up_grad[...] = dot_three(split(mix), weights, 0, 1) + up_part[...]
    left = split(
        jnp.concatenate([weighted[...], dot_three(pieces, weights, 1, 1)], axis=1)
    )
    left_high[...], left_low[...] = left
    by_pos = by_position(left, grads, feature_high, feature_low, kvec, wave_high, wave_low)
    to_tiles(mine_charge, mine)
    to_tiles(other_charge, other)
    core, column = lax.axis_index("c"), lax.axis_index("x")
    for member in range(MEMBERS):
        number = member % 4
        out = (mine, other)[member // 4].at[number]
        place = jnp.where(core == member // 4, 0, 4) + (column ^ number)
        piece = pl.ds(pl.multiple_of(place * 16, 16), 16)
        if member < 4:
            out[N : N + 8, :] = jnp.zeros((8, N), jnp.float32)
        else:
            out[N : N + 8, :] = by_pos[:, number * N : (number + 1) * N]
        out[N + 8 : N + 24, :] = up_grad[piece, :]
        out[N + 24 : N + 40, :] = charge_grad[piece, :]


def wave_back_late_kernel(*refs):
    (
        left_high, left_low, projected, charge_factor, kvec, wave_high, wave_low,
        feature_high, feature_low, late, grad_filter,
    ) = refs[4:]
    mixed = charge_factor[...] * projected[...]
    grad_filter[...] = SCALE * (mixed[0:SHARD] + mixed[SHARD:])
    left = (left_high[...], left_low[...])
    by_pos = by_position(left, refs[:4], feature_high, feature_low, kvec, wave_high, wave_low)
    for member in range(4):
        late[member, :, :] = by_pos[:, member * N : (member + 1) * N]


def body(
    positions, species, neighbours, face_sends, corner_sends,
    embed, radial, w_up, w_charge, kvec, kfilter, read,
):
    near, far, own_x, home, positions, species, neighbours, embed, radial, read = call(
        pack_kernel,
        (f32(8, N),) * 3
        + (
            i32(8, N), f32(3, N), i32(1, N), i32(SLOTS, N), f32(KINDS, N), f32(2, BASIS, N),
            f32(1, N),
        ),
        positions, species.reshape(1, N), face_sends, corner_sends, neighbours, embed, radial,
        read.reshape(1, N),
        scratch=(
            pltpu.VMEM((4, N // 2), jnp.int32),
            pltpu.VMEM((4, N // 4), jnp.int32),
            pltpu.SemaphoreType.DMA((8,)),
        ),
        far=True,
    )
    near_y, far_y = swapped(near, GY, 0), swapped(far, GY, 1)
    near, far = call(relay_kernel, (f32(8, N),) * 2, own_x, near_y, far_y)
    near_x, far_x = swapped(near, GX, 0), swapped(far, GX, 1)
    shared, active, invariants, vectors, sums, edges, places = call(
        edge_kernel,
        (
            f32(N + 8, N), f32(N, N), f32(N, N), f32(3, N, N), f32(4, KINDS * BASIS, N),
            f32(7, SLOTS, N), i32(2, SLOTS, N),
        ),
        positions, species, neighbours, near_x, far_x, near_y, far_y, embed, radial,
    )
    swap = [(0, 1), (1, 0)]

    def other_core(value):
        return lax.ppermute(value, "c", swap)

    def step_x(value, step):
        return lax.ppermute(value, "x", [(at, at ^ step) for at in range(4)])

    def gather(value, beside=()):
        one, two, three = (step_x(value, step) for step in (1, 2, 3))
        two, *beside = lax.optimization_barrier((two, *beside))
        values = [value, one, two, three]
        return values + [other_core(item) for item in values], beside

    def scatter(kernel, parts, other):
        shape = f32(*other.shape[1:])
        tiles = call(kernel, (shape,) * 4, *parts, other_core(other))
        return [tiles[0]] + [step_x(tiles[step], step) for step in (1, 2, 3)]

    shared, _ = gather(shared)
    half = jax.ShapeDtypeStruct((2 * SHARD, 4 * N), jnp.bfloat16)
    feature = jax.ShapeDtypeStruct((4 * N, N), jnp.bfloat16)
    part = (half, half, feature, feature)
    both = f32(2 * SHARD, N)
    factor, *mine_part = call(
        structure_mine_kernel, (both,) + part, *shared[:4], kvec, embed, w_up
    )
    factor, *other_part = call(
        structure_other_kernel, (f32(CROSSES, 16, N),) + part, *shared[4:], kvec, embed, w_up,
        factor,
    )
    mine_waves, mine_features = mine_part[:2], mine_part[2:]
    other_waves, other_features = other_part[:2], other_part[2:]

    def cross_sum(tiles):
        tiles = lax.all_to_all(tiles, CROSS, 0, 0)
        tiles = call(sum_kernel, f32(CROSSES, 16, N), tiles)
        return lax.all_to_all(tiles, CROSS, 0, 0).reshape(2 * SHARD, N)

    factor = cross_sum(factor)
    rows = jax.ShapeDtypeStruct((2 * N, 2 * SHARD), jnp.bfloat16)
    other, weighted, charge_factor, rows = call(
        potential_other_kernel, (f32(4, N, N), both, both, rows),
        factor, w_charge, kfilter, *other_waves,
    )
    mine = call(potential_mine_kernel, f32(4, N, N), rows, *mine_waves)
    grad_out, result = call(
        energy_kernel, (f32(N, N),) * 2,
        *scatter(core_sum_kernel, (mine,), other), *mine_features, read,
    )
    beside = call(read_kernel, (f32(1, N), f32(1, N), f32(N, N)), result, grad_out, active, read)
    grads, (energy, read_row, up_part) = gather(grad_out, beside)
    projected = call(projection_mine_kernel, both, *grads[:4], *mine_waves)
    others = grads[4:]
    projected = cross_sum(
        call(projection_other_kernel, f32(CROSSES, 16, N), *others, *other_waves, projected)
    )
    square = pltpu.VMEM((N, N), jnp.float32)
    left = jax.ShapeDtypeStruct((2 * SHARD, 2 * N), jnp.bfloat16)
    mine, other, *left = call(
        wave_back_kernel,
        (f32(4, N + 40, N), f32(4, N + 40, N), left, left),
        *others, *shared, projected, factor, weighted, kfilter, kvec, *mine_waves,
        *other_waves, *other_features, w_charge, up_part,
        scratch=(square, square),
    )
    late, shard = call(
        wave_back_late_kernel, (f32(4, 8, N), f32(SHARD, N)),
        *grads[:4], *left, projected, charge_factor, kvec, *mine_waves, *mine_features,
    )
    tiles = scatter(core_sum_late_kernel, (mine, late), other)
    next_shard = lax.ppermute(shard, "x", [(at, at ^ 1) for at in range(4)])
    payload, own_grad, charge_piece = call(
        edge_back_kernel,
        (f32(8, 56, N), f32(8, N), f32(16, N)),
        *tiles, active, invariants, vectors, sums, edges, places, embed, radial, w_up,
        w_charge, species, grad_out, read_row,
        cost=pl.CostEstimate(flops=10**9, bytes_accessed=10**7, transcendentals=10**5),
    )
    near_shards = jnp.concatenate([shard, next_shard], axis=0)
    far_shards = lax.ppermute(near_shards, "x", [(at, at ^ 2) for at in range(4)])
    payload = lax.all_to_all(payload, DEPTH, 0, 0)
    payload = call(depth_sum_kernel, f32(16, 56, N), payload, charge_piece)
    payload = lax.all_to_all(payload, PLANE, 0, 0)
    payload, threes = call(plane_sum_kernel, (f32(160, N), f32(8, N)), payload)
    shards = [near_shards, far_shards, other_core(near_shards), other_core(far_shards)]
    payload_other = other_core(payload)
    grad_filter = call(spread_kernel, f32(WAVES, N), *shards)
    forces, grad_embed, grad_radial, grad_up, grad_charge, grad_read = call(
        finish_kernel,
        (f32(3, N), f32(KINDS, N), f32(2, BASIS, N), f32(N, N), f32(N, N), f32(1, N)),
        payload, payload_other, threes, own_grad, home,
    )
    return (
        energy.reshape(N), forces, grad_embed, grad_radial, grad_up, grad_charge, grad_filter,
        grad_read.reshape(N),
    )


def solution(mesh):
    fine = Mesh(mesh.devices.reshape(4, 4, 2, 2, 4), ALL)
    atoms = P(ALL)
    rows = P(None, ALL)
    return jax.shard_map(
        body,
        mesh=fine,
        in_specs=(rows, atoms, rows, rows, rows) + (P(),) * 7,
        out_specs=(atoms, rows) + (P(),) * 6,
        check_vma=False,
    )
```

```python
import functools
import math

import jax
import jax.numpy as jnp
from jax import lax
from jax.experimental import pallas as pl
from jax.experimental.pallas import tpu as pltpu
from jax.sharding import Mesh
from jax.sharding import PartitionSpec as P

CUTOFF = 5.0
SOFTEN = 0.01
WIDTH_GAUSS = 2.0
DOMAIN = 8.8
N = 128
SLOTS = 64
KINDS = 6
BASIS = 8
WAVES = 2048
ATOMS = 32768
SHARD = 256
HIGHEST = lax.Precision.HIGHEST
SCALE = 1.0 / math.sqrt(ATOMS * WAVES)

GX = ("y", "zh", "c")
GY = ("zl", "x")
ALL = GX + GY
GROUP = ("c", "x")
CROSS = ("y", "zh", "zl")
MEMBERS = 8
CROSSES = 32
DEPTH = ("zh", "zl")
PLANE = ("y", "x")

COS_POLY = (
    0.999999989059021,
    -19.73920449945393,
    64.93911745989678,
    -85.45013953089901,
    60.16763095102345,
    -25.96759924855853,
    6.528658161204758,
)
SIN_POLY = (
    6.283184916495438,
    -41.34158923268875,
    81.59994332978647,
    -76.61447253128671,
    41.34288235472546,
    -12.471243535272281,
)


def dims(left, right):
    return (((left,), (right,)), ((), ()))


def exact_dot(left, right, left_dim=1, right_dim=0):
    return lax.dot_general(
        left,
        right,
        dims(left_dim, right_dim),
        precision=HIGHEST,
        preferred_element_type=jnp.float32,
    )


def half_dot(left, right, left_dim=1, right_dim=0):
    return lax.dot_general(
        left, right, dims(left_dim, right_dim), preferred_element_type=jnp.float32
    )


def split(value):
    high = value.astype(jnp.bfloat16)
    return high, (value - high.astype(jnp.float32)).astype(jnp.bfloat16)


def dot_three(left, right, left_dim=1, right_dim=0):
    left_high, left_low = left
    right_high, right_low = right
    return (
        half_dot(left_high, right_high, left_dim, right_dim)
        + half_dot(left_high, right_low, left_dim, right_dim)
        + half_dot(left_low, right_high, left_dim, right_dim)
    )


def dot(left, right, left_dim=1, right_dim=0):
    return dot_three(split(left), split(right), left_dim, right_dim)


def sigmoid(value):
    return 1.0 / (1.0 + jnp.exp(-value))


def lane(shape):
    return lax.broadcasted_iota(jnp.int32, shape, 1)


def row_of(shape):
    return lax.broadcasted_iota(jnp.int32, shape, 0)


def call(kernel, out_shape, *args, scratch=(), vmem=32, far=False, cost=None):
    more = {}
    if far:
        more["in_specs"] = [pl.BlockSpec(memory_space=pltpu.HBM)] * len(args)
        args = [pltpu.with_memory_space_constraint(value, pltpu.HBM) for value in args]
    return pl.pallas_call(
        kernel,
        out_shape=out_shape,
        scratch_shapes=list(scratch),
        cost_estimate=cost,
        **more,
        compiler_params=pltpu.CompilerParams(vmem_limit_bytes=vmem * 1024 * 1024),
    )(*args)


def f32(*shape):
    return jax.ShapeDtypeStruct(shape, jnp.float32)


def i32(*shape):
    return jax.ShapeDtypeStruct(shape, jnp.int32)


def take(row, index):
    return jnp.take_along_axis(
        jnp.broadcast_to(row, index.shape), index, axis=1, mode="promise_in_bounds"
    )


def joined(face, corner, faces, corners):
    return jnp.concatenate(
        [face[f : f + 1, :] for f in faces] + [corner[f : f + 1, :] for f in corners], axis=1
    )


def pack_kernel(pos_in, species_in, face_in, corner_in, nbr_in, embed_in, radial_in, read_in,
                near, far, own, home, pos, species, nbr, embed, radial, read, face, corner, sems):
    pairs = (
        (pos_in, pos), (species_in, species), (face_in, face), (corner_in, corner),
        (nbr_in, nbr), (embed_in, embed), (radial_in, radial), (read_in, read),
    )
    copies = [
        pltpu.make_async_copy(source, target, sems.at[number])
        for number, (source, target) in enumerate(pairs)
    ]
    for copy in copies:
        copy.start()
    for copy in copies[:4]:
        copy.wait()
    even = lax.axis_index("x") % 2 == 0
    rows = [pos[0:1, :], pos[1:2, :], pos[2:3, :], species[...].astype(jnp.float32)]
    padding = jnp.zeros((5, N), jnp.int32)
    where_from = jnp.concatenate(
        [
            joined(face, corner, (2,), (0, 2)),
            joined(face, corner, (3,), (1, 3)),
            joined(face, corner, (0, 1), ()),
            padding,
        ],
        axis=0,
    )
    home[...] = jnp.concatenate(
        [
            joined(face, corner, (0,), (0, 1)),
            joined(face, corner, (1,), (2, 3)),
            joined(face, corner, (2, 3), ()),
            padding,
        ],
        axis=0,
    )
    for number, row in enumerate(rows):
        got = take(row, where_from)
        near[number : number + 1, :] = jnp.where(even, got[1:2, :], got[0:1, :])
        far[number : number + 1, :] = jnp.where(even, got[0:1, :], got[1:2, :])
        own[number : number + 1, :] = got[2:3, :]
    zero = jnp.zeros((4, N), jnp.float32)
    near[4:8, :] = zero
    far[4:8, :] = zero
    own[4:8, :] = zero
    for copy in copies[4:]:
        copy.wait()


def swapped(value, axes, odd):
    count = math.prod(lax.axis_size(axis) for axis in axes)
    places = [(at, ((((at + odd) % count) ^ 1) - odd) % count) for at in range(count)]
    return lax.ppermute(value, axes, places)


def relay_kernel(own, near, far, one, two):
    at = lane((8, N))
    even = lax.axis_index("x") % 2 == 0
    a = own[...]
    b = jnp.where(even, near[...], far[...])
    d = jnp.where(even, far[...], near[...])
    to_minus = jnp.where(at < 64, a, jnp.where(at < 96, b, pltpu.roll(d, 32, 1)))
    to_plus = jnp.where(
        at < 64, pltpu.roll(a, 64, 1), jnp.where(at < 96, pltpu.roll(b, 96, 1), d)
    )
    first = lax.axis_index("c") == 0
    one[...] = jnp.where(first, to_plus, to_minus)
    two[...] = jnp.where(first, to_minus, to_plus)


def pair_weights(embed, radial):
    scalar, vector = [], []
    for kind in range(KINDS):
        row = embed[kind : kind + 1, :]
        scalar.append(radial[0] * row * 0.25)
        vector.append(radial[1] * row * 0.05)
    return jnp.concatenate(scalar, axis=0), jnp.concatenate(vector, axis=0)


def basis_centers():
    return row_of((BASIS, N)).astype(jnp.float32) * (CUTOFF / (BASIS - 1))


def edge_kernel(
    pos, species, nbr, near_x, far_x, near_y, far_y, embed, radial,
    shared, active, invariants, vectors, sums, edges, places,
):
    at = lane((8, N))
    own = [pos[0:1, :], pos[1:2, :], pos[2:3, :], species[...].astype(jnp.float32)]
    core_zero = lax.axis_index("c") == 0
    even = lax.axis_index("x") % 2 == 0
    first = jnp.where(core_zero, near_x[...], far_x[...])
    second = jnp.where(core_zero, far_x[...], near_x[...])
    plus_y = jnp.where(even, near_y[...], far_y[...])
    minus_y = jnp.where(even, far_y[...], near_y[...])
    third = jnp.where(at < 64, plus_y, pltpu.roll(minus_y, 64, 1))
    line = lane((1, N))
    corner_y = jnp.where(line < 64, 0.0, jnp.where(line < 96, DOMAIN, -DOMAIN))
    tables = [
        own,
        [first[0:1] + DOMAIN, first[1:2] + corner_y, first[2:3], first[3:4]],
        [second[0:1] - DOMAIN, second[1:2] + corner_y, second[2:3], second[3:4]],
        [third[0:1], third[1:2] + jnp.where(line < 64, DOMAIN, -DOMAIN), third[2:3], third[3:4]],
    ]
    for group in range(SLOTS // 8):
        rows = slice(8 * group, 8 * group + 8)
        slot = nbr[rows, :]
        block = lax.shift_right_logical(slot, 6)
        table = jnp.where(
            block < 2,
            0,
            jnp.where(
                (block == 4) | (block == 5), 3, jnp.where((block & 1) == 0, 1, 2)
            ),
        )
        table = jnp.where(block == 8, 4, table)
        half = jnp.where((block == 1) | ((block >= 5) & (block < 8)), 64, 0)
        place = (slot & 63) + half
        found = []
        for number in range(4):
            value = take(tables[0][number], place)
            for other in range(1, 4):
                value = jnp.where(table == other, take(tables[other][number], place), value)
            found.append(value)
        offset = [found[d] - own[d] for d in range(3)]
        dist_sq = offset[0] * offset[0] + offset[1] * offset[1] + offset[2] * offset[2]
        valid = (table < 4).astype(jnp.float32)
        ramp = jnp.maximum(1.0 - dist_sq / (CUTOFF * CUTOFF), 0.0)
        edges[0, rows, :] = offset[0]
        edges[1, rows, :] = offset[1]
        edges[2, rows, :] = offset[2]
        edges[3, rows, :] = found[3]
        edges[4, rows, :] = jnp.sqrt(dist_sq + SOFTEN)
        edges[5, rows, :] = ramp * ramp * valid
        edges[6, rows, :] = (-2.0 / (CUTOFF * CUTOFF)) * ramp * valid
        places[0, rows, :] = table
        places[1, rows, :] = place
    centers = basis_centers()

    def step(slot, carry):
        row = pl.ds(slot, 1)
        away = edges[4, row, :] - centers
        basis = jnp.exp(-WIDTH_GAUSS * away * away) * edges[5, row, :]
        parts = [basis] + [basis * edges[d, row, :] for d in range(3)]
        kind_row = jnp.broadcast_to(edges[3, row, :], (BASIS, N))
        out = []
        for kind in range(KINDS):
            mask = kind_row == float(kind)
            for number in range(4):
                out.append(carry[4 * kind + number] + jnp.where(mask, parts[number], 0.0))
        return tuple(out)

    zero = jnp.zeros((BASIS, N), jnp.float32)
    total = lax.fori_loop(0, SLOTS, step, (zero,) * (4 * KINDS), unroll=16)
    for number in range(4):
        sums[number, :, :] = jnp.concatenate(
            [total[4 * kind + number] for kind in range(KINDS)], axis=0
        )
    scalar_w, vector_w = pair_weights(embed, radial)
    value = dot(sums[0], scalar_w, 0, 0)
    for d in range(3):
        vector = dot(sums[1 + d], vector_w, 0, 0)
        vectors[d, :, :] = vector
        value = value + vector * vector
    invariants[...] = value
    result = value * sigmoid(value)
    active[...] = result
    anchor_x = lax.convert_element_type(lax.axis_index(GX), jnp.float32) * DOMAIN
    anchor_y = lax.convert_element_type(lax.axis_index(GY), jnp.float32) * DOMAIN
    zero_row = jnp.zeros((1, N), jnp.float32)
    tail = jnp.concatenate(
        [own[0] + anchor_x, own[1] + anchor_y, own[2], own[3]] + [zero_row] * 4, axis=0
    )
    shared[0:N, :] = result
    shared[N : N + 8, :] = tail


def edge_back_kernel(
    tile_0, tile_1, tile_2, tile_3, active, invariants, vectors, sums, edges, places, embed, radial, w_up, w_charge,
    species, grad_out, read_row,
    payload, own_grad, charge_piece,
):
    total = tile_0[...] + tile_1[...] + tile_2[...] + tile_3[...]
    grad_charges = jnp.transpose(total[0:N, :])
    updated = grad_out[...] + dot(grad_charges, w_charge[...], 1, 1)
    value = invariants[...]
    logistic = sigmoid(value)
    slope = logistic * (1.0 + value * (1.0 - logistic))
    grad_inv = dot(updated, w_up[...], 1, 1) * slope
    scalar_w, vector_w = pair_weights(embed, radial)
    pulls = [dot(scalar_w, grad_inv, 1, 1)]
    grad_scalar = dot(sums[0], grad_inv)
    grad_vector = jnp.zeros((KINDS * BASIS, N), jnp.float32)
    for d in range(3):
        along = 2.0 * vectors[d] * grad_inv
        pulls.append(dot(vector_w, along, 1, 1))
        grad_vector = grad_vector + dot(sums[1 + d], along)
    onehot = (row_of((8, N)) == species[...]).astype(jnp.float32)
    grad_table = dot(onehot, updated)
    radial_zero = jnp.zeros((BASIS, N), jnp.float32)
    radial_one = jnp.zeros((BASIS, N), jnp.float32)
    table_rows = []
    for kind in range(KINDS):
        rows = slice(kind * BASIS, (kind + 1) * BASIS)
        row = embed[kind : kind + 1, :]
        part_zero, part_one = grad_scalar[rows] * 0.25, grad_vector[rows] * 0.05
        radial_zero = radial_zero + part_zero * row
        radial_one = radial_one + part_one * row
        table_rows.append(
            grad_table[kind : kind + 1]
            + jnp.sum(radial[0] * part_zero + radial[1] * part_one, axis=0, keepdims=True)
        )
    rest = jnp.concatenate(
        [radial_zero, radial_one] + table_rows + [read_row[...], jnp.zeros((1, N), jnp.float32)],
        axis=0,
    )
    up_piece = total[N + 8 : N + 24, :]
    charge_piece[...] = total[N + 24 : N + 40, :]
    centers = basis_centers()
    sub = row_of((8, N))
    sub_table = sub & 3
    high_rows = sub < 4
    lane_rows = row_of((N, N))
    pull = [
        [pulls[number][kind * BASIS : (kind + 1) * BASIS] for number in range(4)]
        for kind in range(KINDS)
    ]

    def one(slot):
        row = pl.ds(slot, 1)
        kind_row = jnp.broadcast_to(edges[3, row, :], (BASIS, N))
        own_pull = list(pull[KINDS - 1])
        for kind in range(KINDS - 1):
            mask = kind_row == float(kind)
            own_pull = [jnp.where(mask, pull[kind][n], own_pull[n]) for n in range(4)]
        radius = edges[4, row, :]
        envelope = edges[5, row, :]
        away = radius - centers
        bell = jnp.exp(-WIDTH_GAUSS * away * away)
        offset = [jnp.broadcast_to(edges[d, row, :], (BASIS, N)) for d in range(3)]
        by_basis = own_pull[0]
        for d in range(3):
            by_basis = by_basis + offset[d] * own_pull[1 + d]
        by_square = by_basis * bell * (edges[6, row, :] - (2.0 * envelope / radius) * away)
        basis = bell * envelope
        table = jnp.broadcast_to(places[0, row, :], (8, N)) == sub_table
        place = lane_rows == places[1, row, :]
        onehot = jnp.where(place, 1.0, 0.0).astype(jnp.bfloat16)
        parts, pieces = [], []
        for d in range(3):
            part = basis * own_pull[1 + d] + 2.0 * offset[d] * by_square
            parts.append(part)
            whole = jnp.broadcast_to(jnp.sum(part, axis=0, keepdims=True), (8, N))
            high = whole.astype(jnp.bfloat16).astype(jnp.float32)
            pieces.append(jnp.where(table, jnp.where(high_rows, high, whole - high), 0.0))
        return parts, jnp.concatenate(pieces, axis=0).astype(jnp.bfloat16), onehot

    def step(group, carry):
        found = [one(group * 8 + number) for number in range(8)]
        centre = list(carry[:3])
        for parts, _, _ in found:
            centre = [centre[d] + parts[d] for d in range(3)]
        rows = jnp.concatenate([item[1] for item in found], axis=1)
        onehot = jnp.concatenate([item[2] for item in found], axis=1)
        return (*centre, carry[3] + half_dot(rows, onehot, 1, 1))

    zero = jnp.zeros((8, N), jnp.float32)
    out = (zero, zero, zero, jnp.zeros((24, N), jnp.float32))
    for group in range(SLOTS // 8):
        out = step(group, out)
    scattered = out[3]
    waves = total[N : N + 8, :]
    own_rows, one_rows, two_rows, three_rows = [], [], [], []
    for d in range(3):
        both = scattered[8 * d : 8 * d + 4] + scattered[8 * d + 4 : 8 * d + 8]
        centre = jnp.sum(out[d], axis=0, keepdims=True)
        own_rows.append(both[0:1] - centre + waves[d : d + 1])
        one_rows.append(both[1:2])
        two_rows.append(both[2:3])
        three_rows.append(both[3:4])
    pad = [jnp.zeros((5, N), jnp.float32)]
    own_grad[...] = jnp.concatenate(own_rows + pad, axis=0)
    depth_of = [depth_after(step_x, step_y) for step_x, step_y in TABLE_DIRS]
    line = lane((8, N))
    ones = jnp.concatenate(one_rows + pad, axis=0)
    twos = jnp.concatenate(two_rows + pad, axis=0)
    threes = jnp.concatenate(three_rows + pad, axis=0)
    home_one = segments(line, depth_of[0:3])
    home_two = segments(line, depth_of[3:6])
    home_three = jnp.where(line < 64, depth_of[6], depth_of[7])
    for other in range(8):
        payload[other, 0:16, :] = up_piece
        payload[other, 16:40, :] = rest
        payload[other, 40:48, :] = pack_six(
            jnp.where(home_one == other, ones, 0.0), jnp.where(home_two == other, twos, 0.0)
        )
        payload[other, 48:56, :] = jnp.where(home_three == other, threes, 0.0)


TABLE_DIRS = ((1, 0), (1, 1), (1, -1), (-1, 0), (-1, 1), (-1, -1), (0, 1), (0, -1))


def segments(line, values):
    return jnp.where(line < 64, values[0], jnp.where(line < 96, values[1], values[2]))


def pack_six(one, two):
    return jnp.where(row_of((8, N)) < 4, one, pltpu.roll(two, 4, 0))


def depth_after(step_x, step_y):
    core, high = lax.axis_index("c"), lax.axis_index("zh")
    low, column = lax.axis_index("zl"), lax.axis_index("x")
    if step_x == 1:
        high = jnp.where(core == 1, (high + 1) % 4, high)
    if step_x == -1:
        high = jnp.where(core == 0, (high + 3) % 4, high)
    if step_y == 1:
        low = jnp.where(column == 3, 1 - low, low)
    if step_y == -1:
        low = jnp.where(column == 0, 1 - low, low)
    return high * 2 + low


def plane_after(step_x, step_y):
    core, high = lax.axis_index("c"), lax.axis_index("zh")
    row, column = lax.axis_index("y"), lax.axis_index("x")
    if step_x == 1:
        row = jnp.where((core == 1) & (high == 0), (row + 1) % 4, row)
    if step_x == -1:
        row = jnp.where((core == 0) & (high == 3), (row + 3) % 4, row)
    return row * 4 + (column + step_y + 4) % 4


def depth_sum_kernel(tiles, charge_piece, out):
    total = jnp.sum(tiles[...], axis=0)
    place_of = [plane_after(step_x, step_y) for step_x, step_y in TABLE_DIRS]
    line = lane((8, N))
    home = jnp.where(
        row_of((8, N)) < 4, segments(line, place_of[0:3]), segments(line, place_of[3:6])
    )
    home_three = jnp.where(line < 64, place_of[6], place_of[7])
    sixes, threes = total[40:48], total[48:56]
    row = lax.axis_index("y")
    quarter = charge_piece[0:4, :]
    for number in range(1, 4):
        quarter = jnp.where(row == number, charge_piece[4 * number : 4 * number + 4, :], quarter)
    for other in range(16):
        out[other, 0:40, :] = total[0:40]
        out[other, 40:48, :] = jnp.where(home == other, sixes, 0.0)
        out[other, 48:56, :] = jnp.where(home_three == other, threes, 0.0)
        out[other, 52:56, :] = quarter


def plane_sum_kernel(tiles, swap, threes):
    for column in range(4):
        total = tiles[column, 0:16, :]
        for row in range(1, 4):
            total = total + tiles[4 * row + column, 0:16, :]
        swap[16 * column : 16 * column + 16, :] = total
        for row in range(4):
            at = 96 + 16 * column + 4 * row
            swap[at : at + 4, :] = tiles[4 * row + column, 52:56, :]
    rest = tiles[0, 16:56, :]
    for other in range(1, 16):
        rest = rest + tiles[other, 16:56, :]
    swap[64:96, :] = rest[0:32]
    threes[...] = jnp.where(row_of((8, N)) < 4, rest[32:40], 0.0)


def finish_kernel(own, other, threes, own_grad, home, forces, grad_embed, grad_radial, grad_up,
                  grad_charge, grad_read):
    mean = 1.0 / ATOMS
    core = lax.axis_index("c")
    mine = pl.ds(pl.multiple_of(core * 64, 64), 64)
    theirs = pl.ds(pl.multiple_of((1 - core) * 64, 64), 64)
    grad_up[mine, :] = own[0:64, :] * mean
    grad_up[theirs, :] = other[0:64, :] * mean
    grad_charge[mine, :] = own[96:160, :] * mean
    grad_charge[theirs, :] = other[96:160, :] * mean
    total = (own[64:88, :] + other[64:88, :]) * mean
    grad_radial[0, :, :] = total[0:8]
    grad_radial[1, :, :] = total[8:16]
    grad_embed[...] = total[16:22]
    grad_read[...] = total[22:23]
    sixes = other[88:96, :]
    grad = own_grad[...]
    lane_rows = row_of((N, N))
    for number, piece in enumerate((sixes, pltpu.roll(sixes, 4, 0), threes[...])):
        onehot = jnp.where(lane_rows == home[number : number + 1, :], 1.0, 0.0)
        grad = grad + dot(piece, onehot, 1, 1)
    forces[...] = -grad[0:3, :]


def spread_kernel(*refs):
    out = refs[-1]
    core, column = lax.axis_index("c"), lax.axis_index("x")
    for number, pair in enumerate(refs[:-1]):
        for half in range(2):
            source = column ^ (2 * (number % 2) + half)
            member = jnp.where(number < 2, core, 1 - core) * 4 + source
            place = pl.ds(pl.multiple_of(member * SHARD, SHARD), SHARD)
            out[place, :] = pair[half * SHARD : (half + 1) * SHARD, :]


def structure_part(tiles, kvec, embed, w_up, wave_high, wave_low, feature_high, feature_low):
    me = lax.axis_index(GROUP)
    at = pl.multiple_of(me * SHARD, SHARD)
    rows = jnp.concatenate(
        [kvec[:, pl.ds(at, SHARD)], jnp.zeros((5, SHARD), jnp.float32)], axis=0
    )
    turns = jnp.transpose(rows * (1.0 / (2.0 * math.pi)))
    table = jnp.concatenate([embed[...], jnp.zeros((2, N), jnp.float32)], axis=0)
    up = split(w_up[...])
    for member, tile in enumerate(tiles):
        part = slice(member * N, (member + 1) * N)
        tail = tile[N : N + 8, :]
        onehot = (row_of((8, N)).astype(jnp.float32) == tail[3:4, :]).astype(jnp.float32)
        feature = exact_dot(onehot, table, 0, 0) + dot_three(split(tile[0:N, :]), up)
        high, low = split(feature)
        feature_high[part, :] = high
        feature_low[part, :] = low
        for chunk in range(SHARD // 64):
            waves = slice(chunk * 64, chunk * 64 + 64)
            angle = (
                turns[waves, 0:1] * tail[0:1, :]
                + turns[waves, 1:2] * tail[1:2, :]
                + turns[waves, 2:3] * tail[2:3, :]
            )
            angle = angle - jnp.round(angle)
            square = angle * angle
            cosine = jnp.full(square.shape, COS_POLY[-1], jnp.float32)
            for value in COS_POLY[-2::-1]:
                cosine = cosine * square + value
            sine = jnp.full(square.shape, SIN_POLY[-1], jnp.float32)
            for value in SIN_POLY[-2::-1]:
                sine = sine * square + value
            sine = sine * angle
            high, low = split(cosine)
            wave_high[waves, part] = high
            wave_low[waves, part] = low
            high, low = split(sine)
            waves = slice(SHARD + chunk * 64, SHARD + chunk * 64 + 64)
            wave_high[waves, part] = high
            wave_low[waves, part] = low
    return project(wave_high, wave_low, feature_high[...], feature_low[...])


def structure_mine_kernel(*refs):
    kvec, embed, w_up, factor, *part = refs[4:]
    factor[...] = structure_part(refs[:4], kvec, embed, w_up, *part)


def structure_other_kernel(*refs):
    kvec, embed, w_up, mine, factor, *part = refs[4:]
    total = mine[...] + structure_part(refs[:4], kvec, embed, w_up, *part)
    factor[...] = total.reshape(CROSSES, 16, N)


def whole(tiles):
    return jnp.concatenate([tile[0:N, :] for tile in tiles], axis=0)


def project(wave_high, wave_low, high, low):
    wide = half_dot(wave_high[...], jnp.concatenate([high, low], axis=1))
    return wide[:, 0:N] + wide[:, N:] + half_dot(wave_low[...], high)


def projection_mine_kernel(*refs):
    wave_high, wave_low, out = refs[4:]
    out[...] = project(wave_high, wave_low, *split(whole(refs[:4])))


def projection_other_kernel(*refs):
    wave_high, wave_low, mine, out = refs[4:]
    total = mine[...] + project(wave_high, wave_low, *split(whole(refs[:4])))
    out[...] = total.reshape(CROSSES, 16, N)


def sum_kernel(tiles, out):
    total = jnp.sum(tiles[...], axis=0)
    for other in range(out.shape[0]):
        out[other, :, :] = total


def filter_of(kfilter):
    me = lax.axis_index(GROUP)
    return kfilter[pl.ds(pl.multiple_of(me * SHARD, SHARD), SHARD), :] * SCALE


def core_sum_kernel(mine, other, *out):
    for number, ref in enumerate(out):
        ref[...] = mine[number] + other[number]


def core_sum_late_kernel(mine, late, other, *out):
    for number, ref in enumerate(out):
        ref[...] = mine[number] + other[number]
        ref[N : N + 8, :] = mine[number, N : N + 8, :] + (
            late[number] + other[number, N : N + 8, :]
        )


def field_rows(field):
    return jnp.concatenate(split(jnp.transpose(field)), axis=0)


def waves_to_atoms(rows, wave_high, wave_low):
    wide = half_dot(rows, wave_high[...])
    return wide[0:N] + wide[N:] + half_dot(rows[0:N], wave_low[...])


def to_tiles(total, out):
    for member in range(4):
        out[member, 0:N, :] = total[:, member * N : (member + 1) * N]


def potential_other_kernel(factor, w_charge, kfilter, wave_high, wave_low,
                           other, weighted, charge_factor, rows_out):
    scaled = filter_of(kfilter)
    charged = dot(factor[...], w_charge[...])
    charge_factor[...] = charged
    field = charged * jnp.concatenate([scaled, scaled], axis=0)
    weighted[...] = field
    rows = field_rows(field)
    rows_out[...] = rows
    to_tiles(waves_to_atoms(rows, wave_high, wave_low), other)


def potential_mine_kernel(rows, wave_high, wave_low, mine):
    to_tiles(waves_to_atoms(rows[...], wave_high, wave_low), mine)


def energy_kernel(tile_0, tile_1, tile_2, tile_3, feature_high, feature_low, read,
                  grad_out, result_out):
    total = tile_0[...] + tile_1[...] + tile_2[...] + tile_3[...]
    feature = feature_high[0:N, :].astype(jnp.float32) + feature_low[0:N, :].astype(jnp.float32)
    combined = feature + jnp.transpose(total)
    logistic = sigmoid(combined)
    result_out[...] = combined * logistic
    grad_out[...] = read[...] * (logistic * (1.0 + combined * (1.0 - logistic)))


def read_kernel(result, grad, active, read, energy, read_row, up_part):
    value = result[...]
    energy[...] = dot(jnp.broadcast_to(read[...], (8, N)), value, 1, 1)[0:1, :]
    read_row[...] = jnp.sum(value, axis=0, keepdims=True)
    up_part[...] = dot(active[...], grad[...], 0, 0)


def wave_trig(wave_high, wave_low):
    cosine = wave_high[0:SHARD, :].astype(jnp.float32) + wave_low[0:SHARD, :].astype(jnp.float32)
    sine = wave_high[SHARD:, :].astype(jnp.float32) + wave_low[SHARD:, :].astype(jnp.float32)
    return cosine, sine


def by_position(left, grads, feature_high, feature_low, kvec, wave_high, wave_low):
    grad_high, grad_low = split(whole(grads))
    along = dot_three(
        left,
        (
            jnp.concatenate([grad_high, feature_high[...]], axis=1),
            jnp.concatenate([grad_low, feature_low[...]], axis=1),
        ),
        1, 1,
    )
    cosine, sine = wave_trig(wave_high, wave_low)
    phase = cosine * along[SHARD:] - sine * along[0:SHARD]
    me = lax.axis_index(GROUP)
    rows = jnp.concatenate(
        [
            kvec[:, pl.ds(pl.multiple_of(me * SHARD, SHARD), SHARD)],
            jnp.zeros((5, SHARD), jnp.float32),
        ],
        axis=0,
    )
    return dot_three(split(rows), split(phase))


def wave_back_kernel(*refs):
    grads, shared = refs[:4], refs[4:12]
    (
        projected, factor, weighted, kfilter, kvec, mine_high, mine_low, wave_high, wave_low,
        feature_high, feature_low, w_charge, up_part,
        mine, other, left_high, left_low, up_grad, charge_grad,
    ) = refs[12:]
    scaled = filter_of(kfilter)
    field = projected[...] * jnp.concatenate([scaled, scaled], axis=0)
    pieces = split(field)
    rows = field_rows(field)
    mine_charge = waves_to_atoms(rows, mine_high, mine_low)
    other_charge = waves_to_atoms(rows, wave_high, wave_low)
    charge_grad[...] = dot_three(split(factor[...]), pieces, 0, 0)
    mix = dot(mine_charge, whole(shared[:4])) + dot(other_charge, whole(shared[4:]))
    weights = split(w_charge[...])
    up_grad[...] = dot_three(split(mix), weights, 0, 1) + up_part[...]
    left = split(
        jnp.concatenate([weighted[...], dot_three(pieces, weights, 1, 1)], axis=1)
    )
    left_high[...], left_low[...] = left
    by_pos = by_position(left, grads, feature_high, feature_low, kvec, wave_high, wave_low)
    to_tiles(mine_charge, mine)
    to_tiles(other_charge, other)
    core, column = lax.axis_index("c"), lax.axis_index("x")
    for member in range(MEMBERS):
        number = member % 4
        out = (mine, other)[member // 4].at[number]
        place = jnp.where(core == member // 4, 0, 4) + (column ^ number)
        piece = pl.ds(pl.multiple_of(place * 16, 16), 16)
        if member < 4:
            out[N : N + 8, :] = jnp.zeros((8, N), jnp.float32)
        else:
            out[N : N + 8, :] = by_pos[:, number * N : (number + 1) * N]
        out[N + 8 : N + 24, :] = up_grad[piece, :]
        out[N + 24 : N + 40, :] = charge_grad[piece, :]


def wave_back_late_kernel(*refs):
    (
        left_high, left_low, projected, charge_factor, kvec, wave_high, wave_low,
        feature_high, feature_low, late, grad_filter,
    ) = refs[4:]
    mixed = charge_factor[...] * projected[...]
    grad_filter[...] = SCALE * (mixed[0:SHARD] + mixed[SHARD:])
    left = (left_high[...], left_low[...])
    by_pos = by_position(left, refs[:4], feature_high, feature_low, kvec, wave_high, wave_low)
    for member in range(4):
        late[member, :, :] = by_pos[:, member * N : (member + 1) * N]


def body(
    positions, species, neighbours, face_sends, corner_sends,
    embed, radial, w_up, w_charge, kvec, kfilter, read,
):
    near, far, own_x, home, positions, species, neighbours, embed, radial, read = call(
        pack_kernel,
        (f32(8, N),) * 3
        + (
            i32(8, N), f32(3, N), i32(1, N), i32(SLOTS, N), f32(KINDS, N), f32(2, BASIS, N),
            f32(1, N),
        ),
        positions, species.reshape(1, N), face_sends, corner_sends, neighbours, embed, radial,
        read.reshape(1, N),
        scratch=(
            pltpu.VMEM((4, N // 2), jnp.int32),
            pltpu.VMEM((4, N // 4), jnp.int32),
            pltpu.SemaphoreType.DMA((8,)),
        ),
        far=True,
    )
    near_y, far_y = swapped(near, GY, 0), swapped(far, GY, 1)
    near, far = call(relay_kernel, (f32(8, N),) * 2, own_x, near_y, far_y)
    near_x, far_x = swapped(near, GX, 0), swapped(far, GX, 1)
    shared, active, invariants, vectors, sums, edges, places = call(
        edge_kernel,
        (
            f32(N + 8, N), f32(N, N), f32(N, N), f32(3, N, N), f32(4, KINDS * BASIS, N),
            f32(7, SLOTS, N), i32(2, SLOTS, N),
        ),
        positions, species, neighbours, near_x, far_x, near_y, far_y, embed, radial,
    )
    swap = [(0, 1), (1, 0)]

    def other_core(value):
        return lax.ppermute(value, "c", swap)

    def step_x(value, step):
        return lax.ppermute(value, "x", [(at, at ^ step) for at in range(4)])

    def gather(value, beside=()):
        one, three, two = (step_x(value, step) for step in (1, 3, 2))
        two, *beside = lax.optimization_barrier((two, *beside))
        values = [value, one, two, three]
        return values + [other_core(item) for item in values], beside

    def scatter(kernel, parts, other):
        shape = f32(*other.shape[1:])
        tiles = call(kernel, (shape,) * 4, *parts, other_core(other))
        two, one, three = (step_x(tiles[step], step) for step in (2, 1, 3))
        return [tiles[0], one, two, three]

    shared, _ = gather(shared)
    half = jax.ShapeDtypeStruct((2 * SHARD, 4 * N), jnp.bfloat16)
    feature = jax.ShapeDtypeStruct((4 * N, N), jnp.bfloat16)
    part = (half, half, feature, feature)
    both = f32(2 * SHARD, N)
    factor, *mine_part = call(
        structure_mine_kernel, (both,) + part, *shared[:4], kvec, embed, w_up
    )
    factor, *other_part = call(
        structure_other_kernel, (f32(CROSSES, 16, N),) + part, *shared[4:], kvec, embed, w_up,
        factor,
    )
    mine_waves, mine_features = mine_part[:2], mine_part[2:]
    other_waves, other_features = other_part[:2], other_part[2:]

    def cross_sum(tiles):
        tiles = lax.all_to_all(tiles, CROSS, 0, 0)
        tiles = call(sum_kernel, f32(CROSSES, 16, N), tiles)
        return lax.all_to_all(tiles, CROSS, 0, 0).reshape(2 * SHARD, N)

    factor = cross_sum(factor)
    rows = jax.ShapeDtypeStruct((2 * N, 2 * SHARD), jnp.bfloat16)
    other, weighted, charge_factor, rows = call(
        potential_other_kernel, (f32(4, N, N), both, both, rows),
        factor, w_charge, kfilter, *other_waves,
    )
    mine = call(potential_mine_kernel, f32(4, N, N), rows, *mine_waves)
    grad_out, result = call(
        energy_kernel, (f32(N, N),) * 2,
        *scatter(core_sum_kernel, (mine,), other), *mine_features, read,
    )
    beside = call(read_kernel, (f32(1, N), f32(1, N), f32(N, N)), result, grad_out, active, read)
    grads, (energy, read_row, up_part) = gather(grad_out, beside)
    projected = call(projection_mine_kernel, both, *grads[:4], *mine_waves)
    others = grads[4:]
    projected = cross_sum(
        call(projection_other_kernel, f32(CROSSES, 16, N), *others, *other_waves, projected)
    )
    square = pltpu.VMEM((N, N), jnp.float32)
    left = jax.ShapeDtypeStruct((2 * SHARD, 2 * N), jnp.bfloat16)
    mine, other, *left = call(
        wave_back_kernel,
        (f32(4, N + 40, N), f32(4, N + 40, N), left, left),
        *others, *shared, projected, factor, weighted, kfilter, kvec, *mine_waves,
        *other_waves, *other_features, w_charge, up_part,
        scratch=(square, square),
    )
    late, shard = call(
        wave_back_late_kernel, (f32(4, 8, N), f32(SHARD, N)),
        *grads[:4], *left, projected, charge_factor, kvec, *mine_waves, *mine_features,
    )
    tiles = scatter(core_sum_late_kernel, (mine, late), other)
    next_shard = lax.ppermute(shard, "x", [(at, at ^ 1) for at in range(4)])
    payload, own_grad, charge_piece = call(
        edge_back_kernel,
        (f32(8, 56, N), f32(8, N), f32(16, N)),
        *tiles, active, invariants, vectors, sums, edges, places, embed, radial, w_up,
        w_charge, species, grad_out, read_row,
        cost=pl.CostEstimate(flops=10**9, bytes_accessed=10**7, transcendentals=10**5),
    )
    near_shards = jnp.concatenate([shard, next_shard], axis=0)
    far_shards = lax.ppermute(near_shards, "x", [(at, at ^ 2) for at in range(4)])
    payload = lax.all_to_all(payload, DEPTH, 0, 0)
    payload = call(depth_sum_kernel, f32(16, 56, N), payload, charge_piece)
    payload = lax.all_to_all(payload, PLANE, 0, 0)
    payload, threes = call(plane_sum_kernel, (f32(160, N), f32(8, N)), payload)
    shards = [near_shards, far_shards, other_core(near_shards), other_core(far_shards)]
    payload_other = other_core(payload)
    grad_filter = call(spread_kernel, f32(WAVES, N), *shards)
    forces, grad_embed, grad_radial, grad_up, grad_charge, grad_read = call(
        finish_kernel,
        (f32(3, N), f32(KINDS, N), f32(2, BASIS, N), f32(N, N), f32(N, N), f32(1, N)),
        payload, payload_other, threes, own_grad, home,
    )
    return (
        energy.reshape(N), forces, grad_embed, grad_radial, grad_up, grad_charge, grad_filter,
        grad_read.reshape(N),
    )


def solution(mesh):
    fine = Mesh(mesh.devices.reshape(4, 4, 2, 2, 4), ALL)
    atoms = P(ALL)
    rows = P(None, ALL)
    return jax.shard_map(
        body,
        mesh=fine,
        in_specs=(rows, atoms, rows, rows, rows) + (P(),) * 7,
        out_specs=(atoms, rows) + (P(),) * 6,
        check_vma=False,
    )
```
